32 devices in a mesh: cell: 16 (over z, y, x), qgrp: 2 (over core).
Axes of the slice: x: 2, y: 2, z: 4, core: 2. Of those that a mesh axis runs over, the one named last changes fastest.
Arguments:
- supernode_embeddings: bfloat16 [8192, 768], P('cell'), may hold values from -6 to 6
- filled_supernode_tally: int32 [16], P('cell'), may hold values from 1 to 512, 6144 in all
- hidden_probe_states: bfloat16 [1024, 768], replicated, may hold values from -6 to 6
- softness_per_channel: float32 [2, 12], replicated, may hold values from 1 to 12, as said below
- gather_probe_projector: bfloat16 [768, 768], P(None, 'qgrp'), may hold values from -0.4375 to 0.4375
- gather_lookup_projector: bfloat16 [768, 768], P(None, 'qgrp'), may hold values from -0.4375 to 0.4375
- gather_content_projector: bfloat16 [768, 768], P(None, 'qgrp'), may hold values from -0.21875 to 0.21875
- gather_final_projector: bfloat16 [768, 768], P('qgrp'), may hold values from -0.21875 to 0.21875
- unpack_probe_projector: bfloat16 [768, 768], P(None, 'qgrp'), may hold values from -0.21875 to 0.21875
- unpack_lookup_projector: bfloat16 [768, 768], P(None, 'qgrp'), may hold values from -0.21875 to 0.21875
- unpack_content_projector: bfloat16 [768, 768], P(None, 'qgrp'), may hold values from -0.21875 to 0.21875
- unpack_final_projector: bfloat16 [768, 768], P('qgrp'), may hold values from -0.21875 to 0.21875
- hidden_state_gain: float32 [768], replicated, may hold values from 0.1 to 1.9
Outputs:
- latent_out: float32 [1024, 768], replicated
- tokens_out: float32 [8192, 768], P(('cell', 'qgrp'))
The draws below stay inside these ranges and needn't reach their ends.
Inputs may be any that keep to these rules, and one draw needn't show every extreme that they name: Slots 0 to filled_supernode_tally[c] - 1 of cell block c hold its valid supernodes; its other slots are padding. `softness_per_channel`: A positive temperature for each head.
All inputs are finite; a program needn't handle non-finite values.
Results may differ from the reference program's by a relative error of at most 0.009.
The reference program's roundings to bfloat16 on the way count: a program that leaves them out, or rounds other values in their place, can miss the bound.
Values may be sent and summed in bfloat16 or wider, within the bound.
No kernel may reach another device: no remote copies, remote signals or barrier semaphores. Data moves between devices by JAX's collectives and lax.ppermute only.
A program may use at most 448 MiB of HBM per device.

```python
import math
import jax
import jax.numpy as jnp
import numpy as np
from jax import lax

D = 768
HEADS = 12
L = 1024
CAP = 512
NTOK = 8192
N_CELL = 16


def draw_softness_per_channel(key, part):
    base = jax.random.uniform(key, (2, HEADS), jnp.float32)
    return jnp.exp(base * math.log(3.0))


def level_of(own_key, extent, pieces, least, top_value):
    def one(position, shards_of):
        steps = jax.random.uniform(jax.random.fold_in(jax.random.fold_in(own_key, 6), position), (shards_of,), jnp.float32, least / len(pieces), top_value / len(pieces))
        return jnp.repeat(jnp.exp(steps), extent[position] // shards_of).reshape((-1,) + (1,) * (len(extent) - position - 1))

    loudness = one(*pieces[0])
    for cut in pieces[1:]:
        loudness = loudness * one(*cut)
    return loudness


def profile(count, total, bound, slope):
    portions = [(1 << 20) // math.isqrt(rank ** slope) + 1 for rank in range(2, count + 1)]
    surplus, counts = total - bound - (count - 1), [1] * (count - 1)
    while surplus > 0:
        candidates = [i for i in range(count - 1) if counts[i] < bound]
        pool, budget = sum([portions[i] for i in candidates]), surplus
        for i in candidates:
            addition = min(bound - counts[i], max(1, budget * portions[i] // pool), surplus)
            counts[i] = counts[i] + addition
            surplus = surplus - addition
    return np.array([bound] + counts)


def uneven(stream_key, amount, total, reach, slope):
    if amount == 2:
        one = jax.random.randint(stream_key, (), max(1, total - reach), min(reach, total - 1) + 1)
        return jnp.stack([one, total - one])
    tallies = jnp.asarray(profile(amount, total, reach, slope), jnp.int32)
    pairs = (amount - 1) // 2
    source_of, receiver = tallies[1:1 + 2 * pairs:2], tallies[2:2 + 2 * pairs:2]
    slack = jnp.minimum(source_of - 1, reach - receiver)
    passed = jax.random.randint(jax.random.fold_in(stream_key, 1), (pairs,), 0, 1 << 20) % (slack + 1)
    tallies = tallies.at[1:1 + 2 * pairs:2].set(source_of - passed).at[2:2 + 2 * pairs:2].set(receiver + passed)
    return tallies[jax.random.permutation(jax.random.fold_in(stream_key, 2), amount)]


def scatter_about(own_key, extent, spread, limit, split=(), kind=jnp.bfloat16):
    loudness = level_of(own_key, extent, split, -0.22, 0.18) if split else 1.0
    entries = jax.random.normal(own_key, extent, jnp.float32) * spread * loudness
    return jnp.minimum(jnp.maximum(entries, -limit), limit).astype(kind)


def setup_inputs(seed: int = 0) -> dict:
    seeds = jax.random.split(jax.random.key(seed), 14)
    supernode_embeddings = scatter_about(seeds[0], (NTOK, D), 1.0, 6.0, ((0, 16),))
    filled_supernode_tally = uneven(seeds[1], N_CELL, 3 * N_CELL * CAP // 4, CAP, 1).astype(jnp.int32)
    hidden_probe_states = scatter_about(seeds[2], (L, D), 1.0, 6.0)
    softness_per_channel = draw_softness_per_channel(jax.random.fold_in(seeds[13], 71), 0)
    gather_probe_projector = scatter_about(seeds[4], (D, D), (D // 4) ** -0.5, 0.4375, ((1, 2),))
    gather_lookup_projector = scatter_about(seeds[5], (D, D), (D // 4) ** -0.5, 0.4375, ((1, 2),))
    gather_content_projector = scatter_about(seeds[6], (D, D), D ** -0.5, 0.21875, ((1, 2),))
    gather_final_projector = scatter_about(seeds[7], (D, D), D ** -0.5, 0.21875, ((0, 2),))
    unpack_probe_projector = scatter_about(seeds[8], (D, D), D ** -0.5, 0.21875, ((1, 2),))
    unpack_lookup_projector = scatter_about(seeds[9], (D, D), D ** -0.5, 0.21875, ((1, 2),))
    unpack_content_projector = scatter_about(seeds[10], (D, D), D ** -0.5, 0.21875, ((1, 2),))
    unpack_final_projector = scatter_about(seeds[11], (D, D), D ** -0.5, 0.21875, ((0, 2),))
    hidden_state_gain = jnp.clip(1.0 + 0.18 * jax.random.normal(seeds[12], (D,), jnp.float32), 0.1, 1.9)
    return dict(supernode_embeddings=supernode_embeddings, filled_supernode_tally=filled_supernode_tally, hidden_probe_states=hidden_probe_states, softness_per_channel=softness_per_channel, gather_probe_projector=gather_probe_projector, gather_lookup_projector=gather_lookup_projector, gather_content_projector=gather_content_projector, gather_final_projector=gather_final_projector, unpack_probe_projector=unpack_probe_projector, unpack_lookup_projector=unpack_lookup_projector, unpack_content_projector=unpack_content_projector, unpack_final_projector=unpack_final_projector, hidden_state_gain=hidden_state_gain)


MASKED_SCORE = -1e+30
NORM_EPSILON = 1e-06

def rounded(values):
    return lax.optimization_barrier(values.astype(jnp.bfloat16)).astype(jnp.float32)

def rms_norm(values, gain):
    mean_square = lax.optimization_barrier(jnp.mean(values * values, axis=-1, keepdims=True))
    return values * lax.rsqrt(mean_square + NORM_EPSILON) * gain

def reference(supernode_embeddings, filled_supernode_tally, hidden_probe_states, softness_per_channel, gather_probe_projector, gather_lookup_projector, gather_content_projector, gather_final_projector, unpack_probe_projector, unpack_lookup_projector, unpack_content_projector, unpack_final_projector, hidden_state_gain):
    per_channel_dimension = D // HEADS
    gather_multiplier = softness_per_channel[0] * per_channel_dimension ** (-0.5)
    unpack_multiplier = softness_per_channel[1] * per_channel_dimension ** (-0.5)
    queries = rounded(jnp.dot(hidden_probe_states, gather_probe_projector, preferred_element_type=jnp.float32)).reshape(L, HEADS, per_channel_dimension)
    cell_tokens = supernode_embeddings.reshape(N_CELL, CAP, D)

    def visit(running, item):
        run_max, run_sum, run_acc = running
        block_tokens, live_count = item
        key_rows = rounded(jnp.dot(block_tokens, gather_lookup_projector, preferred_element_type=jnp.float32)).reshape(CAP, HEADS, per_channel_dimension)
        value_rows = rounded(jnp.dot(block_tokens, gather_content_projector, preferred_element_type=jnp.float32)).reshape(CAP, HEADS, per_channel_dimension)
        is_valid = lax.iota(jnp.int32, CAP) < live_count
        scores = jnp.einsum('lhd,khd->lhk', queries, key_rows) * gather_multiplier[None, :, None]
        scores = jnp.where(is_valid[None, None, :], scores, jnp.float32(MASKED_SCORE))
        block_max = lax.optimization_barrier(jnp.max(scores, axis=-1))
        weights = jnp.exp(scores - block_max[:, :, None]) * is_valid[None, None, :].astype(jnp.float32)
        block_sum = lax.optimization_barrier(jnp.sum(weights, axis=-1))
        block_acc = jnp.einsum('lhk,khd->lhd', rounded(weights), value_rows)
        new_max = jnp.maximum(run_max, block_max)
        old_factor = jnp.exp(run_max - new_max)
        block_factor = jnp.exp(block_max - new_max)
        new_sum = run_sum * old_factor + block_sum * block_factor
        new_acc = run_acc * old_factor[:, :, None] + block_acc * block_factor[:, :, None]
        return ((new_max, new_sum, new_acc), None)
    initial = (jnp.full((L, HEADS), MASKED_SCORE, jnp.float32), jnp.zeros((L, HEADS), jnp.float32), jnp.zeros((L, HEADS, per_channel_dimension), jnp.float32))
    (run_max, run_sum, run_acc), unused = lax.scan(visit, initial, (cell_tokens, filled_supernode_tally.astype(jnp.int32)))
    attended = (run_acc / run_sum[:, :, None]).astype(jnp.bfloat16).reshape(L, D)
    latent_pre = hidden_probe_states.astype(jnp.float32) + jnp.dot(attended, gather_final_projector, preferred_element_type=jnp.float32)
    latent_out = rms_norm(latent_pre, hidden_state_gain)
    latent_half = latent_out.astype(jnp.bfloat16)
    dec_keys = rounded(jnp.dot(latent_half, unpack_lookup_projector, preferred_element_type=jnp.float32)).reshape(L, HEADS, per_channel_dimension)
    dec_values = rounded(jnp.dot(latent_half, unpack_content_projector, preferred_element_type=jnp.float32)).reshape(L, HEADS, per_channel_dimension)

    def decode_cell(item):
        block_tokens, live_count = item
        dec_queries = rounded(jnp.dot(block_tokens, unpack_probe_projector, preferred_element_type=jnp.float32)).reshape(CAP, HEADS, per_channel_dimension)
        scores = jnp.einsum('khd,lhd->khl', dec_queries, dec_keys) * unpack_multiplier[None, :, None]
        weights = jnp.exp(scores - lax.optimization_barrier(jnp.max(scores, axis=-1, keepdims=True)))
        denominator = lax.optimization_barrier(jnp.sum(weights, axis=-1))
        mixed_heads = jnp.einsum('khl,lhd->khd', rounded(weights), dec_values) / denominator[:, :, None]
        dec_att = mixed_heads.astype(jnp.bfloat16).reshape(CAP, D)
        update = jnp.dot(dec_att, unpack_final_projector, preferred_element_type=jnp.float32)
        is_valid = lax.iota(jnp.int32, CAP) < live_count
        return jnp.where(is_valid[:, None], block_tokens.astype(jnp.float32) + update, jnp.float32(0.0))
    tokens_out = lax.map(decode_cell, (cell_tokens, filled_supernode_tally.astype(jnp.int32))).reshape(N_CELL * CAP, D)
    return (latent_out, tokens_out)
```

```python
import functools
import math

import jax
import jax.numpy as jnp
from jax import lax
from jax.experimental import pallas as pl
from jax.experimental.pallas import tpu as pltpu
from jax.sharding import PartitionSpec as P

HEAD_DIM = 64
PAIR = 2 * HEAD_DIM
NORM_EPSILON = 1e-06
LOG2E = math.log2(math.e)
F32 = jnp.float32
BF16 = jnp.bfloat16
MIB = 1 << 20

TERMS = 3


def nn(a, b):
    return lax.dot_general(a, b, (((1,), (0,)), ((), ())), preferred_element_type=F32)


def nt(a, b):
    return lax.dot_general(a, b, (((1,), (1,)), ((), ())), preferred_element_type=F32)


def tn(a, b):
    return lax.dot_general(a, b, (((0,), (0,)), ((), ())), preferred_element_type=F32)


def log_rows(width):
    return -(-TERMS * (width // HEAD_DIM) // 16) * 16


def pack_logs(logs):
    width = logs.shape[1]
    heads = width // HEAD_DIM
    shape = (log_rows(width), width)
    row = lax.broadcasted_iota(jnp.int32, shape, 0)
    lane = lax.broadcasted_iota(jnp.int32, shape, 1)
    total, rest = None, logs
    for term in range(TERMS):
        part = rest.astype(BF16)
        rest = rest - part.astype(F32)
        at = row - term * heads
        pick = (at >= 0) & (at < heads) & (lane == at * HEAD_DIM)
        found = nt(jnp.where(pick, 1.0, 0.0).astype(BF16), part)
        total = found if total is None else total + found
    return total.astype(BF16)


def unpack_logs(packed, width):
    heads = width // HEAD_DIM
    shape = (packed.shape[0], width)
    row = lax.broadcasted_iota(jnp.int32, shape, 0)
    lane_head = lax.shift_right_logical(lax.broadcasted_iota(jnp.int32, shape, 1), 6)
    spread = functools.reduce(
        jnp.logical_or, [row == lane_head + term * heads for term in range(TERMS)]
    )
    return tn(packed, jnp.where(spread, 1.0, 0.0).astype(BF16))


def merge(values_a, logs_a, values_b, logs_b):
    top = jnp.maximum(logs_a, logs_b)
    part_a, part_b = jnp.exp2(logs_a - top), jnp.exp2(logs_b - top)
    whole = part_a + part_b
    return (part_a * values_a + part_b * values_b) / whole, top + jnp.log2(whole)


def scale_row(softness_ref, which, heads):
    first = lax.axis_index("qgrp") * heads
    lane_head = lax.shift_right_logical(
        lax.broadcasted_iota(jnp.int32, (1, heads * HEAD_DIM), 1), 6
    )
    row = jnp.zeros((1, heads * HEAD_DIM), F32)
    for head in range(heads):
        row = jnp.where(lane_head == head, softness_ref[which, first + head], row)
    return row * (HEAD_DIM**-0.5 * LOG2E)


def split_scaled(queries, row):
    scaled = queries.astype(BF16).astype(F32) * row
    high = scaled.astype(BF16)
    return high, (scaled - high.astype(F32)).astype(BF16)


def pair_keys(keys):
    lane = lax.broadcasted_iota(jnp.int32, keys.shape, 1)
    zero = jnp.zeros_like(keys)
    first, second = jnp.where(lane < HEAD_DIM, keys, zero), jnp.where(lane < HEAD_DIM, zero, keys)
    return jnp.concatenate(
        [jnp.concatenate([first, first], axis=1), jnp.concatenate([second, second], axis=1)], axis=0
    )


def pair_values(values, counted):
    lane = lax.broadcasted_iota(jnp.int32, values.shape, 1)
    zero = jnp.zeros_like(values)
    low = lane < HEAD_DIM
    top = jnp.concatenate([jnp.where(low, values, zero), jnp.where(low, counted, zero)], axis=1)
    end = jnp.concatenate([jnp.where(low, zero, values), jnp.where(low, zero, counted)], axis=1)
    return jnp.concatenate([top, end], axis=0)


def attend_pair(high, low, keys, values):
    count = keys.shape[0] // 2
    scores = nt(jnp.concatenate([high, low], axis=1), keys)
    top_a = jnp.max(scores[:, :count], axis=1, keepdims=True)
    top_b = jnp.max(scores[:, count:], axis=1, keepdims=True)
    weights = jnp.concatenate(
        [
            jnp.exp2(scores[:, :count] - top_a).astype(BF16),
            jnp.exp2(scores[:, count:] - top_b).astype(BF16),
        ],
        axis=1,
    )
    sums = nn(weights, values)
    lane = lax.broadcasted_iota(jnp.int32, (high.shape[0], PAIR), 1)
    top = jnp.where(lane < HEAD_DIM, top_a, top_b)
    return sums[:, :PAIR], sums[:, PAIR:], top


def encode_quads(quads, latents, query_weight, keys, values, count, softness, put):
    width = query_weight.shape[1]
    rows = latents.shape[0] // 4
    slots = keys.shape[0]
    row = scale_row(softness, 0, width // HEAD_DIM)
    counted = jnp.where(
        lax.broadcasted_iota(jnp.int32, (slots, PAIR), 0) < count, 1.0, 0.0
    ).astype(BF16)
    queries = []
    for quad in quads:
        part = latents[pl.ds(pl.multiple_of(quad * rows, rows), rows), :]
        queries.append(split_scaled(nn(part, query_weight[...]), row))
    for pair in range(width // PAIR):
        lanes = slice(pair * PAIR, (pair + 1) * PAIR)
        key_block = pair_keys(keys[:, lanes])
        value_block = pair_values(values[:, lanes], counted)
        for index in range(len(quads)):
            high, low = queries[index]
            sums, total, top = attend_pair(high[:, lanes], low[:, lanes], key_block, value_block)
            put(index, lanes, sums / total, top + jnp.log2(total))


def bits_of():
    cell, core = lax.axis_index("cell"), lax.axis_index("qgrp")
    quad = jnp.bitwise_and(cell, 3)
    return quad, core


def encode_send_kernel(
    count, softness, latents, tokens, wq, wk, wv, message, keys_out, values_out, logs
):
    quad, core = bits_of()
    slots, rows = tokens.shape[0], latents.shape[0] // 4
    is_valid = lax.broadcasted_iota(jnp.int32, keys_out.shape, 0) < count[0]
    keys = nn(tokens[...], wk[...])
    keys_out[...] = jnp.where(is_valid, keys, keys[0:1, :]).astype(BF16)
    values_out[...] = jnp.where(is_valid, nn(tokens[...], wv[...]), 0.0).astype(BF16)

    def put(index, lanes, values, log):
        message[index, :rows, lanes] = values.astype(BF16)
        logs[index, :, lanes] = log

    quads = [jnp.bitwise_xor(quad, 3), jnp.bitwise_xor(quad, 1 + core)]
    encode_quads(quads, latents, wq, keys_out, values_out, count[0], softness, put)
    for index in range(2):
        message[index, rows:, :] = jnp.zeros_like(message[index, rows:, :])
        message[index, rows:, :rows] = pack_logs(logs[index])


def encode_keep_kernel(count, softness, latents, wq, keys, values, kept, logs):
    quad, core = bits_of()

    def put(index, lanes, part, log):
        kept[index, :, lanes] = part
        logs[index, :, lanes] = log

    quads = [jnp.bitwise_xor(quad, 2 - core), quad]
    encode_quads(quads, latents, wq, keys, values, count[0], softness, put)


def write_message(message, values, logs):
    rows = values.shape[0]
    message[:rows, :] = values.astype(BF16)
    message[rows:, :] = jnp.zeros_like(message[rows:, :])
    message[rows:, :rows] = pack_logs(logs)


def read_message(message, rows):
    width = message.shape[1]
    return message[:rows, :].astype(F32), unpack_logs(message[rows:, :rows], width)


def merge_two_kernel(values, logs, came, message, kept, kept_logs):
    rows = values.shape[1]
    for index in range(2):
        part, log = merge(values[index], logs[index], *read_message(came.at[index], rows))
        if index == 0:
            write_message(message, part, log)
        else:
            kept[...] = part
            kept_logs[...] = log


def merge_one_kernel(values, logs, came, message):
    rows = values.shape[0]
    part, log = merge(values[...], logs[...], *read_message(came, rows))
    write_message(message, part, log)


def merge_even_kernel(own_bit, other_bit, last, rows, mine, came, out):
    core = lax.axis_index("qgrp")
    bit = jnp.where(core == 0, own_bit, other_bit)
    is_low = jnp.bitwise_and(lax.axis_index("cell"), bit) == 0

    def both(first, second):
        part, log = merge(*read_message(first, rows), *read_message(second, rows))
        if last:
            out[...] = part.astype(BF16)
        else:
            write_message(out, part, log)

    @pl.when(is_low)
    def _():
        both(mine, came)

    @pl.when(jnp.logical_not(is_low))
    def _():
        both(came, mine)


def latent_kernel(attended, other, weight, other_weight, latents, gain, out):
    quad, core = bits_of()
    rows = attended.shape[0]
    start = pl.ds(pl.multiple_of(quad * rows, rows), rows)

    def finish(first, second, first_weight, second_weight):
        update = nn(first[...], first_weight[...]) + nn(second[...], second_weight[...])
        pre = latents[start, :].astype(F32) + update
        mean_square = jnp.mean(pre * pre, axis=-1, keepdims=True)
        out[...] = (pre * lax.rsqrt(mean_square + NORM_EPSILON) * gain[...]).astype(BF16)

    @pl.when(core == 0)
    def _():
        finish(attended, other, weight, other_weight)

    @pl.when(core != 0)
    def _():
        finish(other, attended, other_weight, weight)


def decode_kernel(softness, tokens, wq, wk, wv, own, x_side, y_side, diag_low, diag_high,
                  latent_out, send, keep, gathered):
    quad, core = bits_of()
    rows = own.shape[0]
    width = wq.shape[1]
    pieces = [(own, quad), (x_side, quad ^ 1), (y_side, quad ^ 2)]
    for index, (piece, at) in enumerate(pieces):
        gathered[index * rows:(index + 1) * rows, :] = piece[...]
        latent_out[pl.ds(pl.multiple_of(at * rows, rows), rows), :] = piece[...].astype(F32)
    half = diag_low.shape[0]
    for index, piece in enumerate([diag_low, diag_high]):
        start = 3 * rows + index * half
        gathered[start:start + half, :] = piece[...]
        at = (quad ^ 3) * rows + index * half
        latent_out[pl.ds(pl.multiple_of(at, half), half), :] = piece[...].astype(F32)
    keys = nn(gathered[...], wk[...]).astype(BF16)
    values = nn(gathered[...], wv[...]).astype(BF16)
    row = scale_row(softness, 1, width // HEAD_DIM)
    block = tokens.shape[0] // 2
    outs = [send, keep]
    queries = []
    for index in range(2):
        at = core if index else 1 - core
        part = tokens[pl.ds(pl.multiple_of(at * block, block), block), :]
        queries.append(split_scaled(nn(part, wq[...]), row))
    one = jnp.ones((keys.shape[0], PAIR), BF16)
    for pair in range(width // PAIR):
        lanes = slice(pair * PAIR, (pair + 1) * PAIR)
        key_block = pair_keys(keys[:, lanes])
        value_block = pair_values(values[:, lanes], one)
        for index in range(2):
            high, low = queries[index]
            sums, total, _ = attend_pair(high[:, lanes], low[:, lanes], key_block, value_block)
            outs[index][:, lanes] = (sums / total).astype(BF16)


def tokens_kernel(count, attended, other, weight, other_weight, tokens, out):
    core = lax.axis_index("qgrp")
    rows = attended.shape[0]
    update = nn(attended[...], weight[...]) + nn(other[...], other_weight[...])
    start = core * rows
    own = tokens[pl.ds(pl.multiple_of(start, rows), rows), :].astype(F32)
    is_valid = start + lax.broadcasted_iota(jnp.int32, out.shape, 0) < count[0]
    out[...] = jnp.where(is_valid, own + update, 0.0)


VMEM = pl.BlockSpec(memory_space=pltpu.VMEM)
SMEM = pl.BlockSpec(memory_space=pltpu.SMEM)


def call(kernel, ins, outs, *args, scratch=(), vmem=24, flops=0, name=None):
    shapes = [jax.ShapeDtypeStruct(*out) for out in outs]
    moved = sum(a.size * a.dtype.itemsize for a in [*args, *shapes])
    return pl.pallas_call(
        kernel,
        out_shape=shapes,
        in_specs=[SMEM if kind == "s" else VMEM for kind in ins],
        out_specs=[VMEM] * len(outs),
        scratch_shapes=list(scratch),
        compiler_params=pltpu.CompilerParams(vmem_limit_bytes=vmem * MIB),
        cost_estimate=pl.CostEstimate(flops=flops, bytes_accessed=moved, transcendentals=0),
        name=name,
    )(*args)


def body(tokens, tally, latents, softness, wq, wk, wv, wo, dq, dk, dv, do, gain):
    cells = lax.axis_size("cell")
    total_rows, model = latents.shape
    rows, width = total_rows // 4, wq.shape[1]
    slots = tokens.shape[0]
    half_slots = slots // 2
    deep = rows + log_rows(width)

    def swap(array):
        return lax.ppermute(array, "qgrp", [(0, 1), (1, 0)])

    def trade(array, bit_0, bit_1):
        pairs = []
        for cell in range(cells):
            pairs.append((2 * cell, 2 * (cell ^ bit_0)))
            pairs.append((2 * cell + 1, 2 * (cell ^ bit_1) + 1))
        return lax.ppermute(array, ("cell", "qgrp"), pairs)

    attention = 4 * 512 * slots * width * 4
    message, keys, values = call(
        encode_send_kernel, "ssvvvvv",
        [((2, deep, width), BF16), ((slots, width), BF16), ((slots, width), BF16)],
        tally, softness, latents, tokens, wq, wk, wv,
        scratch=[pltpu.VMEM((2, rows, width), F32)], flops=attention, name="encode_send",
    )
    came = trade(message, 1, 2)
    kept, kept_logs = call(
        encode_keep_kernel, "ssvvvv",
        [((2, rows, width), F32), ((2, rows, width), F32)],
        tally, softness, latents, wq, keys, values, flops=attention, name="encode_keep",
    )
    other_wo, other_do = swap(wo), swap(do)
    message, kept, kept_logs = call(
        merge_two_kernel, "vvv",
        [((deep, width), BF16), ((rows, width), F32), ((rows, width), F32)],
        kept, kept_logs, came, name="merge_two",
    )
    came = trade(message, 2, 1)
    (message,) = call(
        merge_one_kernel, "vvv", [((deep, width), BF16)], kept, kept_logs, came, name="merge_one"
    )
    bits = [4 << i for i in range(max(cells.bit_length() - 3, 0))]
    for index, (bit_0, bit_1) in enumerate(zip(bits, bits[::-1])):
        last = index == len(bits) - 1
        came = trade(message, bit_0, bit_1)
        (message,) = call(
            functools.partial(merge_even_kernel, bit_0, bit_1, last, rows), "vv",
            [((rows if last else deep, width), BF16)], message, came, name="merge_even",
        )
    attended = message[:rows]
    (own,) = call(
        latent_kernel, "vvvvvv", [((rows, model), BF16)],
        attended, swap(attended), wo, other_wo, latents, gain.reshape(1, model), name="latent",
    )
    came = trade(own, 1, 2)
    back = swap(came)
    core = lax.axis_index("qgrp")
    x_side = jnp.where(core == 0, came, back)
    y_side = jnp.where(core == 0, back, came)
    half = rows // 2
    piece = trade(jnp.where(core == 0, y_side[:half], x_side[half:]), 1, 2)
    piece_back = swap(piece)
    diag_low = jnp.where(core == 0, piece, piece_back)
    diag_high = jnp.where(core == 0, piece_back, piece)
    latent_out, send, keep = call(
        decode_kernel, "svvvvvvvvv",
        [((total_rows, model), F32), ((half_slots, width), BF16), ((half_slots, width), BF16)],
        softness, tokens, dq, dk, dv, own, x_side, y_side, diag_low, diag_high,
        scratch=[pltpu.VMEM((total_rows, model), BF16)], vmem=40, name="decode",
    )
    (tokens_out,) = call(
        tokens_kernel, "svvvvv", [((half_slots, model), F32)],
        tally, keep, swap(send), do, other_do, tokens, name="tokens",
    )
    return latent_out, tokens_out


def solution(mesh):
    placed = (
        P("cell", None), P("cell"), P(), P(),
        P(None, "qgrp"), P(None, "qgrp"), P(None, "qgrp"), P("qgrp", None),
        P(None, "qgrp"), P(None, "qgrp"), P(None, "qgrp"), P("qgrp", None), P(),
    )
    return jax.shard_map(
        body, mesh=mesh, in_specs=placed, out_specs=(P(), P(("cell", "qgrp"), None)),
        check_vma=False,
    )
```

```python
import functools
import math

import jax
import jax.numpy as jnp
from jax import lax
from jax.experimental import pallas as pl
from jax.experimental.pallas import tpu as pltpu
from jax.sharding import PartitionSpec as P

HEAD_DIM = 64
PAIR = 2 * HEAD_DIM
NORM_EPSILON = 1e-06
LOG2E = math.log2(math.e)
F32 = jnp.float32
BF16 = jnp.bfloat16
MIB = 1 << 20


def nn(a, b):
    return lax.dot_general(a, b, (((1,), (0,)), ((), ())), preferred_element_type=F32)


def nt(a, b):
    return lax.dot_general(a, b, (((1,), (1,)), ((), ())), preferred_element_type=F32)


def tn(a, b):
    return lax.dot_general(a, b, (((0,), (0,)), ((), ())), preferred_element_type=F32)


def log_rows(width):
    return -(-2 * (width // HEAD_DIM) // 16) * 16


def spread_of(shape, first, heads):
    row = lax.broadcasted_iota(jnp.int32, shape, 0) - first
    lane = lax.broadcasted_iota(jnp.int32, shape, 1)
    return row, lane, (row >= 0) & (row < heads)


def pack_logs(logs):
    rows, width = logs.shape
    heads, half = width // HEAD_DIM, rows // 2

    def found(part, first):
        row, lane, inside = spread_of((log_rows(width), width), first, heads)
        pick = inside & (lane == row * HEAD_DIM)
        return nt(jnp.where(pick, 1.0, 0.0).astype(BF16), part)

    high = logs.astype(BF16)
    rest = logs - high.astype(F32)
    middle = rest.astype(BF16)
    low = (rest - middle.astype(F32)).astype(BF16)
    below = found(high, 0) + found(middle, heads)
    beside = found(low[:half], 0) + found(low[half:], heads)
    return jnp.concatenate([below, beside], axis=1).astype(BF16)


def unpack_logs(packed, width):
    heads = width // HEAD_DIM
    rows = packed.shape[1] * 2 // 3

    def spread(first):
        row, lane, inside = spread_of((packed.shape[0], width), first, heads)
        return inside & (lax.shift_right_logical(lane, 6) == row)

    def as_matrix(mask):
        return jnp.where(mask, 1.0, 0.0).astype(BF16)

    top, end = spread(0), spread(heads)
    beside = packed[:, rows:]
    low = jnp.concatenate([tn(beside, as_matrix(top)), tn(beside, as_matrix(end))], axis=0)
    return tn(packed[:, :rows], as_matrix(top | end)) + low


def merge(values_a, logs_a, values_b, logs_b):
    top = jnp.maximum(logs_a, logs_b)
    part_a, part_b = jnp.exp2(logs_a - top), jnp.exp2(logs_b - top)
    whole = part_a + part_b
    return (part_a * values_a + part_b * values_b) / whole, top + jnp.log2(whole)


def scale_row(softness_ref, which, heads):
    first = lax.axis_index("qgrp") * heads
    lane_head = lax.shift_right_logical(
        lax.broadcasted_iota(jnp.int32, (1, heads * HEAD_DIM), 1), 6
    )
    row = jnp.zeros((1, heads * HEAD_DIM), F32)
    for head in range(heads):
        row = jnp.where(lane_head == head, softness_ref[which, first + head], row)
    return row * (HEAD_DIM**-0.5 * LOG2E)


def split_scaled(queries, row):
    scaled = queries.astype(BF16).astype(F32) * row
    high = scaled.astype(BF16)
    return high, (scaled - high.astype(F32)).astype(BF16)


def pair_keys(keys):
    lane = lax.broadcasted_iota(jnp.int32, keys.shape, 1)
    zero = jnp.zeros_like(keys)
    first, second = jnp.where(lane < HEAD_DIM, keys, zero), jnp.where(lane < HEAD_DIM, zero, keys)
    return jnp.concatenate(
        [jnp.concatenate([first, first], axis=1), jnp.concatenate([second, second], axis=1)], axis=0
    )


def pair_values(values, counted):
    lane = lax.broadcasted_iota(jnp.int32, values.shape, 1)
    zero = jnp.zeros_like(values)
    low = lane < HEAD_DIM
    top = jnp.concatenate([jnp.where(low, values, zero), jnp.where(low, counted, zero)], axis=1)
    end = jnp.concatenate([jnp.where(low, zero, values), jnp.where(low, zero, counted)], axis=1)
    return jnp.concatenate([top, end], axis=0)


def attend_pair(high, low, keys, values):
    count = keys.shape[0] // 2
    scores = nt(jnp.concatenate([high, low], axis=1), keys)
    top_a = jnp.max(scores[:, :count], axis=1, keepdims=True)
    top_b = jnp.max(scores[:, count:], axis=1, keepdims=True)
    weights = jnp.concatenate(
        [
            jnp.exp2(scores[:, :count] - top_a).astype(BF16),
            jnp.exp2(scores[:, count:] - top_b).astype(BF16),
        ],
        axis=1,
    )
    sums = nn(weights, values)
    lane = lax.broadcasted_iota(jnp.int32, (high.shape[0], PAIR), 1)
    top = jnp.where(lane < HEAD_DIM, top_a, top_b)
    return sums[:, :PAIR], sums[:, PAIR:], top


def encode_rows(part, query_weight, keys, values, count, scale, put):
    width = query_weight.shape[1]
    slots = keys.shape[0]
    slot = lax.broadcasted_iota(jnp.int32, (slots, PAIR), 0)
    counted = jnp.where(slot < count, 1.0, 0.0).astype(BF16)
    high, low = split_scaled(nn(part, query_weight[...]), scale)
    for pair in range(width // PAIR):
        lanes = slice(pair * PAIR, (pair + 1) * PAIR)
        key_block = pair_keys(keys[:, lanes])
        value_block = pair_values(values[:, lanes], counted)
        sums, total, top = attend_pair(high[:, lanes], low[:, lanes], key_block, value_block)
        put(lanes, sums / total, top + jnp.log2(total))


def bits_of():
    cell, core = lax.axis_index("cell"), lax.axis_index("qgrp")
    quad = jnp.bitwise_and(cell, 3)
    return quad, core


def start_all(pairs, arrived):
    moves = [
        pltpu.make_async_copy(source, goal, arrived.at[index])
        for index, (source, goal) in enumerate(pairs)
    ]
    for move in moves:
        move.start()
    return moves


def wait_all(moves):
    for move in moves:
        move.wait()


def quarter(latents, quad, rows):
    return latents.at[pl.ds(pl.multiple_of(quad * rows, rows), rows), :]


def encode_first_kernel(
    tally, softness_far, latents_far, tokens_far, wq_far, wk_far, wv_far,
    message, keys, values, scales, count_out,
    count, softness, latents, tokens, wq, wk, wv, logs, arrived,
):
    quad, core = bits_of()
    rows = latents.shape[0]
    moves = start_all(
        [
            (tally, count), (tokens_far, tokens), (wk_far, wk), (wv_far, wv), (wq_far, wq),
            (softness_far, softness), (quarter(latents_far, quad ^ 3, rows), latents),
        ],
        arrived,
    )
    wait_all(moves[:3])
    is_valid = lax.broadcasted_iota(jnp.int32, keys.shape, 0) < count[0]
    made = nn(tokens[...], wk[...])
    keys[...] = jnp.where(is_valid, made, made[0:1, :]).astype(BF16)
    moves[3].wait()
    values[...] = jnp.where(is_valid, nn(tokens[...], wv[...]), 0.0).astype(BF16)
    wait_all(moves[4:])
    count_out[...] = jnp.full(count_out.shape, count[0], jnp.int32)
    for which in range(2):
        row = scale_row(softness, which, wq.shape[1] // HEAD_DIM)
        scales[which] = jnp.broadcast_to(row, scales.shape[1:])
    encode_into(message, latents[...], wq, keys, values, count_out, scales, logs)


def encode_into(message, part, wq, keys, values, count, scales, logs):
    rows = part.shape[0]

    def put(lanes, sums, log):
        message[:rows, lanes] = sums.astype(BF16)
        logs[:, lanes] = log

    encode_rows(part, wq, keys, values, count[0:1, :], scales[0, 0:1, :], put)
    message[rows:, :] = pack_logs(logs[...])


def encode_side_kernel(
    bit_0, bit_1, count, scales, latents, wq, keys, values, message, logs
):
    quad, core = bits_of()
    rows = logs.shape[0]
    side = quad ^ jnp.where(core == 0, bit_0, bit_1)
    part = quarter(latents, side, rows)[...]
    encode_into(message, part, wq, keys, values, count, scales, logs)


def encode_own_kernel(count, scales, latents, wq, keys, values, came, kept, logs):
    quad, core = bits_of()
    rows = kept.shape[0]

    def put(lanes, part, log):
        kept[:, lanes] = part
        logs[:, lanes] = log

    part = quarter(latents, quad, rows)[...]
    encode_rows(part, wq, keys, values, count[0:1, :], scales[0, 0:1, :], put)
    kept[...], logs[...] = merge(kept[...], logs[...], *read_message(came, rows))


def write_message(message, values, logs):
    rows = values.shape[0]
    message[:rows, :] = values.astype(BF16)
    message[rows:, :] = pack_logs(logs)


def read_message(message, rows):
    width = message.shape[1]
    return message[:rows, :].astype(F32), unpack_logs(message[rows:, :], width)


def merge_sides_kernel(values, logs, first, second, message):
    rows = values.shape[0]
    part, log = merge(values[...], logs[...], *read_message(first, rows))
    part, log = merge(part, log, *read_message(second, rows))
    write_message(message, part, log)


def merge_even_kernel(own_bit, other_bit, last, rows, mine, came, out):
    core = lax.axis_index("qgrp")
    bit = jnp.where(core == 0, own_bit, other_bit)
    is_low = jnp.bitwise_and(lax.axis_index("cell"), bit) == 0

    def both(first, second):
        part, log = merge(*read_message(first, rows), *read_message(second, rows))
        if last:
            out[...] = part.astype(BF16)
        else:
            write_message(out, part, log)

    @pl.when(is_low)
    def _():
        both(mine, came)

    @pl.when(jnp.logical_not(is_low))
    def _():
        both(came, mine)


def latent_kernel(attended, other, weight, other_weight, latents, gain, out, half):
    quad, core = bits_of()
    rows = attended.shape[0]
    start = pl.ds(pl.multiple_of(quad * rows, rows), rows)

    def finish(first, second, first_weight, second_weight):
        update = nn(first[...], first_weight[...]) + nn(second[...], second_weight[...])
        pre = latents[start, :].astype(F32) + update
        mean_square = jnp.mean(pre * pre, axis=-1, keepdims=True)
        out[...] = (pre * lax.rsqrt(mean_square + NORM_EPSILON) * gain[...]).astype(BF16)

    @pl.when(core == 0)
    def _():
        finish(attended, other, weight, other_weight)
        half[...] = out[:rows // 2, :]

    @pl.when(core != 0)
    def _():
        finish(other, attended, other_weight, weight)
        half[...] = out[rows // 2:, :]


def decode_queries_kernel(scales, tokens, wq, out):
    width = wq.shape[1]
    high, low = split_scaled(nn(tokens[...], wq[...]), scales[1, 0:1, :])
    for pair in range(width // PAIR):
        lanes = slice(pair * PAIR, (pair + 1) * PAIR)
        out[pair, :, :PAIR] = high[:, lanes]
        out[pair, :, PAIR:] = low[:, lanes]


def place_rows(pieces, spots, latent_out, staged, sent):
    moves, start = [], 0
    for index, (piece, spot) in enumerate(zip(pieces, spots)):
        count = piece.shape[0]
        staged[start:start + count, :] = piece[...].astype(F32)
        moves.append(
            pltpu.make_async_copy(
                staged.at[pl.ds(start, count), :],
                latent_out.at[pl.ds(pl.multiple_of(spot, count), count), :],
                sent.at[index],
            )
        )
        moves[-1].start()
        start += count
    return moves


def decode_part(queries, keys, values, state, lanes):
    high, low = queries[:, :PAIR], queries[:, PAIR:]
    one = jnp.ones((keys.shape[0], PAIR), BF16)
    sums, total, top = attend_pair(high, low, pair_keys(keys), pair_values(values, one))
    if state is None:
        return sums, total, top
    old_sums, old_total, old_top = state
    new_top = jnp.maximum(top, old_top)
    old, new = jnp.exp2(old_top - new_top), jnp.exp2(top - new_top)
    return old * old_sums + new * sums, old * old_total + new * total, new_top


def decode_step_kernel(is_first, where, *refs):
    queries, wk, wv, *refs = refs
    quad, core = bits_of()
    count = len(where(quad, core, 0))
    pieces, refs = refs[:count], refs[count:]
    state = None
    if not is_first:
        _, *state = refs[:4]
        refs = refs[4:]
    latent_out, sums, total, top, gathered, staged, sent = refs
    model = gathered.shape[1]
    rows = latent_out.shape[0] // 4
    moves = place_rows(pieces, where(quad, core, rows), latent_out, staged, sent)
    start = 0
    for piece in pieces:
        gathered[start:start + piece.shape[0], :] = piece[...]
        start += piece.shape[0]
    keys = nn(gathered[...], wk[...]).astype(BF16)
    values = nn(gathered[...], wv[...]).astype(BF16)
    block = queries.shape[1] // 2
    for pair in range(queries.shape[0]):
        lanes = slice(pair * PAIR, (pair + 1) * PAIR)
        for index in range(2):
            at = slice(index * block, (index + 1) * block)
            old = None if is_first else [part[at, lanes] for part in state]
            new = decode_part(queries[pair, at, :], keys[:, lanes], values[:, lanes], old, lanes)
            for out, part in zip((sums, total, top), new):
                out[at, lanes] = part
    for move in moves:
        move.wait()


def decode_send_kernel(
    queries, wk, wv, mine, came, latent_in, sums, total, top,
    latent_out, send, keys, values, gathered, staged, sent,
):
    quad, core = bits_of()
    rows, half = latent_out.shape[0] // 4, mine.shape[0]
    diagonal = (quad ^ 3) * rows
    spots = [diagonal + core * half, diagonal + (1 - core) * half]
    moves = place_rows([mine, came], spots, latent_out, staged, sent)
    gathered[:half, :] = mine[...]
    gathered[half:, :] = came[...]
    keys[...] = nn(gathered[...], wk[...]).astype(BF16)
    values[...] = nn(gathered[...], wv[...]).astype(BF16)
    decode_last(1 - core, queries, keys, values, sums, total, top, send)
    for move in moves:
        move.wait()


def decode_last(which, queries, keys, values, sums, total, top, out):
    block = out.shape[0]
    at = pl.ds(pl.multiple_of(which * block, block), block)
    for pair in range(queries.shape[0]):
        lanes = slice(pair * PAIR, (pair + 1) * PAIR)
        old = [part[at, lanes] for part in (sums, total, top)]
        new = decode_part(queries[pair, at, :], keys[:, lanes], values[:, lanes], old, lanes)
        out[:, lanes] = (new[0] / new[1]).astype(BF16)


def decode_keep_kernel(queries, keys, values, sums, total, top, keep):
    core = lax.axis_index("qgrp")
    decode_last(core, queries, keys, values, sums, total, top, keep)


def tokens_kernel(count, attended, other, weight, other_weight, tokens, out):
    core = lax.axis_index("qgrp")
    rows = attended.shape[0]
    update = nn(attended[...], weight[...]) + nn(other[...], other_weight[...])
    start = core * rows
    own = tokens[pl.ds(pl.multiple_of(start, rows), rows), :].astype(F32)
    is_valid = start + lax.broadcasted_iota(jnp.int32, out.shape, 0) < count[0:1, 0:1]
    out[...] = jnp.where(is_valid, own + update, 0.0)


SPACES = {
    "v": pl.BlockSpec(memory_space=pltpu.VMEM),
    "h": pl.BlockSpec(memory_space=pltpu.HBM),
    "a": pl.BlockSpec(memory_space=pl.ANY),
}


def call(kernel, ins, outs, *args, far=(), alias=None, scratch=(), vmem=24, flops=0, after=(),
         name=None):
    given, more = len(args), len(after)
    args = [
        pltpu.with_memory_space_constraint(arg, pltpu.HBM) if kind == "h" else arg
        for kind, arg in zip(ins, args)
    ]
    if more:
        alone = kernel

        def kernel(*refs):
            alone(*refs[:given], *refs[given + more:])

    shapes = [jax.ShapeDtypeStruct(*out) for out in outs]
    moved = sum(a.size * a.dtype.itemsize for a in [*args, *shapes])
    return pl.pallas_call(
        kernel,
        out_shape=shapes,
        in_specs=[SPACES[kind] for kind in ins + "h" * more],
        out_specs=[SPACES["h" if index in far else "v"] for index in range(len(outs))],
        input_output_aliases=alias or {},
        scratch_shapes=list(scratch),
        compiler_params=pltpu.CompilerParams(vmem_limit_bytes=vmem * MIB),
        cost_estimate=pl.CostEstimate(flops=flops, bytes_accessed=moved, transcendentals=0),
        name=name,
    )(*args, *after)


def body(tokens, tally, latents, softness, wq, wk, wv, wo, dq, dk, dv, do, gain):
    cells = lax.axis_size("cell")
    total_rows, model = latents.shape
    rows, width = total_rows // 4, wq.shape[1]
    slots = tokens.shape[0]
    half_slots = slots // 2
    deep = rows + log_rows(width)

    def swap(array):
        return lax.ppermute(array, "qgrp", [(0, 1), (1, 0)])

    def trade(array, bit_0, bit_1):
        pairs = []
        for cell in range(cells):
            pairs.append((2 * cell, 2 * (cell ^ bit_0)))
            pairs.append((2 * cell + 1, 2 * (cell ^ bit_1) + 1))
        return lax.ppermute(array, ("cell", "qgrp"), pairs)

    attention = 4 * 256 * slots * width * 4
    sent = ((deep, width), BF16)
    message, keys, values, scales, count = call(
        encode_first_kernel, "ahhhhhh",
        [
            sent, *[((slots, width), BF16)] * 2,
            ((2, 8, width), F32), ((8, PAIR), jnp.int32),
        ],
        tally, softness, latents, tokens, wq, wk, wv,
        scratch=[
            pltpu.SMEM(tally.shape, tally.dtype), pltpu.SMEM(softness.shape, F32),
            pltpu.VMEM((rows, model), BF16), pltpu.VMEM(tokens.shape, BF16),
            *[pltpu.VMEM((model, width), BF16)] * 3, pltpu.VMEM((rows, width), F32),
            pltpu.SemaphoreType.DMA((7,)),
        ],
        flops=attention, name="encode_corner",
    )
    corner = trade(message, 3, 3)

    def encode_side(bit_0, bit_1, after):
        (message,) = call(
            functools.partial(encode_side_kernel, bit_0, bit_1), "vvvvvv", [sent],
            count, scales, latents, wq, keys, values,
            scratch=[pltpu.VMEM((rows, width), F32)],
            flops=attention, after=after, name="encode_side",
        )
        return message

    message = encode_side(1, 2, [])
    first = trade(message, 1, 2)
    message = encode_side(2, 1, [message])
    second = trade(message, 2, 1)
    kept, kept_logs = call(
        encode_own_kernel, "vvvvvvv", [((rows, width), F32)] * 2,
        count, scales, latents, wq, keys, values, corner,
        flops=attention, after=[message], name="encode_own",
    )
    other_wo, other_do = swap(wo), swap(do)
    (message,) = call(
        merge_sides_kernel, "vvvv", [sent], kept, kept_logs, first, second, name="merge_sides"
    )
    (queries,) = call(
        decode_queries_kernel, "vvv", [((width // PAIR, slots, 2 * PAIR), BF16)],
        scales, tokens, dq, after=[message], name="decode_queries",
    )
    bits = [4 << i for i in range(max(cells.bit_length() - 3, 0))]
    for index, (bit_0, bit_1) in enumerate(zip(bits, bits[::-1])):
        last = index == len(bits) - 1
        came = trade(message, bit_0, bit_1)
        (message,) = call(
            functools.partial(merge_even_kernel, bit_0, bit_1, last, rows), "vv",
            [((rows, width), BF16) if last else sent], message, came,
            after=[queries] if last else [], name="merge_even",
        )
    attended = message[:rows]
    half = rows // 2
    own, own_half = call(
        latent_kernel, "vvvvvv", [((rows, model), BF16), ((half, model), BF16)],
        attended, swap(attended), wo, other_wo, latents, gain.reshape(1, model), name="latent",
    )
    first = trade(own_half, 1, 2)
    second = trade(own_half, 2, 1)
    whole = ((total_rows, model), F32)
    state_out = [((slots, width), F32)] * 3

    def scratch(count, pieces):
        return [
            pltpu.VMEM((count, model), BF16), pltpu.VMEM((count, model), F32),
            pltpu.SemaphoreType.DMA((pieces,)),
        ]

    def own_spot(quad, core, rows):
        return [quad * rows]

    def side_spots(quad, core, rows):
        half = rows // 2
        return [
            (quad ^ (1 + core)) * rows + core * half,
            (quad ^ (2 - core)) * rows + (1 - core) * half,
            (quad ^ (2 - core)) * rows + core * half,
            (quad ^ (1 + core)) * rows + (1 - core) * half,
        ]

    latent_out, *state = call(
        functools.partial(decode_step_kernel, True, own_spot), "vvvv",
        [whole, *state_out], queries, dk, dv, own,
        far=(0,), scratch=scratch(rows, 1), flops=attention, name="decode_own",
    )
    first, own = lax.optimization_barrier((first, state[0]))
    state[0] = own
    third = trade(first, 2, 1)
    latent_out, *state = call(
        functools.partial(decode_step_kernel, False, side_spots), "vvvvvvvhvvv",
        [whole, *state_out], queries, dk, dv, first, swap(first), second, swap(second),
        latent_out, *state, far=(0,), alias={7: 0},
        scratch=scratch(2 * rows, 4), vmem=32, flops=2 * attention, name="decode_sides",
    )
    third, late = lax.optimization_barrier((third, state[0]))
    state[0] = late
    latent_out, send, keys, values = call(
        decode_send_kernel, "vvvvvhvvv",
        [whole, ((half_slots, width), BF16), *[((rows, width), BF16)] * 2],
        queries, dk, dv, third, swap(third), latent_out, *state, far=(0,), alias={5: 0},
        scratch=scratch(rows, 2), flops=attention // 2, name="decode_send",
    )
    (keep,) = call(
        decode_keep_kernel, "vvvvvv", [((half_slots, width), BF16)],
        queries, keys, values, *state, flops=attention // 2, name="decode_keep",
    )
    (tokens_out,) = call(
        tokens_kernel, "vvvvvv", [((half_slots, model), F32)],
        count, keep, swap(send), do, other_do, tokens, name="tokens",
    )
    return latent_out, tokens_out


def solution(mesh):
    placed = (
        P("cell", None), P("cell"), P(), P(),
        P(None, "qgrp"), P(None, "qgrp"), P(None, "qgrp"), P("qgrp", None),
        P(None, "qgrp"), P(None, "qgrp"), P(None, "qgrp"), P("qgrp", None), P(),
    )
    return jax.shard_map(
        body, mesh=mesh, in_specs=placed, out_specs=(P(), P(("cell", "qgrp"), None)),
        check_vma=False,
    )
```

```python
import functools
import math

import jax
import jax.numpy as jnp
from jax import lax
from jax.experimental import pallas as pl
from jax.experimental.pallas import tpu as pltpu
from jax.sharding import PartitionSpec as P

HEAD_DIM = 64
PAIR = 2 * HEAD_DIM
NORM_EPSILON = 1e-06
LOG2E = math.log2(math.e)
F32 = jnp.float32
BF16 = jnp.bfloat16
MIB = 1 << 20


def nn(a, b):
    return lax.dot_general(a, b, (((1,), (0,)), ((), ())), preferred_element_type=F32)


def nt(a, b):
    return lax.dot_general(a, b, (((1,), (1,)), ((), ())), preferred_element_type=F32)


def tn(a, b):
    return lax.dot_general(a, b, (((0,), (0,)), ((), ())), preferred_element_type=F32)


def log_rows(width):
    return -(-2 * (width // HEAD_DIM) // 16) * 16


def spread_of(shape, first, heads):
    row = lax.broadcasted_iota(jnp.int32, shape, 0) - first
    lane = lax.broadcasted_iota(jnp.int32, shape, 1)
    return row, lane, (row >= 0) & (row < heads)


def pack_logs(logs):
    rows, width = logs.shape
    heads, half = width // HEAD_DIM, rows // 2

    def found(part, first):
        row, lane, inside = spread_of((log_rows(width), width), first, heads)
        pick = inside & (lane == row * HEAD_DIM)
        return nt(jnp.where(pick, 1.0, 0.0).astype(BF16), part)

    high = logs.astype(BF16)
    rest = logs - high.astype(F32)
    middle = rest.astype(BF16)
    low = (rest - middle.astype(F32)).astype(BF16)
    if 3 * rows <= width:
        return jnp.concatenate([found(part, 0) for part in (high, middle, low)], axis=1).astype(BF16)
    below = found(high, 0) + found(middle, heads)
    beside = found(low[:half], 0) + found(low[half:], heads)
    return jnp.concatenate([below, beside], axis=1).astype(BF16)


def unpack_logs(packed, rows, width):
    heads = width // HEAD_DIM

    def spread(first):
        row, lane, inside = spread_of((packed.shape[0], width), first, heads)
        return inside & (lax.shift_right_logical(lane, 6) == row)

    def as_matrix(mask):
        return jnp.where(mask, 1.0, 0.0).astype(BF16)

    top, end = spread(0), spread(heads)
    if 3 * rows <= width:
        terms = [packed[:, term * rows:(term + 1) * rows] for term in range(3)]
        return sum(tn(term, as_matrix(top)) for term in terms)
    beside = packed[:, rows:]
    low = jnp.concatenate([tn(beside, as_matrix(top)), tn(beside, as_matrix(end))], axis=0)
    return tn(packed[:, :rows], as_matrix(top | end)) + low


def merge(values_a, logs_a, values_b, logs_b):
    top = jnp.maximum(logs_a, logs_b)
    part_a, part_b = jnp.exp2(logs_a - top), jnp.exp2(logs_b - top)
    whole = part_a + part_b
    return (part_a * values_a + part_b * values_b) / whole, top + jnp.log2(whole)


def scale_row(softness_ref, which, heads):
    first = lax.axis_index("qgrp") * heads
    lane_head = lax.shift_right_logical(
        lax.broadcasted_iota(jnp.int32, (1, heads * HEAD_DIM), 1), 6
    )
    row = jnp.zeros((1, heads * HEAD_DIM), F32)
    for head in range(heads):
        row = jnp.where(lane_head == head, softness_ref[which, first + head], row)
    return row * (HEAD_DIM**-0.5 * LOG2E)


def split_scaled(queries, row):
    scaled = queries.astype(BF16).astype(F32) * row
    high = scaled.astype(BF16)
    return high, (scaled - high.astype(F32)).astype(BF16)


def pair_keys(keys):
    lane = lax.broadcasted_iota(jnp.int32, keys.shape, 1)
    zero = jnp.zeros_like(keys)
    first, second = jnp.where(lane < HEAD_DIM, keys, zero), jnp.where(lane < HEAD_DIM, zero, keys)
    return jnp.concatenate(
        [jnp.concatenate([first, first], axis=1), jnp.concatenate([second, second], axis=1)], axis=0
    )


def pair_values(values, counted):
    lane = lax.broadcasted_iota(jnp.int32, values.shape, 1)
    zero = jnp.zeros_like(values)
    low = lane < HEAD_DIM
    top = jnp.concatenate([jnp.where(low, values, zero), jnp.where(low, counted, zero)], axis=1)
    end = jnp.concatenate([jnp.where(low, zero, values), jnp.where(low, zero, counted)], axis=1)
    return jnp.concatenate([top, end], axis=0)


def attend_pair(high, low, keys, values):
    count = keys.shape[0] // 2
    scores = nt(jnp.concatenate([high, low], axis=1), keys)
    top_a = jnp.max(scores[:, :count], axis=1, keepdims=True)
    top_b = jnp.max(scores[:, count:], axis=1, keepdims=True)
    weights = jnp.concatenate(
        [
            jnp.exp2(scores[:, :count] - top_a).astype(BF16),
            jnp.exp2(scores[:, count:] - top_b).astype(BF16),
        ],
        axis=1,
    )
    sums = nn(weights, values)
    lane = lax.broadcasted_iota(jnp.int32, (high.shape[0], PAIR), 1)
    top = jnp.where(lane < HEAD_DIM, top_a, top_b)
    return sums[:, :PAIR], sums[:, PAIR:], top


def encode_rows(part, query_weight, keys, values, count, scale, put):
    width = query_weight.shape[1]
    slots = keys.shape[0]
    slot = lax.broadcasted_iota(jnp.int32, (slots, PAIR), 0)
    counted = jnp.where(slot < count, 1.0, 0.0).astype(BF16)
    high, low = split_scaled(nn(part, query_weight[...]), scale)
    for pair in range(width // PAIR):
        lanes = slice(pair * PAIR, (pair + 1) * PAIR)
        key_block = pair_keys(keys[:, lanes])
        value_block = pair_values(values[:, lanes], counted)
        sums, total, top = attend_pair(high[:, lanes], low[:, lanes], key_block, value_block)
        put(lanes, sums / total, top + jnp.log2(total))


def bits_of():
    cell, core = lax.axis_index("cell"), lax.axis_index("qgrp")
    quad = jnp.bitwise_and(cell, 3)
    return quad, core


def start_all(pairs, arrived):
    moves = [
        pltpu.make_async_copy(source, goal, arrived.at[index])
        for index, (source, goal) in enumerate(pairs)
    ]
    for move in moves:
        move.start()
    return moves


def wait_all(moves):
    for move in moves:
        move.wait()


def quarter(latents, quad, rows):
    return latents.at[pl.ds(pl.multiple_of(quad * rows, rows), rows), :]


def encode_first_kernel(
    tally, softness_far, latents_far, tokens_far, wq_far, wk_far, wv_far,
    message, keys, values, scales, count_out,
    count, softness, latents, tokens, wq, wk, wv, logs, arrived,
):
    quad, core = bits_of()
    rows = latents.shape[0]
    moves = start_all(
        [
            (tally, count), (tokens_far, tokens), (wk_far, wk), (wv_far, wv), (wq_far, wq),
            (softness_far, softness), (quarter(latents_far, quad ^ 3, rows), latents),
        ],
        arrived,
    )
    wait_all(moves[:3])
    is_valid = lax.broadcasted_iota(jnp.int32, keys.shape, 0) < count[0]
    made = nn(tokens[...], wk[...])
    keys[...] = jnp.where(is_valid, made, made[0:1, :]).astype(BF16)
    moves[3].wait()
    values[...] = jnp.where(is_valid, nn(tokens[...], wv[...]), 0.0).astype(BF16)
    wait_all(moves[4:])
    count_out[...] = jnp.full(count_out.shape, count[0], jnp.int32)
    for which in range(2):
        row = scale_row(softness, which, wq.shape[1] // HEAD_DIM)
        scales[which] = jnp.broadcast_to(row, scales.shape[1:])
    encode_into(message, latents[...], wq, keys, values, count_out, scales, logs)


def encode_into(message, part, wq, keys, values, count, scales, logs):
    rows = part.shape[0]

    def put(lanes, sums, log):
        message[:rows, lanes] = sums.astype(BF16)
        logs[:, lanes] = log

    encode_rows(part, wq, keys, values, count[0:1, :], scales[0, 0:1, :], put)
    message[rows:, :] = pack_logs(logs[...])


def encode_side_kernel(count, scales, latents, wq, keys, values, message, logs):
    quad, core = bits_of()
    rows = logs.shape[0]
    side = quad ^ jnp.where(core == 0, 1, 2)
    part = quarter(latents, side, rows)[...]
    encode_into(message, part, wq, keys, values, count, scales, logs)


def encode_keep_kernel(is_own, count, scales, latents, wq, keys, values, kept, logs):
    quad, core = bits_of()
    rows = kept.shape[0]

    def put(lanes, part, log):
        kept[:, lanes] = part
        logs[:, lanes] = log

    at = quad if is_own else quad ^ jnp.where(core == 0, 2, 1)
    part = quarter(latents, at, rows)[...]
    encode_rows(part, wq, keys, values, count[0:1, :], scales[0, 0:1, :], put)

def write_message(message, values, logs):
    rows = values.shape[0]
    message[:rows, :] = values.astype(BF16)
    message[rows:, :] = pack_logs(logs)


def read_message(message, rows):
    width = message.shape[1]
    return message[:rows, :].astype(F32), unpack_logs(message[rows:, :], rows, width)


def merge_one_kernel(values, logs, came, message):
    rows = values.shape[0]
    part, log = merge(values[...], logs[...], *read_message(came, rows))
    write_message(message, part, log)


def merge_sides_kernel(which, values, logs, first, second, message):
    rows = values.shape[0]
    half = rows // 2
    at = slice(which * half, (which + 1) * half)
    part, log = values[at, :], logs[at, :]
    for came in (first, second):
        came_part, came_log = read_message(came, rows)
        part, log = merge(part, log, came_part[at], came_log[at])
    write_message(message, part, log)


def merge_even_kernel(own_bit, other_bit, last, rows, mine, came, out):
    core = lax.axis_index("qgrp")
    bit = jnp.where(core == 0, own_bit, other_bit)
    is_low = jnp.bitwise_and(lax.axis_index("cell"), bit) == 0

    def both(first, second):
        part, log = merge(*read_message(first, rows), *read_message(second, rows))
        if last:
            out[...] = part.astype(BF16)
        else:
            write_message(out, part, log)

    @pl.when(is_low)
    def _():
        both(mine, came)

    @pl.when(jnp.logical_not(is_low))
    def _():
        both(came, mine)


def latent_kernel(which, attended, other, weight, other_weight, latents, gain, *refs):
    quad, core = bits_of()
    half = attended.shape[0]
    start = pl.ds(pl.multiple_of((2 * quad + which) * half, half), half)

    def finish(first, second, first_weight, second_weight):
        update = nn(first[...], first_weight[...]) + nn(second[...], second_weight[...])
        pre = latents[start, :].astype(F32) + update
        mean_square = jnp.mean(pre * pre, axis=-1, keepdims=True)
        done = (pre * lax.rsqrt(mean_square + NORM_EPSILON) * gain[...]).astype(BF16)
        if which == 0:
            refs[0][...] = done
        else:
            low, out, own_half = refs
            out[:half, :] = low[...]
            out[half:, :] = done
            own_half[...] = jnp.where(core == 0, low[...], done)

    @pl.when(core == 0)
    def _():
        finish(attended, other, weight, other_weight)

    @pl.when(core != 0)
    def _():
        finish(other, attended, other_weight, weight)


def groups_of(pairs):
    first = -(-2 * pairs // 3)
    return [range(first), range(first, pairs)]


def decode_prepare_kernel(scales, tokens, wq, wk, wv, out, *weights):
    width = wq.shape[1]
    high, low = split_scaled(nn(tokens[...], wq[...]), scales[1, 0:1, :])
    for pair in range(width // PAIR):
        lanes = slice(pair * PAIR, (pair + 1) * PAIR)
        out[pair, :, :PAIR] = high[:, lanes]
        out[pair, :, PAIR:] = low[:, lanes]
    for group, both in zip(groups_of(width // PAIR), weights):
        lanes = slice(group[0] * PAIR, (group[-1] + 1) * PAIR)
        size = len(group) * PAIR
        both[:, :size] = wk[:, lanes]
        both[:, size:] = wv[:, lanes]


def place_rows(pieces, spots, latent_out, staged, sent):
    moves, start = [], 0
    for index, (piece, spot) in enumerate(zip(pieces, spots)):
        count = piece.shape[0]
        staged[start:start + count, :] = piece[...].astype(F32)
        moves.append(
            pltpu.make_async_copy(
                staged.at[pl.ds(start, count), :],
                latent_out.at[pl.ds(pl.multiple_of(spot, count), count), :],
                sent.at[index],
            )
        )
        moves[-1].start()
        start += count
    return moves


def decode_part(queries, keys, values, state):
    high, low = queries[:, :PAIR], queries[:, PAIR:]
    one = jnp.ones((keys.shape[0], PAIR), BF16)
    sums, total, top = attend_pair(high, low, pair_keys(keys), pair_values(values, one))
    if state is None:
        return sums, total, top
    old_sums, old_total, old_top = state
    new_top = jnp.maximum(top, old_top)
    old, new = jnp.exp2(old_top - new_top), jnp.exp2(top - new_top)
    return old * old_sums + new * sums, old * old_total + new * total, new_top


def decode_group(group, queries, both, at, state, put):
    size = len(group) * PAIR
    for place, pair in enumerate(group):
        lanes = slice(place * PAIR, (place + 1) * PAIR)
        value_lanes = slice(size + place * PAIR, size + (place + 1) * PAIR)
        old = None if state is None else [part[at, lanes] for part in state]
        put(lanes, pair, decode_part(queries[pair, at, :], both[:, lanes], both[:, value_lanes], old))


def decode_tokens(group, queries, both, state, new_state):
    block = queries.shape[1] // 2
    for index in range(2):
        at = slice(index * block, (index + 1) * block)

        def put(lanes, pair, new):
            for out, part in zip(new_state, new):
                out[at, lanes] = part

        decode_group(group, queries, both, at, state, put)


def decode_own_kernel(queries, weights, more_weights, own, latent_out, *refs):
    *states, staged, sent = refs
    quad, core = bits_of()
    rows = own.shape[0]
    moves = place_rows([own], [quad * rows], latent_out, staged, sent)
    for group, weight, state in zip(
        groups_of(queries.shape[0]), [weights, more_weights], [states[:3], states[3:]]
    ):
        both = nn(own[...], weight[...]).astype(BF16)
        decode_tokens(group, queries, both, None, state)
    wait_all(moves)


def decode_sides_kernel(queries, weights, mine_a, came_a, mine_b, came_b, latent_in, *refs):
    state, (latent_out, gathered, *new_state, staged, sent) = refs[:3], refs[3:]
    quad, core = bits_of()
    half = mine_a.shape[0]
    rows = 2 * half
    near, far = (quad ^ (1 + core)) * rows, (quad ^ (2 - core)) * rows
    this, that = core * half, (1 - core) * half
    pieces = [mine_a, came_a, mine_b, came_b]
    moves = place_rows(
        pieces, [near + this, far + that, far + this, near + that], latent_out, staged, sent
    )
    for index, piece in enumerate(pieces):
        gathered[index * half:(index + 1) * half, :] = piece[...]
    both = nn(gathered[...], weights[...]).astype(BF16)
    decode_tokens(groups_of(queries.shape[0])[0], queries, both, state, new_state)
    wait_all(moves)


def decode_rest_kernel(queries, weights, gathered, *refs):
    both = nn(gathered[...], weights[...]).astype(BF16)
    decode_tokens(groups_of(queries.shape[0])[1], queries, both, refs[:3], refs[3:])


def decode_send_kernel(queries, weights, more_weights, mine, came, latent_in, *refs):
    states, (latent_out, send, *boths, gathered, staged, sent) = refs[:6], refs[6:]
    quad, core = bits_of()
    rows, half = latent_out.shape[0] // 4, mine.shape[0]
    diagonal = (quad ^ 3) * rows
    spots = [diagonal + core * half, diagonal + (1 - core) * half]
    moves = place_rows([mine, came], spots, latent_out, staged, sent)
    gathered[:half, :] = mine[...]
    gathered[half:, :] = came[...]
    for both, weight in zip(boths, [weights, more_weights]):
        both[...] = nn(gathered[...], weight[...]).astype(BF16)
    decode_last(1 - core, queries, boths, states, send)
    wait_all(moves)


def decode_last(which, queries, boths, states, out):
    block = out.shape[0]
    at = pl.ds(pl.multiple_of(which * block, block), block)

    def put(lanes, pair, new):
        out[:, pair * PAIR:(pair + 1) * PAIR] = (new[0] / new[1]).astype(BF16)

    for group, both, state in zip(
        groups_of(queries.shape[0]), boths, [states[:3], states[3:]]
    ):
        decode_group(group, queries, both, at, state, put)


def decode_keep_kernel(queries, both, more_both, tokens, weight, *refs):
    *states, base, attended = refs
    core = lax.axis_index("qgrp")
    decode_last(core, queries, [both, more_both], states, attended)
    rows = base.shape[0]
    own = tokens[pl.ds(pl.multiple_of(core * rows, rows), rows), :].astype(F32)
    base[...] = own + nn(attended[...], weight[...])


def tokens_kernel(count, base, other, weight, out, staged, sent):
    start = lax.axis_index("qgrp") * base.shape[0]
    rows = base.shape[0] // 2
    moves = []
    for index in range(2):
        at = pl.ds(index * rows, rows)
        value = base[at, :] + nn(other[at, :], weight[...])
        slot = start + index * rows + lax.broadcasted_iota(jnp.int32, value.shape, 0)
        staged[at, :] = jnp.where(slot < count[0:1, 0:1], value, 0.0)
        moves.append(pltpu.make_async_copy(staged.at[at, :], out.at[at, :], sent.at[index]))
        moves[-1].start()
    wait_all(moves)


SPACES = {
    "v": pl.BlockSpec(memory_space=pltpu.VMEM),
    "h": pl.BlockSpec(memory_space=pltpu.HBM),
    "a": pl.BlockSpec(memory_space=pl.ANY),
}


def call(kernel, ins, outs, *args, far=(), alias=None, scratch=(), vmem=24, flops=0, moved=0, after=(),
         name=None):
    given, more = len(args), len(after)
    args = [
        pltpu.with_memory_space_constraint(arg, pltpu.HBM) if kind == "h" else arg
        for kind, arg in zip(ins, args)
    ]
    if more:
        alone = kernel

        def kernel(*refs):
            alone(*refs[:given], *refs[given + more:])

    shapes = [jax.ShapeDtypeStruct(*out) for out in outs]
    moved = moved or sum(a.size * a.dtype.itemsize for a in [*args, *shapes])
    return pl.pallas_call(
        kernel,
        out_shape=shapes,
        in_specs=[SPACES[kind] for kind in ins + "h" * more],
        out_specs=[SPACES["h" if index in far else "v"] for index in range(len(outs))],
        input_output_aliases=alias or {},
        scratch_shapes=list(scratch),
        compiler_params=pltpu.CompilerParams(vmem_limit_bytes=vmem * MIB),
        cost_estimate=pl.CostEstimate(flops=flops, bytes_accessed=moved, transcendentals=0),
        name=name,
    )(*args, *after)


def body(tokens, tally, latents, softness, wq, wk, wv, wo, dq, dk, dv, do, gain):
    cells = lax.axis_size("cell")
    total_rows, model = latents.shape
    rows, width = total_rows // 4, wq.shape[1]
    slots = tokens.shape[0]
    half_slots = slots // 2
    deep = rows + log_rows(width)

    def swap(array):
        return lax.ppermute(array, "qgrp", [(0, 1), (1, 0)])

    def trade(array, bit_0, bit_1):
        pairs = []
        for cell in range(cells):
            pairs.append((2 * cell, 2 * (cell ^ bit_0)))
            pairs.append((2 * cell + 1, 2 * (cell ^ bit_1) + 1))
        return lax.ppermute(array, ("cell", "qgrp"), pairs)

    attention = 4 * 256 * slots * width * 4
    sent = ((deep, width), BF16)
    message, keys, values, scales, count = call(
        encode_first_kernel, "ahhhhhh",
        [
            sent, *[((slots, width), BF16)] * 2,
            ((2, 8, width), F32), ((8, PAIR), jnp.int32),
        ],
        tally, softness, latents, tokens, wq, wk, wv,
        scratch=[
            pltpu.SMEM(tally.shape, tally.dtype), pltpu.SMEM(softness.shape, F32),
            pltpu.VMEM((rows, model), BF16), pltpu.VMEM(tokens.shape, BF16),
            *[pltpu.VMEM((model, width), BF16)] * 3, pltpu.VMEM((rows, width), F32),
            pltpu.SemaphoreType.DMA((7,)),
        ],
        flops=attention, name="encode_corner",
    )
    came = trade(message, 1, 2)
    state = [((rows, width), F32)] * 2
    passed = call(
        functools.partial(encode_keep_kernel, False), "vvvvvv", state,
        count, scales, latents, wq, keys, values, flops=attention, name="encode_pass",
    )
    (message,) = call(
        encode_side_kernel, "vvvvvv", [sent], count, scales, latents, wq, keys, values,
        scratch=[pltpu.VMEM((rows, width), F32)], flops=attention, after=passed[1:],
        name="encode_side",
    )
    first = trade(message, 1, 2)
    (message,) = call(
        merge_one_kernel, "vvv", [sent], *passed, came, after=[message], name="merge_pass"
    )
    second = trade(message, 2, 1)
    kept, kept_logs = call(
        functools.partial(encode_keep_kernel, True), "vvvvvv", state,
        count, scales, latents, wq, keys, values,
        flops=attention, after=[message], name="encode_own",
    )
    other_wo, other_do = swap(wo), swap(do)
    half = rows // 2
    parts = []
    for which in range(2):
        parts += call(
            functools.partial(merge_sides_kernel, which), "vvvv",
            [((half + log_rows(width), width), BF16)], kept, kept_logs, first, second,
            after=parts, name="merge_sides",
        )
    sizes = [len(group) * PAIR for group in groups_of(width // PAIR)]
    queries, *weights = call(
        decode_prepare_kernel, "vvvvv",
        [
            ((width // PAIR, slots, 2 * PAIR), BF16),
            *[((model, 2 * size), BF16) for size in sizes],
        ],
        scales, tokens, dq, dk, dv, after=parts, name="decode_prepare",
    )
    bits = [4 << i for i in range(max(cells.bit_length() - 3, 0))]
    for index, (bit_0, bit_1) in enumerate(zip(bits, bits[::-1])):
        last = index == len(bits) - 1
        merged = []
        for part, came in [(part, trade(part, bit_0, bit_1)) for part in parts]:
            merged += call(
                functools.partial(merge_even_kernel, bit_0, bit_1, last, half), "vv",
                [((half, width), BF16) if last else (part.shape, BF16)], part, came,
                after=[*merged, queries] if last else merged, name="merge_even",
            )
        parts = merged
    parts = [part[:half] for part in parts]
    (own_low,) = call(
        functools.partial(latent_kernel, 0), "vvvvvv", [((half, model), BF16)],
        parts[0], swap(parts[0]), wo, other_wo, latents, gain.reshape(1, model),
        after=parts[1:], name="latent_low",
    )
    own, own_half = call(
        functools.partial(latent_kernel, 1), "vvvvvvv",
        [((rows, model), BF16), ((half, model), BF16)],
        parts[1], swap(parts[1]), wo, other_wo, latents, gain.reshape(1, model), own_low,
        name="latent",
    )
    first = trade(own_half, 1, 2)
    second = trade(own_half, 2, 1)
    whole = ((total_rows, model), F32)
    states_out = [((slots, size), F32) for size in sizes for _ in range(3)]

    def scratch(count, pieces):
        return [pltpu.VMEM((count, model), F32), pltpu.SemaphoreType.DMA((pieces,))]

    latent_out, *states = call(
        decode_own_kernel, "vvvv", [whole, *states_out], queries, *weights, own,
        far=(0,), scratch=scratch(rows, 1), flops=attention, name="decode_own",
    )
    first, states[0] = lax.optimization_barrier((first, states[0]))
    third = trade(first, 2, 1)
    latent_out, gathered, *side = call(
        decode_sides_kernel, "vvvvvvhvvv", [whole, ((2 * rows, model), BF16), *states_out[:3]],
        queries, weights[0], first, swap(first), second, swap(second), latent_out, *states[:3],
        far=(0,), alias={6: 0}, scratch=scratch(2 * rows, 4), vmem=28, flops=attention,
        name="decode_sides",
    )
    third, side[0] = lax.optimization_barrier((third, side[0]))
    came = swap(third)
    rest = call(
        decode_rest_kernel, "vvvvvv", states_out[3:], queries, weights[1], gathered, *states[3:],
        flops=attention, after=side[1:2], name="decode_rest",
    )
    states = [*side, *rest]
    latent_out, send, *boths = call(
        decode_send_kernel, "vvvvvhvvvvvv",
        [
            whole, ((half_slots, width), BF16),
            *[((rows, 2 * size), BF16) for size in sizes],
        ],
        queries, *weights, third, came, latent_out, *states, far=(0,), alias={5: 0},
        scratch=[pltpu.VMEM((rows, model), BF16), *scratch(rows, 2)],
        flops=attention // 2, name="decode_send",
    )
    (base,) = call(
        decode_keep_kernel, "vvvvvvvvvvv", [((half_slots, model), F32)],
        queries, *boths, tokens, do, *states, scratch=[pltpu.VMEM((half_slots, width), BF16)],
        flops=attention // 2, name="decode_keep",
    )
    (tokens_out,) = call(
        tokens_kernel, "vvvv", [((half_slots, model), F32)], count, base, swap(send), other_do,
        far=(0,), scratch=scratch(half_slots, 2), name="tokens",
    )
    return latent_out, tokens_out


def solution(mesh):
    placed = (
        P("cell", None), P("cell"), P(), P(),
        P(None, "qgrp"), P(None, "qgrp"), P(None, "qgrp"), P("qgrp", None),
        P(None, "qgrp"), P(None, "qgrp"), P(None, "qgrp"), P("qgrp", None), P(),
    )
    return jax.shard_map(
        body, mesh=mesh, in_specs=placed, out_specs=(P(), P(("cell", "qgrp"), None)),
        check_vma=False,
    )
```

```python
import functools
import math

import jax
import jax.numpy as jnp
from jax import lax
from jax.experimental import pallas as pl
from jax.experimental.pallas import tpu as pltpu
from jax.sharding import PartitionSpec as P

HEAD_DIM = 64
PAIR = 2 * HEAD_DIM
NORM_EPSILON = 1e-06
LOG2E = math.log2(math.e)
F32 = jnp.float32
BF16 = jnp.bfloat16
MIB = 1 << 20


def nn(a, b):
    return lax.dot_general(a, b, (((1,), (0,)), ((), ())), preferred_element_type=F32)


def nt(a, b):
    return lax.dot_general(a, b, (((1,), (1,)), ((), ())), preferred_element_type=F32)


def tn(a, b):
    return lax.dot_general(a, b, (((0,), (0,)), ((), ())), preferred_element_type=F32)


def log_rows(width):
    return 16


def head_of(row):
    return 2 * jnp.bitwise_and(row, 3) + jnp.bitwise_and(lax.shift_right_logical(row, 2), 1)


def compact_logs(totals, tops):
    lane = lax.broadcasted_iota(jnp.int32, tops[0].shape, 1)

    def chosen(parts):
        out = parts[-1]
        for pair in range(len(parts) - 1):
            out = jnp.where(jnp.bitwise_and(lane, 3) == pair, parts[pair], out)
        return out

    turned = (chosen(tops) + jnp.log2(chosen(totals))).T
    row = lax.broadcasted_iota(jnp.int32, (8, turned.shape[1]), 0)
    return jnp.where(row < 4, turned[:8], turned[HEAD_DIM:HEAD_DIM + 8])


def pack_logs(logs, width):
    rows = logs.shape[1]
    high = logs.astype(BF16).astype(F32)
    middle = (logs - high).astype(BF16).astype(F32)
    low = (logs - high - middle).astype(BF16).astype(F32)
    if 3 * rows <= width:
        terms = jnp.concatenate([high, middle, low], axis=1)
        return jnp.concatenate([terms, jnp.zeros_like(terms)], axis=0).astype(BF16)
    half = rows // 2
    below = jnp.concatenate([high, middle], axis=0)
    beside = jnp.concatenate([low[:, :half], low[:, half:]], axis=0)
    return jnp.concatenate([below, beside], axis=1).astype(BF16)


def unpack_logs(packed, rows):
    packed = packed.astype(F32)
    if 3 * rows <= packed.shape[1]:
        return packed[:8, :rows] + packed[:8, rows:2 * rows] + packed[:8, 2 * rows:3 * rows]
    low = jnp.concatenate([packed[:8, rows:], packed[8:, rows:]], axis=1)
    return packed[:8, :rows] + packed[8:, :rows] + low


def merge(values_a, logs_a, values_b, logs_b):
    width = values_a.shape[1]
    top = jnp.maximum(logs_a, logs_b)
    part_a, part_b = jnp.exp2(logs_a - top), jnp.exp2(logs_b - top)
    whole = part_a + part_b
    share = part_a / whole
    high = share.astype(BF16).astype(F32)
    terms = jnp.concatenate([high, share - high], axis=0).astype(BF16)
    row = lax.broadcasted_iota(jnp.int32, (16, width), 0)
    lane = lax.broadcasted_iota(jnp.int32, (16, width), 1)
    inside = jnp.bitwise_and(row, 3) < width // PAIR
    spread = inside & (lax.shift_right_logical(lane, 6) == head_of(row))
    share = tn(terms, jnp.where(spread, 1.0, 0.0).astype(BF16))
    return share * values_a + (1.0 - share) * values_b, top + jnp.log2(whole)


def scale_row(softness_ref, which, heads):
    first = lax.axis_index("qgrp") * heads
    lane_head = lax.shift_right_logical(
        lax.broadcasted_iota(jnp.int32, (1, heads * HEAD_DIM), 1), 6
    )
    row = jnp.zeros((1, heads * HEAD_DIM), F32)
    for head in range(heads):
        row = jnp.where(lane_head == head, softness_ref[which, first + head], row)
    return row * (HEAD_DIM**-0.5 * LOG2E)


def split_scaled(queries, row):
    scaled = queries.astype(BF16).astype(F32) * row
    high = scaled.astype(BF16)
    return high, (scaled - high.astype(F32)).astype(BF16)


def pair_keys(keys):
    lane = lax.broadcasted_iota(jnp.int32, keys.shape, 1)
    zero = jnp.zeros_like(keys)
    first, second = jnp.where(lane < HEAD_DIM, keys, zero), jnp.where(lane < HEAD_DIM, zero, keys)
    return jnp.concatenate(
        [jnp.concatenate([first, first], axis=1), jnp.concatenate([second, second], axis=1)], axis=0
    )


def pair_values(values, counted):
    lane = lax.broadcasted_iota(jnp.int32, values.shape, 1)
    zero = jnp.zeros_like(values)
    low = lane < HEAD_DIM
    top = jnp.concatenate([jnp.where(low, values, zero), jnp.where(low, counted, zero)], axis=1)
    end = jnp.concatenate([jnp.where(low, zero, values), jnp.where(low, zero, counted)], axis=1)
    return jnp.concatenate([top, end], axis=0)


def attend_pair(high, low, keys, values):
    count = keys.shape[0] // 2
    scores = nt(jnp.concatenate([high, low], axis=1), keys)
    top_a = jnp.max(scores[:, :count], axis=1, keepdims=True)
    top_b = jnp.max(scores[:, count:], axis=1, keepdims=True)
    weights = jnp.concatenate(
        [
            jnp.exp2(scores[:, :count] - top_a).astype(BF16),
            jnp.exp2(scores[:, count:] - top_b).astype(BF16),
        ],
        axis=1,
    )
    sums = nn(weights, values)
    lane = lax.broadcasted_iota(jnp.int32, (high.shape[0], PAIR), 1)
    top = jnp.where(lane < HEAD_DIM, top_a, top_b)
    return sums[:, :PAIR], sums[:, PAIR:], top


def encode_rows(part, query_weight, keys, values, count, scale, put):
    width = query_weight.shape[1]
    slots = keys.shape[0]
    slot = lax.broadcasted_iota(jnp.int32, (slots, PAIR), 0)
    counted = jnp.where(slot < count, 1.0, 0.0).astype(BF16)
    high, low = split_scaled(nn(part, query_weight[...]), scale)
    totals, tops = [], []
    for pair in range(width // PAIR):
        lanes = slice(pair * PAIR, (pair + 1) * PAIR)
        key_block = pair_keys(keys[:, lanes])
        value_block = pair_values(values[:, lanes], counted)
        sums, total, top = attend_pair(high[:, lanes], low[:, lanes], key_block, value_block)
        put(lanes, sums / total)
        totals.append(total)
        tops.append(top)
    return compact_logs(totals, tops)


def bits_of():
    cell, core = lax.axis_index("cell"), lax.axis_index("qgrp")
    quad = jnp.bitwise_and(cell, 3)
    return quad, core


def start_all(pairs, arrived):
    moves = [
        pltpu.make_async_copy(source, goal, arrived.at[index])
        for index, (source, goal) in enumerate(pairs)
    ]
    for move in moves:
        move.start()
    return moves


def wait_all(moves):
    for move in moves:
        move.wait()


def quarter(latents, quad, rows):
    return latents.at[pl.ds(pl.multiple_of(quad * rows, rows), rows), :]


def encode_first_kernel(
    tally, softness_far, latents_far, tokens_far, wq_far, wk_far, wv_far,
    message, keys, values, scales, count_out,
    count, softness, latents, tokens, wq, wk, wv, arrived,
):
    quad, core = bits_of()
    rows = latents.shape[0]
    moves = start_all(
        [
            (tally, count), (tokens_far, tokens), (wk_far, wk), (wv_far, wv), (wq_far, wq),
            (softness_far, softness), (quarter(latents_far, quad ^ 3, rows), latents),
        ],
        arrived,
    )
    wait_all(moves[:3])
    is_valid = lax.broadcasted_iota(jnp.int32, keys.shape, 0) < count[0]
    made = nn(tokens[...], wk[...])
    keys[...] = jnp.where(is_valid, made, made[0:1, :]).astype(BF16)
    wait_all(moves[3:])
    values[...] = jnp.where(is_valid, nn(tokens[...], wv[...]), 0.0).astype(BF16)
    count_out[...] = jnp.full(count_out.shape, count[0], jnp.int32)
    for which in range(2):
        row = scale_row(softness, which, wq.shape[1] // HEAD_DIM)
        scales[which] = jnp.broadcast_to(row, scales.shape[1:])
    encode_into(message, latents[...], wq, keys, values, count_out, scales)


def encode_into(message, part, wq, keys, values, count, scales):
    rows = part.shape[0]

    def put(lanes, sums):
        message[:rows, lanes] = sums.astype(BF16)

    logs = encode_rows(part, wq, keys, values, count[0:1, :], scales[0, 0:1, :], put)
    message[rows:, :] = pack_logs(logs, message.shape[1])


def encode_side_kernel(count, scales, latents, wq, keys, values, message):
    quad, core = bits_of()
    rows = latents.shape[0] // 4
    side = quad ^ jnp.where(core == 0, 1, 2)
    part = quarter(latents, side, rows)[...]
    encode_into(message, part, wq, keys, values, count, scales)


def encode_keep_kernel(is_own, count, scales, latents, wq, keys, values, kept, logs):
    quad, core = bits_of()
    rows = kept.shape[0]

    def put(lanes, part):
        kept[:, lanes] = part

    at = quad if is_own else quad ^ jnp.where(core == 0, 2, 1)
    part = quarter(latents, at, rows)[...]
    logs[...] = encode_rows(part, wq, keys, values, count[0:1, :], scales[0, 0:1, :], put)

def write_message(message, values, logs):
    rows = values.shape[0]
    message[:rows, :] = values.astype(BF16)
    message[rows:, :] = pack_logs(logs, message.shape[1])


def read_message(message, rows):
    return message[:rows, :].astype(F32), unpack_logs(message[rows:, :], rows)


def merge_pass_kernel(values, logs, came, *messages):
    rows = values.shape[0]
    half = rows // 2
    part, log = merge(values[...], logs[...], *read_message(came, rows))
    for which, message in enumerate(messages):
        at = slice(which * half, (which + 1) * half)
        write_message(message, part[at], log[:, at])


def merge_sides_kernel(which, values, logs, first, second, message):
    rows = values.shape[0]
    half = rows // 2
    at = slice(which * half, (which + 1) * half)
    part, log = values[at, :], logs[:, at]
    came_part, came_log = read_message(first, rows)
    part, log = merge(part, log, came_part[at], came_log[:, at])
    part, log = merge(part, log, *read_message(second, half))
    write_message(message, part, log)


def merge_even_kernel(own_bit, other_bit, last, rows, mine, came, out):
    core = lax.axis_index("qgrp")
    bit = jnp.where(core == 0, own_bit, other_bit)
    is_low = jnp.bitwise_and(lax.axis_index("cell"), bit) == 0

    def both(first, second):
        part, log = merge(*read_message(first, rows), *read_message(second, rows))
        if last:
            out[...] = part.astype(BF16)
        else:
            write_message(out, part, log)

    @pl.when(is_low)
    def _():
        both(mine, came)

    @pl.when(jnp.logical_not(is_low))
    def _():
        both(came, mine)


def latent_kernel(which, attended, other, weight, other_weight, latents, gain, *refs):
    quad, core = bits_of()
    half = attended.shape[0]
    start = pl.ds(pl.multiple_of((2 * quad + which) * half, half), half)

    def finish(first, second, first_weight, second_weight):
        update = nn(first[...], first_weight[...]) + nn(second[...], second_weight[...])
        pre = latents[start, :].astype(F32) + update
        mean_square = jnp.mean(pre * pre, axis=-1, keepdims=True)
        done = (pre * lax.rsqrt(mean_square + NORM_EPSILON) * gain[...]).astype(BF16)
        if which == 0:
            refs[0][...] = done
        else:
            low, out, own_half = refs
            out[:half, :] = low[...]
            out[half:, :] = done
            own_half[...] = jnp.where(core == 0, low[...], done)

    @pl.when(core == 0)
    def _():
        finish(attended, other, weight, other_weight)

    @pl.when(core != 0)
    def _():
        finish(other, attended, other_weight, weight)


def groups_of(pairs):
    first = -(-2 * pairs // 3)
    return [range(first), range(first, pairs)]


def decode_prepare_kernel(scales, tokens, wq, wk, wv, out, *weights):
    width = wq.shape[1]
    high, low = split_scaled(nn(tokens[...], wq[...]), scales[1, 0:1, :])
    for pair in range(width // PAIR):
        lanes = slice(pair * PAIR, (pair + 1) * PAIR)
        out[pair, :, :PAIR] = high[:, lanes]
        out[pair, :, PAIR:] = low[:, lanes]
    for group, both in zip(groups_of(width // PAIR), weights):
        lanes = slice(group[0] * PAIR, (group[-1] + 1) * PAIR)
        size = len(group) * PAIR
        both[:, :size] = wk[:, lanes]
        both[:, size:] = wv[:, lanes]


def apart(work):
    pl.when(lax.axis_index("qgrp") >= 0)(work)


def place_rows(pieces, spots, latent_out, staged, sent):
    moves, start = [], 0
    for index, (piece, spot) in enumerate(zip(pieces, spots)):
        count = piece.shape[0]
        staged[start:start + count, :] = piece[...].astype(F32)
        moves.append(
            pltpu.make_async_copy(
                staged.at[pl.ds(start, count), :],
                latent_out.at[pl.ds(pl.multiple_of(spot, count), count), :],
                sent.at[index],
            )
        )
        moves[-1].start()
        start += count
    return moves


def decode_part(queries, keys, values, state):
    high, low = queries[:, :PAIR], queries[:, PAIR:]
    one = jnp.ones((keys.shape[0], PAIR), BF16)
    sums, total, top = attend_pair(high, low, pair_keys(keys), pair_values(values, one))
    if state is None:
        return sums, total, top
    old_sums, old_total, old_top = state
    new_top = jnp.maximum(top, old_top)
    old, new = jnp.exp2(old_top - new_top), jnp.exp2(top - new_top)
    return old * old_sums + new * sums, old * old_total + new * total, new_top


def decode_group(group, queries, both, at, state, put):
    size = len(group) * PAIR
    for place, pair in enumerate(group):
        lanes = slice(place * PAIR, (place + 1) * PAIR)
        value_lanes = slice(size + place * PAIR, size + (place + 1) * PAIR)
        old = None if state is None else [part[at, lanes] for part in state]
        put(lanes, pair, decode_part(queries[pair, at, :], both[:, lanes], both[:, value_lanes], old))


def decode_tokens(group, queries, both, state, new_state):
    block = queries.shape[1] // 2
    for index in range(2):
        at = slice(index * block, (index + 1) * block)

        def put(lanes, pair, new):
            for out, part in zip(new_state, new):
                out[at, lanes] = part

        decode_group(group, queries, both, at, state, put)


def decode_own_kernel(queries, weights, more_weights, own, latent_out, *refs):
    *states, staged, sent = refs
    quad, core = bits_of()
    rows = own.shape[0]
    moves = place_rows([own], [quad * rows], latent_out, staged, sent)

    @apart
    def _():
        for group, weight, state in zip(
            groups_of(queries.shape[0]), [weights, more_weights], [states[:3], states[3:]]
        ):
            both = nn(own[...], weight[...]).astype(BF16)
            decode_tokens(group, queries, both, None, state)

    wait_all(moves)


def decode_sides_kernel(came, queries, weights, more_weights, near, far, latent_in, *refs):
    states, (latent_out, *refs) = refs[:6], refs[6:]
    new_states, (gathered, staged, sent) = refs[:6], refs[6:]
    quad, core = bits_of()
    half = near.shape[0]
    across = [quad ^ (1 + core), quad ^ (2 - core)]
    which = 1 - core if came else core
    pieces = [near, far]
    spots = [(at * 2 + which) * half for at in (across[::-1] if came else across)]
    moves = place_rows(pieces, spots, latent_out, staged, sent)

    @apart
    def _():
        for index, piece in enumerate(pieces):
            gathered[index * half:(index + 1) * half, :] = piece[...]
        for group, weight, state, new_state in zip(
            groups_of(queries.shape[0]), [weights, more_weights],
            [states[:3], states[3:]], [new_states[:3], new_states[3:]],
        ):
            both = nn(gathered[...], weight[...]).astype(BF16)
            decode_tokens(group, queries, both, state, new_state)

    wait_all(moves)


def decode_send_kernel(queries, weights, more_weights, mine, came, *refs):
    states, (send, *boths, gathered) = refs[:6], refs[6:]
    core = lax.axis_index("qgrp")
    half = mine.shape[0]
    gathered[:half, :] = mine[...]
    gathered[half:, :] = came[...]
    for both, weight in zip(boths, [weights, more_weights]):
        both[...] = nn(gathered[...], weight[...]).astype(BF16)
    decode_last(1 - core, queries, boths, states, send)


def decode_last(which, queries, boths, states, out):
    block = out.shape[0]
    at = pl.ds(pl.multiple_of(which * block, block), block)

    def put(lanes, pair, new):
        out[:, pair * PAIR:(pair + 1) * PAIR] = (new[0] / new[1]).astype(BF16)

    for group, both, state in zip(
        groups_of(queries.shape[0]), boths, [states[:3], states[3:]]
    ):
        decode_group(group, queries, both, at, state, put)


def decode_keep_kernel(queries, both, more_both, tokens, weight, mine, came, latent_in, *refs):
    *states, latent_out, base, attended, staged, sent = refs
    quad, core = bits_of()
    half = mine.shape[0]
    corner = (quad ^ 3) * 2 * half
    spots = [corner + core * half, corner + (1 - core) * half]
    moves = place_rows([mine, came], spots, latent_out, staged, sent)

    @apart
    def _():
        decode_last(core, queries, [both, more_both], states, attended)
        rows = base.shape[0]
        own = tokens[pl.ds(pl.multiple_of(core * rows, rows), rows), :].astype(F32)
        base[...] = own + nn(attended[...], weight[...])

    wait_all(moves)


def tokens_kernel(count, base, other, weight, out, staged, sent):
    start = lax.axis_index("qgrp") * base.shape[0]
    pieces = sent.shape[0]
    columns = base.shape[1] // pieces
    moves = []
    for index in range(pieces):
        at = pl.ds(index * columns, columns)
        value = base[:, at] + nn(other[...], weight[:, at])
        slot = start + lax.broadcasted_iota(jnp.int32, value.shape, 0)
        staged[:, at] = jnp.where(slot < count[0:1, 0:1], value, 0.0)
        moves.append(pltpu.make_async_copy(staged.at[:, at], out.at[:, at], sent.at[index]))
        moves[-1].start()
    wait_all(moves)


SPACES = {
    "v": pl.BlockSpec(memory_space=pltpu.VMEM),
    "h": pl.BlockSpec(memory_space=pltpu.HBM),
    "a": pl.BlockSpec(memory_space=pl.ANY),
}


def call(kernel, ins, outs, *args, far=(), alias=None, scratch=(), vmem=24, flops=0, moved=0, after=(),
         name=None):
    given, more = len(args), len(after)
    args = [
        pltpu.with_memory_space_constraint(arg, pltpu.HBM) if kind == "h" else arg
        for kind, arg in zip(ins, args)
    ]
    if more:
        alone = kernel

        def kernel(*refs):
            alone(*refs[:given], *refs[given + more:])

    shapes = [jax.ShapeDtypeStruct(*out) for out in outs]
    moved = moved or sum(a.size * a.dtype.itemsize for a in [*args, *shapes])
    return pl.pallas_call(
        kernel,
        out_shape=shapes,
        in_specs=[SPACES[kind] for kind in ins + "h" * more],
        out_specs=[SPACES["h" if index in far else "v"] for index in range(len(outs))],
        input_output_aliases=alias or {},
        scratch_shapes=list(scratch),
        compiler_params=pltpu.CompilerParams(vmem_limit_bytes=vmem * MIB),
        cost_estimate=pl.CostEstimate(flops=flops, bytes_accessed=moved, transcendentals=0),
        name=name,
    )(*args, *after)


def body(tokens, tally, latents, softness, wq, wk, wv, wo, dq, dk, dv, do, gain):
    cells = lax.axis_size("cell")
    total_rows, model = latents.shape
    rows, width = total_rows // 4, wq.shape[1]
    slots = tokens.shape[0]
    half_slots = slots // 2
    deep = rows + log_rows(width)

    def swap(array):
        return lax.ppermute(array, "qgrp", [(0, 1), (1, 0)])

    def trade(array, bit_0, bit_1):
        pairs = []
        for cell in range(cells):
            pairs.append((2 * cell, 2 * (cell ^ bit_0)))
            pairs.append((2 * cell + 1, 2 * (cell ^ bit_1) + 1))
        return lax.ppermute(array, ("cell", "qgrp"), pairs)

    attention = 4 * 256 * slots * width * 4
    sent = ((deep, width), BF16)
    message, keys, values, scales, count = call(
        encode_first_kernel, "ahhhhhh",
        [
            sent, *[((slots, width), BF16)] * 2,
            ((2, 8, width), F32), ((8, PAIR), jnp.int32),
        ],
        tally, softness, latents, tokens, wq, wk, wv,
        scratch=[
            pltpu.SMEM(tally.shape, tally.dtype), pltpu.SMEM(softness.shape, F32),
            pltpu.VMEM((rows, model), BF16), pltpu.VMEM(tokens.shape, BF16),
            *[pltpu.VMEM((model, width), BF16)] * 3, pltpu.SemaphoreType.DMA((7,)),
        ],
        flops=attention, name="encode_corner",
    )
    came = trade(message, 1, 2)
    state = [((rows, width), F32), ((8, rows), F32)]
    (message,) = call(
        encode_side_kernel, "vvvvvv", [sent], count, scales, latents, wq, keys, values,
        flops=attention, name="encode_side",
    )
    first = trade(message, 1, 2)
    passed = call(
        functools.partial(encode_keep_kernel, False), "vvvvvv", state,
        count, scales, latents, wq, keys, values, flops=attention, after=[message],
        name="encode_pass",
    )
    half = rows // 2
    half_sent = ((half + log_rows(width), width), BF16)
    messages = call(
        merge_pass_kernel, "vvv", [half_sent] * 2, *passed, came, name="merge_pass"
    )
    seconds = [trade(message, 2, 1) for message in messages]
    kept, kept_logs = call(
        functools.partial(encode_keep_kernel, True), "vvvvvv", state,
        count, scales, latents, wq, keys, values,
        flops=attention, after=messages, name="encode_own",
    )
    other_wo, other_do = swap(wo), swap(do)
    parts = []
    for which in range(2):
        parts += call(
            functools.partial(merge_sides_kernel, which), "vvvv",
            [half_sent], kept, kept_logs, first, seconds[which],
            after=parts, name="merge_sides",
        )
    sizes = [len(group) * PAIR for group in groups_of(width // PAIR)]
    queries, *weights = call(
        decode_prepare_kernel, "vvvvv",
        [
            ((width // PAIR, slots, 2 * PAIR), BF16),
            *[((model, 2 * size), BF16) for size in sizes],
        ],
        scales, tokens, dq, dk, dv, after=parts, name="decode_prepare",
    )
    bits = [4 << i for i in range(max(cells.bit_length() - 3, 0))]
    for index, (bit_0, bit_1) in enumerate(zip(bits, bits[::-1])):
        last = index == len(bits) - 1
        merged = []
        for part, came in [(part, trade(part, bit_0, bit_1)) for part in parts]:
            merged += call(
                functools.partial(merge_even_kernel, bit_0, bit_1, last, half), "vv",
                [((half, width), BF16) if last else (part.shape, BF16)], part, came,
                after=[*merged, queries] if last else merged, name="merge_even",
            )
        parts = merged
    parts = [part[:half] for part in parts]
    (own_low,) = call(
        functools.partial(latent_kernel, 0), "vvvvvv", [((half, model), BF16)],
        parts[0], swap(parts[0]), wo, other_wo, latents, gain.reshape(1, model),
        after=parts[1:], name="latent_low",
    )
    own, own_half = call(
        functools.partial(latent_kernel, 1), "vvvvvvv",
        [((rows, model), BF16), ((half, model), BF16)],
        parts[1], swap(parts[1]), wo, other_wo, latents, gain.reshape(1, model), own_low,
        name="latent",
    )
    first = trade(own_half, 1, 2)
    second = trade(own_half, 2, 1)
    whole = ((total_rows, model), F32)
    states_out = [((slots, size), F32) for size in sizes for _ in range(3)]

    def scratch(count, pieces):
        return [pltpu.VMEM((count, model), F32), pltpu.SemaphoreType.DMA((pieces,))]

    latent_out, *states = call(
        decode_own_kernel, "vvvv", [whole, *states_out], queries, *weights, own,
        after=[other_do], far=(0,), scratch=scratch(rows, 1), flops=attention, name="decode_own",
    )
    first, states[0] = lax.optimization_barrier((first, states[0]))
    third = trade(first, 2, 1)

    def decode_sides(came, near, far, latent_out, states):
        latent_out, *states = call(
            functools.partial(decode_sides_kernel, came), "vvvvvhvvvvvv", [whole, *states_out],
            queries, *weights, near, far, latent_out, *states, far=(0,), alias={5: 0},
            scratch=[pltpu.VMEM((rows, model), BF16), *scratch(rows, 2)], flops=attention,
            name="decode_sides",
        )
        return latent_out, states

    came_first, came_second = swap(first), swap(second)
    latent_out, states = decode_sides(False, first, second, latent_out, states)
    third, states[0] = lax.optimization_barrier((third, states[0]))
    came = swap(third)
    latent_out, states = decode_sides(True, came_first, came_second, latent_out, states)
    send, *boths = call(
        decode_send_kernel, "vvvvvvvvvvv",
        [((half_slots, width), BF16), *[((rows, 2 * size), BF16) for size in sizes]],
        queries, *weights, third, came, *states, scratch=[pltpu.VMEM((rows, model), BF16)],
        flops=attention // 2, name="decode_send",
    )
    latent_out, base = call(
        decode_keep_kernel, "vvvvvvvhvvvvvv", [whole, ((half_slots, model), F32)],
        queries, *boths, tokens, do, third, came, latent_out, *states, far=(0,), alias={7: 0},
        scratch=[pltpu.VMEM((half_slots, width), BF16), *scratch(rows, 2)],
        flops=attention // 2, name="decode_keep",
    )
    (tokens_out,) = call(
        tokens_kernel, "vvvv", [((half_slots, model), F32)], count, base, swap(send), other_do,
        far=(0,), scratch=scratch(half_slots, 3 if model % 384 == 0 else 1), name="tokens",
    )
    return latent_out, tokens_out


def solution(mesh):
    placed = (
        P("cell", None), P("cell"), P(), P(),
        P(None, "qgrp"), P(None, "qgrp"), P(None, "qgrp"), P("qgrp", None),
        P(None, "qgrp"), P(None, "qgrp"), P(None, "qgrp"), P("qgrp", None), P(),
    )
    return jax.shard_map(
        body, mesh=mesh, in_specs=placed, out_specs=(P(), P(("cell", "qgrp"), None)),
        check_vma=False,
    )
```

```python
import functools
import math

import jax
import jax.numpy as jnp
from jax import lax
from jax.experimental import pallas as pl
from jax.experimental.pallas import tpu as pltpu
from jax.sharding import PartitionSpec as P

HEAD_DIM = 64
PAIR = 2 * HEAD_DIM
NORM_EPSILON = 1e-06
LOG2E = math.log2(math.e)
F32 = jnp.float32
BF16 = jnp.bfloat16
MIB = 1 << 20


def nn(a, b):
    return lax.dot_general(a, b, (((1,), (0,)), ((), ())), preferred_element_type=F32)


def nt(a, b):
    return lax.dot_general(a, b, (((1,), (1,)), ((), ())), preferred_element_type=F32)


def tn(a, b):
    return lax.dot_general(a, b, (((0,), (0,)), ((), ())), preferred_element_type=F32)


def log_rows(rows, width):
    return 8 if 3 * rows <= width else 16


def head_of(row):
    return 2 * jnp.bitwise_and(row, 3) + jnp.bitwise_and(lax.shift_right_logical(row, 2), 1)


def compact_logs(totals, tops):
    lane = lax.broadcasted_iota(jnp.int32, tops[0].shape, 1)

    def chosen(parts):
        out = parts[-1]
        for pair in range(len(parts) - 1):
            out = jnp.where(jnp.bitwise_and(lane, 3) == pair, parts[pair], out)
        return out

    turned = (chosen(tops) + jnp.log2(chosen(totals))).T
    row = lax.broadcasted_iota(jnp.int32, (8, turned.shape[1]), 0)
    return jnp.where(row < 4, turned[:8], turned[HEAD_DIM:HEAD_DIM + 8])


def pack_logs(logs, width):
    rows = logs.shape[1]
    high = logs.astype(BF16).astype(F32)
    middle = (logs - high).astype(BF16).astype(F32)
    low = (logs - high - middle).astype(BF16).astype(F32)
    if 3 * rows <= width:
        return jnp.concatenate([high, middle, low], axis=1).astype(BF16)
    half = rows // 2
    below = jnp.concatenate([high, middle], axis=0)
    beside = jnp.concatenate([low[:, :half], low[:, half:]], axis=0)
    return jnp.concatenate([below, beside], axis=1).astype(BF16)


def unpack_logs(packed, rows):
    packed = packed.astype(F32)
    if 3 * rows <= packed.shape[1]:
        return packed[:8, :rows] + packed[:8, rows:2 * rows] + packed[:8, 2 * rows:3 * rows]
    low = jnp.concatenate([packed[:8, rows:], packed[8:, rows:]], axis=1)
    return packed[:8, :rows] + packed[8:, :rows] + low


def merge(values_a, logs_a, values_b, logs_b):
    width = values_a.shape[1]
    top = jnp.maximum(logs_a, logs_b)
    part_a, part_b = jnp.exp2(logs_a - top), jnp.exp2(logs_b - top)
    whole = part_a + part_b
    share = part_a / whole
    high = share.astype(BF16).astype(F32)
    terms = jnp.concatenate([high, share - high], axis=0).astype(BF16)
    row = lax.broadcasted_iota(jnp.int32, (16, width), 0)
    lane = lax.broadcasted_iota(jnp.int32, (16, width), 1)
    inside = jnp.bitwise_and(row, 3) < width // PAIR
    spread = inside & (lax.shift_right_logical(lane, 6) == head_of(row))
    share = tn(terms, jnp.where(spread, 1.0, 0.0).astype(BF16))
    return share * values_a + (1.0 - share) * values_b, top + jnp.log2(whole)


def scale_row(softness_ref, which, heads):
    first = lax.axis_index("qgrp") * heads
    lane_head = lax.shift_right_logical(
        lax.broadcasted_iota(jnp.int32, (1, heads * HEAD_DIM), 1), 6
    )
    row = jnp.zeros((1, heads * HEAD_DIM), F32)
    for head in range(heads):
        row = jnp.where(lane_head == head, softness_ref[which, first + head], row)
    return row * (HEAD_DIM**-0.5 * LOG2E)


def split_scaled(queries, row):
    scaled = queries.astype(BF16).astype(F32) * row
    high = scaled.astype(BF16)
    return high, (scaled - high.astype(F32)).astype(BF16)


def pair_keys(keys):
    lane = lax.broadcasted_iota(jnp.int32, keys.shape, 1)
    zero = jnp.zeros_like(keys)
    first, second = jnp.where(lane < HEAD_DIM, keys, zero), jnp.where(lane < HEAD_DIM, zero, keys)
    return jnp.concatenate(
        [jnp.concatenate([first, first], axis=1), jnp.concatenate([second, second], axis=1)], axis=0
    )


def pair_values(values, counted):
    lane = lax.broadcasted_iota(jnp.int32, values.shape, 1)
    zero = jnp.zeros_like(values)
    low = lane < HEAD_DIM
    top = jnp.concatenate([jnp.where(low, values, zero), jnp.where(low, counted, zero)], axis=1)
    end = jnp.concatenate([jnp.where(low, zero, values), jnp.where(low, zero, counted)], axis=1)
    return jnp.concatenate([top, end], axis=0)


def attend_pair(high, low, keys, values):
    count = keys.shape[0] // 2
    scores = nt(jnp.concatenate([high, low], axis=1), keys)
    top_a = jnp.max(scores[:, :count], axis=1, keepdims=True)
    top_b = jnp.max(scores[:, count:], axis=1, keepdims=True)
    weights = jnp.concatenate(
        [
            jnp.exp2(scores[:, :count] - top_a).astype(BF16),
            jnp.exp2(scores[:, count:] - top_b).astype(BF16),
        ],
        axis=1,
    )
    sums = nn(weights, values)
    lane = lax.broadcasted_iota(jnp.int32, (high.shape[0], PAIR), 1)
    top = jnp.where(lane < HEAD_DIM, top_a, top_b)
    return sums[:, :PAIR], sums[:, PAIR:], top


def encode_rows(part, query_weight, keys, values, count, scale, put):
    width = query_weight.shape[1]
    slots = keys.shape[0]
    slot = lax.broadcasted_iota(jnp.int32, (slots, PAIR), 0)
    counted = jnp.where(slot < count, 1.0, 0.0).astype(BF16)
    high, low = split_scaled(nn(part, query_weight[...]), scale)
    totals, tops = [], []
    for pair in range(width // PAIR):
        lanes = slice(pair * PAIR, (pair + 1) * PAIR)
        key_block = pair_keys(keys[:, lanes])
        value_block = pair_values(values[:, lanes], counted)
        sums, total, top = attend_pair(high[:, lanes], low[:, lanes], key_block, value_block)
        put(lanes, sums / total)
        totals.append(total)
        tops.append(top)
    return compact_logs(totals, tops)


def bits_of():
    cell, core = lax.axis_index("cell"), lax.axis_index("qgrp")
    quad = jnp.bitwise_and(cell, 3)
    return quad, core


def start_all(pairs, arrived):
    moves = [
        pltpu.make_async_copy(source, goal, arrived.at[index])
        for index, (source, goal) in enumerate(pairs)
    ]
    for move in moves:
        move.start()
    return moves


def wait_all(moves):
    for move in moves:
        move.wait()


def quarter(latents, quad, rows):
    return latents.at[pl.ds(pl.multiple_of(quad * rows, rows), rows), :]


def encode_first_kernel(
    tally, softness_far, latents_far, tokens_far, wq_far, wk_far, wv_far, wo_far, do_far,
    message, keys, values, scales, count_out, wq, latents, outputs,
    count, softness, tokens, wk, wv, arrived,
):
    quad, core = bits_of()
    rows, model = latents.shape[0] // 4, wo_far.shape[1]
    moves = start_all(
        [
            (tally, count), (tokens_far, tokens), (wk_far, wk), (wv_far, wv), (wq_far, wq),
            (softness_far, softness),
            *[
                (quarter(latents_far, quad ^ other, rows), quarter(latents, quad ^ other, rows))
                for other in (3, 1, 2, 0)
            ],
            (wo_far, outputs.at[:, :model]), (do_far, outputs.at[:, model:]),
        ],
        arrived,
    )
    wait_all(moves[:3])
    is_valid = lax.broadcasted_iota(jnp.int32, keys.shape, 0) < count[0]
    made = nn(tokens[...], wk[...])
    keys[...] = jnp.where(is_valid, made, made[0:1, :]).astype(BF16)
    wait_all(moves[3:7])
    values[...] = jnp.where(is_valid, nn(tokens[...], wv[...]), 0.0).astype(BF16)
    count_out[...] = jnp.full(count_out.shape, count[0], jnp.int32)
    for which in range(2):
        row = scale_row(softness, which, wq.shape[1] // HEAD_DIM)
        scales[which] = jnp.broadcast_to(row, scales.shape[1:])
    part = quarter(latents, quad ^ 3, rows)[...]
    encode_into(message, part, wq, keys, values, count_out, scales)
    wait_all(moves[7:])


def encode_into(message, part, wq, keys, values, count, scales):
    rows = part.shape[0]

    def put(lanes, sums):
        message[:rows, lanes] = sums.astype(BF16)

    logs = encode_rows(part, wq, keys, values, count[0:1, :], scales[0, 0:1, :], put)
    message[rows:, :] = pack_logs(logs, message.shape[1])


def encode_side_kernel(count, scales, latents, wq, keys, values, message):
    quad, core = bits_of()
    rows = latents.shape[0] // 4
    side = quad ^ jnp.where(core == 0, 1, 2)
    part = quarter(latents, side, rows)[...]
    encode_into(message, part, wq, keys, values, count, scales)


def encode_keep_kernel(is_own, count, scales, latents, wq, keys, values, kept, logs):
    quad, core = bits_of()
    rows = kept.shape[0]

    def put(lanes, part):
        kept[:, lanes] = part

    at = quad if is_own else quad ^ jnp.where(core == 0, 2, 1)
    part = quarter(latents, at, rows)[...]
    logs[...] = encode_rows(part, wq, keys, values, count[0:1, :], scales[0, 0:1, :], put)

def write_message(message, values, logs):
    rows = values.shape[0]
    message[:rows, :] = values.astype(BF16)
    message[rows:, :] = pack_logs(logs, message.shape[1])


def read_message(message, rows):
    return message[:rows, :].astype(F32), unpack_logs(message[rows:, :], rows)


def merge_pass_kernel(values, logs, came, *messages):
    rows = values.shape[0]
    half = rows // 2
    part, log = merge(values[...], logs[...], *read_message(came, rows))
    for which, message in enumerate(messages):
        at = slice(which * half, (which + 1) * half)
        write_message(message, part[at], log[:, at])


def merge_sides_kernel(which, values, logs, first, second, message):
    rows = values.shape[0]
    half = rows // 2
    at = slice(which * half, (which + 1) * half)
    part, log = values[at, :], logs[:, at]
    came_part, came_log = read_message(first, rows)
    part, log = merge(part, log, came_part[at], came_log[:, at])
    part, log = merge(part, log, *read_message(second, half))
    write_message(message, part, log)


def merge_even_kernel(own_bit, other_bit, last, rows, mine, came, out):
    core = lax.axis_index("qgrp")
    bit = jnp.where(core == 0, own_bit, other_bit)
    is_low = jnp.bitwise_and(lax.axis_index("cell"), bit) == 0

    def both(first, second):
        part, log = merge(*read_message(first, rows), *read_message(second, rows))
        if last:
            out[...] = part.astype(BF16)
        else:
            write_message(out, part, log)

    @pl.when(is_low)
    def _():
        both(mine, came)

    @pl.when(jnp.logical_not(is_low))
    def _():
        both(came, mine)


def latent_kernel(which, attended, other, weight, other_weight, latents, gain, *refs):
    quad, core = bits_of()
    half, model = attended.shape[0], weight.shape[1]
    start = pl.ds(pl.multiple_of((2 * quad + which) * half, half), half)

    def finish(first, second, first_weight, second_weight):
        update = nn(first[...], first_weight) + nn(second[...], second_weight)
        pre = latents[start, :].astype(F32) + update
        mean_square = jnp.mean(pre * pre, axis=-1, keepdims=True)
        done = (pre * lax.rsqrt(mean_square + NORM_EPSILON) * gain[...]).astype(BF16)
        if which == 0:
            refs[0][...] = done
        else:
            low, out, own_half = refs
            out[:half, :] = low[...]
            out[half:, :] = done
            own_half[...] = jnp.where(core == 0, low[...], done)

    @pl.when(core == 0)
    def _():
        finish(attended, other, weight[...], other_weight[:, :model])

    @pl.when(core != 0)
    def _():
        finish(other, attended, other_weight[:, :model], weight[...])


def groups_of(pairs):
    first = -(-2 * pairs // 3)
    return [range(first), range(first, pairs)]


def decode_prepare_kernel(scales, tokens, wq, wk, wv, out, *weights):
    width = wq.shape[1]
    high, low = split_scaled(nn(tokens[...], wq[...]), scales[1, 0:1, :])
    for pair in range(width // PAIR):
        lanes = slice(pair * PAIR, (pair + 1) * PAIR)
        out[pair, :, :PAIR] = high[:, lanes]
        out[pair, :, PAIR:] = low[:, lanes]
    for group, both in zip(groups_of(width // PAIR), weights):
        lanes = slice(group[0] * PAIR, (group[-1] + 1) * PAIR)
        size = len(group) * PAIR
        both[:, :size] = wk[:, lanes]
        both[:, size:] = wv[:, lanes]


def apart(work):
    pl.when(lax.axis_index("qgrp") >= 0)(work)


def place_rows(pieces, spots, latent_out, staged, sent):
    moves, start = [], 0
    for index, (piece, spot) in enumerate(zip(pieces, spots)):
        count = piece.shape[0]
        staged[start:start + count, :] = piece[...].astype(F32)
        moves.append(
            pltpu.make_async_copy(
                staged.at[pl.ds(start, count), :],
                latent_out.at[pl.ds(pl.multiple_of(spot, count), count), :],
                sent.at[index],
            )
        )
        moves[-1].start()
        start += count
    return moves


def decode_part(queries, keys, values, state):
    high, low = queries[:, :PAIR], queries[:, PAIR:]
    one = jnp.ones((keys.shape[0], PAIR), BF16)
    sums, total, top = attend_pair(high, low, pair_keys(keys), pair_values(values, one))
    if state is None:
        return sums, total, top
    old_sums, old_total, old_top = state
    new_top = jnp.maximum(top, old_top)
    old, new = jnp.exp2(old_top - new_top), jnp.exp2(top - new_top)
    return old * old_sums + new * sums, old * old_total + new * total, new_top


def decode_group(group, queries, both, at, state, put):
    size = len(group) * PAIR
    for place, pair in enumerate(group):
        lanes = slice(place * PAIR, (place + 1) * PAIR)
        value_lanes = slice(size + place * PAIR, size + (place + 1) * PAIR)
        old = None if state is None else [part[at, lanes] for part in state]
        put(lanes, pair, decode_part(queries[pair, at, :], both[:, lanes], both[:, value_lanes], old))


def decode_tokens(group, queries, both, state, new_state):
    block = queries.shape[1] // 2
    for index in range(2):
        at = slice(index * block, (index + 1) * block)

        def put(lanes, pair, new):
            for out, part in zip(new_state, new):
                out[at, lanes] = part

        decode_group(group, queries, both, at, state, put)


def decode_own_kernel(queries, weights, more_weights, own, latent_out, *refs):
    *states, staged, sent = refs
    quad, core = bits_of()
    rows = own.shape[0]
    moves = place_rows([own], [quad * rows], latent_out, staged, sent)

    @apart
    def _():
        for group, weight, state in zip(
            groups_of(queries.shape[0]), [weights, more_weights], [states[:3], states[3:]]
        ):
            both = nn(own[...], weight[...]).astype(BF16)
            decode_tokens(group, queries, both, None, state)

    wait_all(moves)


def decode_sides_kernel(came, queries, weights, more_weights, near, far, latent_in, *refs):
    groups = groups_of(queries.shape[0])[:1 if came else 2]
    count = 3 * len(groups)
    states, (latent_out, *refs) = refs[:count], refs[count:]
    new_states, (gathered, staged, sent) = refs[:count], refs[count:]
    quad, core = bits_of()
    half = near.shape[0]
    across = [quad ^ (1 + core), quad ^ (2 - core)]
    which = 1 - core if came else core
    pieces = [near, far]
    spots = [(at * 2 + which) * half for at in (across[::-1] if came else across)]
    moves = place_rows(pieces, spots, latent_out, staged, sent)

    @apart
    def _():
        for index, piece in enumerate(pieces):
            gathered[index * half:(index + 1) * half, :] = piece[...]
        for index, (group, weight) in enumerate(zip(groups, [weights, more_weights])):
            both = nn(gathered[...], weight[...]).astype(BF16)
            at = slice(3 * index, 3 * index + 3)
            decode_tokens(group, queries, both, states[at], new_states[at])

    wait_all(moves)


def decode_rest_kernel(queries, weights, near, far, *refs):
    state, (*new_state, gathered) = refs[:3], refs[3:]
    half = near.shape[0]
    gathered[:half, :] = near[...]
    gathered[half:, :] = far[...]
    both = nn(gathered[...], weights[...]).astype(BF16)
    decode_tokens(groups_of(queries.shape[0])[1], queries, both, state, new_state)


def decode_send_kernel(queries, weights, more_weights, mine, came, *refs):
    states, (send, *boths, gathered) = refs[:6], refs[6:]
    core = lax.axis_index("qgrp")
    half = mine.shape[0]
    gathered[:half, :] = mine[...]
    gathered[half:, :] = came[...]
    for both, weight in zip(boths, [weights, more_weights]):
        both[...] = nn(gathered[...], weight[...]).astype(BF16)
    decode_last(1 - core, queries, boths, states, send)


def decode_last(which, queries, boths, states, out):
    block = out.shape[0]
    at = pl.ds(pl.multiple_of(which * block, block), block)

    def put(lanes, pair, new):
        out[:, pair * PAIR:(pair + 1) * PAIR] = (new[0] / new[1]).astype(BF16)

    for group, both, state in zip(
        groups_of(queries.shape[0]), boths, [states[:3], states[3:]]
    ):
        decode_group(group, queries, both, at, state, put)


def decode_keep_kernel(queries, both, more_both, tokens, weight, mine, came, latent_in, *refs):
    *states, latent_out, base, attended, staged, sent = refs
    quad, core = bits_of()
    half = mine.shape[0]
    corner = (quad ^ 3) * 2 * half
    spots = [corner + core * half, corner + (1 - core) * half]
    moves = place_rows([mine, came], spots, latent_out, staged, sent)

    @apart
    def _():
        decode_last(core, queries, [both, more_both], states, attended)
        rows = base.shape[0]
        own = tokens[pl.ds(pl.multiple_of(core * rows, rows), rows), :].astype(F32)
        base[...] = own + nn(attended[...], weight[...])

    wait_all(moves)


def tokens_kernel(count, base, other, weight, out, staged, sent):
    start = lax.axis_index("qgrp") * base.shape[0]
    pieces = sent.shape[0]
    columns = base.shape[1] // pieces
    moves = []
    for index in range(pieces):
        at = pl.ds(index * columns, columns)
        value = base[:, at] + nn(other[...], weight[:, pl.ds(out.shape[1] + index * columns, columns)])
        slot = start + lax.broadcasted_iota(jnp.int32, value.shape, 0)
        staged[:, at] = jnp.where(slot < count[0:1, 0:1], value, 0.0)
        moves.append(pltpu.make_async_copy(staged.at[:, at], out.at[:, at], sent.at[index]))
        moves[-1].start()
    wait_all(moves)


SPACES = {
    "v": pl.BlockSpec(memory_space=pltpu.VMEM),
    "h": pl.BlockSpec(memory_space=pltpu.HBM),
    "a": pl.BlockSpec(memory_space=pl.ANY),
}


def call(kernel, ins, outs, *args, far=(), alias=None, scratch=(), vmem=24, flops=0, moved=0, after=(),
         name=None):
    given, more = len(args), len(after)
    args = [
        pltpu.with_memory_space_constraint(arg, pltpu.HBM) if kind == "h" else arg
        for kind, arg in zip(ins, args)
    ]
    if more:
        alone = kernel

        def kernel(*refs):
            alone(*refs[:given], *refs[given + more:])

    shapes = [jax.ShapeDtypeStruct(*out) for out in outs]
    moved = moved or sum(a.size * a.dtype.itemsize for a in [*args, *shapes])
    return pl.pallas_call(
        kernel,
        out_shape=shapes,
        in_specs=[SPACES[kind] for kind in ins + "h" * more],
        out_specs=[SPACES["h" if index in far else "v"] for index in range(len(outs))],
        input_output_aliases=alias or {},
        scratch_shapes=list(scratch),
        compiler_params=pltpu.CompilerParams(vmem_limit_bytes=vmem * MIB),
        cost_estimate=pl.CostEstimate(flops=flops, bytes_accessed=moved, transcendentals=0),
        name=name,
    )(*args, *after)


def body(tokens, tally, latents, softness, wq, wk, wv, wo, dq, dk, dv, do, gain):
    cells = lax.axis_size("cell")
    total_rows, model = latents.shape
    rows, width = total_rows // 4, wq.shape[1]
    slots = tokens.shape[0]
    half_slots = slots // 2
    deep = rows + log_rows(rows, width)

    def swap(array):
        return lax.ppermute(array, "qgrp", [(0, 1), (1, 0)])

    def trade(array, bit_0, bit_1):
        pairs = []
        for cell in range(cells):
            pairs.append((2 * cell, 2 * (cell ^ bit_0)))
            pairs.append((2 * cell + 1, 2 * (cell ^ bit_1) + 1))
        return lax.ppermute(array, ("cell", "qgrp"), pairs)

    attention = 4 * 256 * slots * width * 4
    sent = ((deep, width), BF16)
    message, keys, values, scales, count, wq, latents, outputs = call(
        encode_first_kernel, "ahhhhhhhh",
        [
            sent, *[((slots, width), BF16)] * 2,
            ((2, 8, width), F32), ((8, PAIR), jnp.int32), (wq.shape, BF16), (latents.shape, BF16),
            ((width, 2 * model), BF16),
        ],
        tally, softness, latents, tokens, wq, wk, wv, wo, do,
        scratch=[
            pltpu.SMEM(tally.shape, tally.dtype), pltpu.SMEM(softness.shape, F32),
            pltpu.VMEM(tokens.shape, BF16), *[pltpu.VMEM((model, width), BF16)] * 2,
            pltpu.SemaphoreType.DMA((12,)),
        ],
        flops=attention, name="encode_corner",
    )
    came = trade(message, 1, 2)
    state = [((rows, width), F32), ((8, rows), F32)]
    (message,) = call(
        encode_side_kernel, "vvvvvv", [sent], count, scales, latents, wq, keys, values,
        flops=attention, name="encode_side",
    )
    first = trade(message, 1, 2)
    passed = call(
        functools.partial(encode_keep_kernel, False), "vvvvvv", state,
        count, scales, latents, wq, keys, values, flops=attention, after=[message],
        name="encode_pass",
    )
    half = rows // 2
    half_sent = ((half + log_rows(half, width), width), BF16)
    messages = call(
        merge_pass_kernel, "vvv", [half_sent] * 2, *passed, came, name="merge_pass"
    )
    seconds = [trade(message, 2, 1) for message in messages]
    kept, kept_logs = call(
        functools.partial(encode_keep_kernel, True), "vvvvvv", state,
        count, scales, latents, wq, keys, values,
        flops=attention, after=messages, name="encode_own",
    )
    other_outputs = swap(outputs)
    parts = []
    for which in range(2):
        parts += call(
            functools.partial(merge_sides_kernel, which), "vvvv",
            [half_sent], kept, kept_logs, first, seconds[which],
            after=parts, name="merge_sides",
        )
    sizes = [len(group) * PAIR for group in groups_of(width // PAIR)]
    queries, *weights = call(
        decode_prepare_kernel, "vvvvv",
        [
            ((width // PAIR, slots, 2 * PAIR), BF16),
            *[((model, 2 * size), BF16) for size in sizes],
        ],
        scales, tokens, dq, dk, dv, after=parts, name="decode_prepare",
    )
    bits = [4 << i for i in range(max(cells.bit_length() - 3, 0))]
    for index, (bit_0, bit_1) in enumerate(zip(bits, bits[::-1])):
        last = index == len(bits) - 1
        merged = []
        for part, came in [(part, trade(part, bit_0, bit_1)) for part in parts]:
            merged += call(
                functools.partial(merge_even_kernel, bit_0, bit_1, last, half), "vv",
                [((half, width), BF16) if last else (part.shape, BF16)], part, came,
                after=[*merged, queries] if last else merged, name="merge_even",
            )
        parts = merged
    parts = [part[:half] for part in parts]
    (own_low,) = call(
        functools.partial(latent_kernel, 0), "vvvvvv", [((half, model), BF16)],
        parts[0], swap(parts[0]), wo, other_outputs, latents, gain.reshape(1, model),
        after=parts[1:], name="latent_low",
    )
    own, own_half = call(
        functools.partial(latent_kernel, 1), "vvvvvvv",
        [((rows, model), BF16), ((half, model), BF16)],
        parts[1], swap(parts[1]), wo, other_outputs, latents, gain.reshape(1, model), own_low,
        name="latent",
    )
    first = trade(own_half, 1, 2)
    second = trade(own_half, 2, 1)
    whole = ((total_rows, model), F32)
    states_out = [((slots, size), F32) for size in sizes for _ in range(3)]

    def scratch(count, pieces):
        return [pltpu.VMEM((count, model), F32), pltpu.SemaphoreType.DMA((pieces,))]

    latent_out, *states = call(
        decode_own_kernel, "vvvv", [whole, *states_out], queries, *weights, own,
        far=(0,), scratch=scratch(rows, 1), flops=attention, name="decode_own",
    )
    first, states[0] = lax.optimization_barrier((first, states[0]))
    third = trade(first, 2, 1)

    def decode_sides(came, near, far, latent_out, states):
        used = states[:3] if came else states
        latent_out, *used = call(
            functools.partial(decode_sides_kernel, came), "vvvvvh" + "v" * len(used),
            [whole, *states_out[:len(used)]],
            queries, *weights, near, far, latent_out, *used, far=(0,), alias={5: 0},
            scratch=[pltpu.VMEM((rows, model), BF16), *scratch(rows, 2)], flops=attention,
            name="decode_sides",
        )
        return latent_out, [*used, *states[len(used):]]

    came_first, came_second = swap(first), swap(second)
    latent_out, states = decode_sides(False, first, second, latent_out, states)
    latent_out, states = decode_sides(True, came_first, came_second, latent_out, states)
    third, states[0] = lax.optimization_barrier((third, states[0]))
    came = swap(third)
    states[3:] = call(
        decode_rest_kernel, "vvvvvvv", states_out[3:],
        queries, weights[1], came_first, came_second, *states[3:],
        scratch=[pltpu.VMEM((rows, model), BF16)], flops=attention, after=states[1:2],
        name="decode_rest",
    )
    send, *boths = call(
        decode_send_kernel, "vvvvvvvvvvv",
        [((half_slots, width), BF16), *[((rows, 2 * size), BF16) for size in sizes]],
        queries, *weights, third, came, *states, scratch=[pltpu.VMEM((rows, model), BF16)],
        flops=attention // 2, name="decode_send",
    )
    latent_out, base = call(
        decode_keep_kernel, "vvvvvvvhvvvvvv", [whole, ((half_slots, model), F32)],
        queries, *boths, tokens, do, third, came, latent_out, *states, far=(0,), alias={7: 0},
        scratch=[pltpu.VMEM((half_slots, width), BF16), *scratch(rows, 2)],
        flops=attention // 2, name="decode_keep",
    )
    (tokens_out,) = call(
        tokens_kernel, "vvvv", [((half_slots, model), F32)], count, base, swap(send), other_outputs,
        far=(0,), scratch=scratch(half_slots, 3 if model % 384 == 0 else 1), name="tokens",
    )
    return latent_out, tokens_out


def solution(mesh):
    placed = (
        P("cell", None), P("cell"), P(), P(),
        P(None, "qgrp"), P(None, "qgrp"), P(None, "qgrp"), P("qgrp", None),
        P(None, "qgrp"), P(None, "qgrp"), P(None, "qgrp"), P("qgrp", None), P(),
    )
    return jax.shard_map(
        body, mesh=mesh, in_specs=placed, out_specs=(P(), P(("cell", "qgrp"), None)),
        check_vma=False,
    )
```

```python
import functools
import math

import jax
import jax.numpy as jnp
from jax import lax
from jax.experimental import pallas as pl
from jax.experimental.pallas import tpu as pltpu
from jax.sharding import PartitionSpec as P

HEAD_DIM = 64
PAIR = 2 * HEAD_DIM
NORM_EPSILON = 1e-06
LOG2E = math.log2(math.e)
F32 = jnp.float32
BF16 = jnp.bfloat16
MIB = 1 << 20


def nn(a, b):
    return lax.dot_general(a, b, (((1,), (0,)), ((), ())), preferred_element_type=F32)


def nt(a, b):
    return lax.dot_general(a, b, (((1,), (1,)), ((), ())), preferred_element_type=F32)


def tn(a, b):
    return lax.dot_general(a, b, (((0,), (0,)), ((), ())), preferred_element_type=F32)


def log_rows(rows, width):
    return 8 if 3 * rows <= width else 16


def head_of(row):
    return 2 * jnp.bitwise_and(row, 3) + jnp.bitwise_and(lax.shift_right_logical(row, 2), 1)


def compact_logs(totals, tops):
    lane = lax.broadcasted_iota(jnp.int32, tops[0].shape, 1)

    def chosen(parts):
        out = parts[-1]
        for pair in range(len(parts) - 1):
            out = jnp.where(jnp.bitwise_and(lane, 3) == pair, parts[pair], out)
        return out

    turned = (chosen(tops) + jnp.log2(chosen(totals))).T
    row = lax.broadcasted_iota(jnp.int32, (8, turned.shape[1]), 0)
    return jnp.where(row < 4, turned[:8], turned[HEAD_DIM:HEAD_DIM + 8])


def pack_logs(logs, width):
    rows = logs.shape[1]
    high = logs.astype(BF16).astype(F32)
    middle = (logs - high).astype(BF16).astype(F32)
    low = (logs - high - middle).astype(BF16).astype(F32)
    if 3 * rows <= width:
        return jnp.concatenate([high, middle, low], axis=1).astype(BF16)
    half = rows // 2
    below = jnp.concatenate([high, middle], axis=0)
    beside = jnp.concatenate([low[:, :half], low[:, half:]], axis=0)
    return jnp.concatenate([below, beside], axis=1).astype(BF16)


def unpack_logs(packed, rows):
    packed = packed.astype(F32)
    if 3 * rows <= packed.shape[1]:
        return packed[:8, :rows] + packed[:8, rows:2 * rows] + packed[:8, 2 * rows:3 * rows]
    low = jnp.concatenate([packed[:8, rows:], packed[8:, rows:]], axis=1)
    return packed[:8, :rows] + packed[8:, :rows] + low


def merge(values_a, logs_a, values_b, logs_b):
    width = values_a.shape[1]
    top = jnp.maximum(logs_a, logs_b)
    part_a, part_b = jnp.exp2(logs_a - top), jnp.exp2(logs_b - top)
    whole = part_a + part_b
    share = part_a / whole
    high = share.astype(BF16).astype(F32)
    terms = jnp.concatenate([high, share - high], axis=0).astype(BF16)
    row = lax.broadcasted_iota(jnp.int32, (16, width), 0)
    lane = lax.broadcasted_iota(jnp.int32, (16, width), 1)
    inside = jnp.bitwise_and(row, 3) < width // PAIR
    spread = inside & (lax.shift_right_logical(lane, 6) == head_of(row))
    share = tn(terms, jnp.where(spread, 1.0, 0.0).astype(BF16))
    return share * values_a + (1.0 - share) * values_b, top + jnp.log2(whole)


def scale_row(softness_ref, which, heads):
    first = lax.axis_index("qgrp") * heads
    lane_head = lax.shift_right_logical(
        lax.broadcasted_iota(jnp.int32, (1, heads * HEAD_DIM), 1), 6
    )
    row = jnp.zeros((1, heads * HEAD_DIM), F32)
    for head in range(heads):
        row = jnp.where(lane_head == head, softness_ref[which, first + head], row)
    return row * (HEAD_DIM**-0.5 * LOG2E)


def split_scaled(queries, row):
    scaled = queries.astype(BF16).astype(F32) * row
    high = scaled.astype(BF16)
    return high, (scaled - high.astype(F32)).astype(BF16)


def pair_keys(keys):
    lane = lax.broadcasted_iota(jnp.int32, keys.shape, 1)
    zero = jnp.zeros_like(keys)
    first, second = jnp.where(lane < HEAD_DIM, keys, zero), jnp.where(lane < HEAD_DIM, zero, keys)
    return jnp.concatenate(
        [jnp.concatenate([first, first], axis=1), jnp.concatenate([second, second], axis=1)], axis=0
    )


def pair_values(values, counted):
    lane = lax.broadcasted_iota(jnp.int32, values.shape, 1)
    zero = jnp.zeros_like(values)
    low = lane < HEAD_DIM
    top = jnp.concatenate([jnp.where(low, values, zero), jnp.where(low, counted, zero)], axis=1)
    end = jnp.concatenate([jnp.where(low, zero, values), jnp.where(low, zero, counted)], axis=1)
    return jnp.concatenate([top, end], axis=0)


def attend_pair(high, low, keys, values):
    count = keys.shape[0] // 2
    scores = nt(jnp.concatenate([high, low], axis=1), keys)
    top_a = jnp.max(scores[:, :count], axis=1, keepdims=True)
    top_b = jnp.max(scores[:, count:], axis=1, keepdims=True)
    weights = jnp.concatenate(
        [
            jnp.exp2(scores[:, :count] - top_a).astype(BF16),
            jnp.exp2(scores[:, count:] - top_b).astype(BF16),
        ],
        axis=1,
    )
    sums = nn(weights, values)
    lane = lax.broadcasted_iota(jnp.int32, (high.shape[0], PAIR), 1)
    top = jnp.where(lane < HEAD_DIM, top_a, top_b)
    return sums[:, :PAIR], sums[:, PAIR:], top


def encode_rows(part, query_weight, keys, values, count, scale, put):
    width = query_weight.shape[1]
    slots = keys.shape[0]
    slot = lax.broadcasted_iota(jnp.int32, (slots, PAIR), 0)
    counted = jnp.where(slot < count, 1.0, 0.0).astype(BF16)
    high, low = split_scaled(nn(part, query_weight[...]), scale)
    totals, tops = [], []
    for pair in range(width // PAIR):
        lanes = slice(pair * PAIR, (pair + 1) * PAIR)
        key_block = pair_keys(keys[:, lanes])
        value_block = pair_values(values[:, lanes], counted)
        sums, total, top = attend_pair(high[:, lanes], low[:, lanes], key_block, value_block)
        put(lanes, sums / total)
        totals.append(total)
        tops.append(top)
    return compact_logs(totals, tops)


def bits_of():
    cell, core = lax.axis_index("cell"), lax.axis_index("qgrp")
    quad = jnp.bitwise_and(cell, 3)
    return quad, core


def start_all(pairs, arrived):
    moves = [
        pltpu.make_async_copy(source, goal, arrived.at[index])
        for index, (source, goal) in enumerate(pairs)
    ]
    for move in moves:
        move.start()
    return moves


def wait_all(moves):
    for move in moves:
        move.wait()


def quarter(latents, quad, rows):
    return latents.at[pl.ds(pl.multiple_of(quad * rows, rows), rows), :]


def encode_first_kernel(
    tally, softness_far, latents_far, tokens_far, wq_far, wk_far, wv_far, wo_far, do_far,
    message, keys, values, scales, count_out, wq, latents, outputs,
    count, softness, tokens, wk, wv, arrived, arrived_later,
):
    quad, core = bits_of()
    rows, model = latents.shape[0] // 4, wo_far.shape[1]
    moves = start_all(
        [
            (tally, count), (tokens_far, tokens), (wk_far, wk), (wv_far, wv), (wq_far, wq),
            (softness_far, softness),
            (quarter(latents_far, quad ^ 3, rows), quarter(latents, quad ^ 3, rows)),
        ],
        arrived,
    )
    wait_all(moves[:3])
    is_valid = lax.broadcasted_iota(jnp.int32, keys.shape, 0) < count[0]
    made = nn(tokens[...], wk[...])
    keys[...] = jnp.where(is_valid, made, made[0:1, :]).astype(BF16)
    wait_all(moves[3:])
    later = start_all(
        [
            (wo_far, outputs.at[:, :model]), (do_far, outputs.at[:, model:]),
            *[
                (quarter(latents_far, quad ^ other, rows), quarter(latents, quad ^ other, rows))
                for other in (1, 2, 0)
            ],
        ],
        arrived_later,
    )
    values[...] = jnp.where(is_valid, nn(tokens[...], wv[...]), 0.0).astype(BF16)

    @apart
    def _():
        count_out[...] = jnp.full(count_out.shape, count[0], jnp.int32)
        for which in range(2):
            row = scale_row(softness, which, wq.shape[1] // HEAD_DIM)
            scales[which] = jnp.broadcast_to(row, scales.shape[1:])
        part = quarter(latents, quad ^ 3, rows)[...]
        encode_into(message, part, wq, keys, values, count_out, scales)

    wait_all(later)


def encode_into(message, part, wq, keys, values, count, scales):
    rows = part.shape[0]

    def put(lanes, sums):
        message[:rows, lanes] = sums.astype(BF16)

    logs = encode_rows(part, wq, keys, values, count[0:1, :], scales[0, 0:1, :], put)
    message[rows:, :] = pack_logs(logs, message.shape[1])


def encode_side_kernel(count, scales, latents, wq, keys, values, message):
    quad, core = bits_of()
    rows = latents.shape[0] // 4
    side = quad ^ jnp.where(core == 0, 1, 2)
    part = quarter(latents, side, rows)[...]
    encode_into(message, part, wq, keys, values, count, scales)


def encode_keep_kernel(is_own, count, scales, latents, wq, keys, values, kept, logs):
    quad, core = bits_of()
    rows = kept.shape[0]

    def put(lanes, part):
        kept[:, lanes] = part

    at = quad if is_own else quad ^ jnp.where(core == 0, 2, 1)
    part = quarter(latents, at, rows)[...]
    logs[...] = encode_rows(part, wq, keys, values, count[0:1, :], scales[0, 0:1, :], put)

def write_message(message, values, logs):
    rows = values.shape[0]
    message[:rows, :] = values.astype(BF16)
    message[rows:, :] = pack_logs(logs, message.shape[1])


def read_message(message, rows):
    return message[:rows, :].astype(F32), unpack_logs(message[rows:, :], rows)


def merge_pass_kernel(values, logs, came, *messages):
    rows = values.shape[0]
    half = rows // 2
    part, log = merge(values[...], logs[...], *read_message(came, rows))
    for which, message in enumerate(messages):
        at = slice(which * half, (which + 1) * half)
        write_message(message, part[at], log[:, at])


def merge_sides_kernel(which, values, logs, first, second, message):
    rows = values.shape[0]
    half = rows // 2
    at = slice(which * half, (which + 1) * half)
    part, log = values[at, :], logs[:, at]
    came_part, came_log = read_message(first, rows)
    part, log = merge(part, log, came_part[at], came_log[:, at])
    part, log = merge(part, log, *read_message(second, half))
    write_message(message, part, log)


def merge_even_kernel(own_bit, other_bit, last, rows, mine, came, out):
    core = lax.axis_index("qgrp")
    bit = jnp.where(core == 0, own_bit, other_bit)
    is_low = jnp.bitwise_and(lax.axis_index("cell"), bit) == 0

    def both(first, second):
        part, log = merge(*read_message(first, rows), *read_message(second, rows))
        if last:
            out[...] = part.astype(BF16)
        else:
            write_message(out, part, log)

    @pl.when(is_low)
    def _():
        both(mine, came)

    @pl.when(jnp.logical_not(is_low))
    def _():
        both(came, mine)


def latent_kernel(which, attended, other, weight, other_weight, latents, gain, *refs):
    quad, core = bits_of()
    half, model = attended.shape[0], weight.shape[1]
    start = pl.ds(pl.multiple_of((2 * quad + which) * half, half), half)

    def finish(first, second, first_weight, second_weight):
        update = nn(first[...], first_weight) + nn(second[...], second_weight)
        pre = latents[start, :].astype(F32) + update
        mean_square = jnp.mean(pre * pre, axis=-1, keepdims=True)
        done = (pre * lax.rsqrt(mean_square + NORM_EPSILON) * gain[...]).astype(BF16)
        if which == 0:
            refs[0][...] = done
        else:
            low, out, own_half = refs
            out[:half, :] = low[...]
            out[half:, :] = done
            own_half[...] = jnp.where(core == 0, low[...], done)

    @pl.when(core == 0)
    def _():
        finish(attended, other, weight[...], other_weight[:, :model])

    @pl.when(core != 0)
    def _():
        finish(other, attended, other_weight[:, :model], weight[...])


def groups_of(pairs):
    first = -(-2 * pairs // 3)
    return [range(first), range(first, pairs)]


def decode_prepare_kernel(scales, tokens, wq, wk, wv, out, *weights):
    width = wq.shape[1]
    high, low = split_scaled(nn(tokens[...], wq[...]), scales[1, 0:1, :])
    for pair in range(width // PAIR):
        lanes = slice(pair * PAIR, (pair + 1) * PAIR)
        out[pair, :, :PAIR] = high[:, lanes]
        out[pair, :, PAIR:] = low[:, lanes]
    for group, both in zip(groups_of(width // PAIR), weights):
        lanes = slice(group[0] * PAIR, (group[-1] + 1) * PAIR)
        size = len(group) * PAIR
        both[:, :size] = wk[:, lanes]
        both[:, size:] = wv[:, lanes]


def apart(work):
    pl.when(lax.axis_index("qgrp") >= 0)(work)


def place_rows(pieces, spots, latent_out, staged, sent):
    moves, start = [], 0
    for index, (piece, spot) in enumerate(zip(pieces, spots)):
        count = piece.shape[0]
        staged[start:start + count, :] = piece[...].astype(F32)
        moves.append(
            pltpu.make_async_copy(
                staged.at[pl.ds(start, count), :],
                latent_out.at[pl.ds(pl.multiple_of(spot, count), count), :],
                sent.at[index],
            )
        )
        moves[-1].start()
        start += count
    return moves


def decode_part(queries, keys, values, state):
    high, low = queries[:, :PAIR], queries[:, PAIR:]
    one = jnp.ones((keys.shape[0], PAIR), BF16)
    sums, total, top = attend_pair(high, low, pair_keys(keys), pair_values(values, one))
    if state is None:
        return sums, total, top
    old_sums, old_total, old_top = state
    new_top = jnp.maximum(top, old_top)
    old, new = jnp.exp2(old_top - new_top), jnp.exp2(top - new_top)
    return old * old_sums + new * sums, old * old_total + new * total, new_top


def decode_group(group, queries, both, at, state, put):
    size = len(group) * PAIR
    for place, pair in enumerate(group):
        lanes = slice(place * PAIR, (place + 1) * PAIR)
        value_lanes = slice(size + place * PAIR, size + (place + 1) * PAIR)
        old = None if state is None else [part[at, lanes] for part in state]
        put(lanes, pair, decode_part(queries[pair, at, :], both[:, lanes], both[:, value_lanes], old))


def decode_tokens(group, queries, both, state, new_state):
    block = queries.shape[1] // 2
    for index in range(2):
        at = slice(index * block, (index + 1) * block)

        def put(lanes, pair, new):
            for out, part in zip(new_state, new):
                out[at, lanes] = part

        decode_group(group, queries, both, at, state, put)


def decode_own_kernel(queries, weights, more_weights, own, latent_out, *refs):
    *states, staged, sent = refs
    quad, core = bits_of()
    rows = own.shape[0]
    moves = place_rows([own], [quad * rows], latent_out, staged, sent)

    @apart
    def _():
        for group, weight, state in zip(
            groups_of(queries.shape[0]), [weights, more_weights], [states[:3], states[3:]]
        ):
            both = nn(own[...], weight[...]).astype(BF16)
            decode_tokens(group, queries, both, None, state)

    wait_all(moves)


def decode_sides_kernel(came, queries, weights, more_weights, near, far, latent_in, *refs):
    groups = groups_of(queries.shape[0])[:1 if came else 2]
    count = 3 * len(groups)
    states, (latent_out, *refs) = refs[:count], refs[count:]
    new_states, (gathered, staged, sent) = refs[:count], refs[count:]
    quad, core = bits_of()
    half = near.shape[0]
    across = [quad ^ (1 + core), quad ^ (2 - core)]
    which = 1 - core if came else core
    pieces = [near, far]
    spots = [(at * 2 + which) * half for at in (across[::-1] if came else across)]
    moves = place_rows(pieces, spots, latent_out, staged, sent)

    @apart
    def _():
        for index, piece in enumerate(pieces):
            gathered[index * half:(index + 1) * half, :] = piece[...]
        for index, (group, weight) in enumerate(zip(groups, [weights, more_weights])):
            both = nn(gathered[...], weight[...]).astype(BF16)
            at = slice(3 * index, 3 * index + 3)
            decode_tokens(group, queries, both, states[at], new_states[at])

    wait_all(moves)


def decode_rest_kernel(queries, weights, near, far, *refs):
    state, (*new_state, gathered) = refs[:3], refs[3:]
    half = near.shape[0]
    gathered[:half, :] = near[...]
    gathered[half:, :] = far[...]
    both = nn(gathered[...], weights[...]).astype(BF16)
    decode_tokens(groups_of(queries.shape[0])[1], queries, both, state, new_state)


def decode_send_kernel(queries, weights, more_weights, mine, came, *refs):
    states, (send, *boths, gathered) = refs[:6], refs[6:]
    core = lax.axis_index("qgrp")
    half = mine.shape[0]
    gathered[:half, :] = mine[...]
    gathered[half:, :] = came[...]
    for both, weight in zip(boths, [weights, more_weights]):
        both[...] = nn(gathered[...], weight[...]).astype(BF16)
    decode_last(1 - core, queries, boths, states, send)


def decode_last(which, queries, boths, states, out):
    block = out.shape[0]
    at = pl.ds(pl.multiple_of(which * block, block), block)

    def put(lanes, pair, new):
        out[:, pair * PAIR:(pair + 1) * PAIR] = (new[0] / new[1]).astype(BF16)

    for group, both, state in zip(
        groups_of(queries.shape[0]), boths, [states[:3], states[3:]]
    ):
        decode_group(group, queries, both, at, state, put)


def decode_keep_kernel(queries, both, more_both, tokens, weight, mine, came, latent_in, *refs):
    *states, latent_out, base, attended, staged, sent = refs
    quad, core = bits_of()
    half = mine.shape[0]
    corner = (quad ^ 3) * 2 * half
    spots = [corner + core * half, corner + (1 - core) * half]
    moves = place_rows([mine, came], spots, latent_out, staged, sent)

    @apart
    def _():
        decode_last(core, queries, [both, more_both], states, attended)
        rows = base.shape[0]
        own = tokens[pl.ds(pl.multiple_of(core * rows, rows), rows), :].astype(F32)
        base[...] = own + nn(attended[...], weight[...])

    wait_all(moves)


def tokens_kernel(count, base, other, weight, out, staged, sent):
    start = lax.axis_index("qgrp") * base.shape[0]
    pieces = sent.shape[0]
    columns = base.shape[1] // pieces
    moves = []
    for index in range(pieces):
        at = pl.ds(index * columns, columns)
        value = base[:, at] + nn(other[...], weight[:, pl.ds(out.shape[1] + index * columns, columns)])
        slot = start + lax.broadcasted_iota(jnp.int32, value.shape, 0)
        staged[:, at] = jnp.where(slot < count[0:1, 0:1], value, 0.0)
        moves.append(pltpu.make_async_copy(staged.at[:, at], out.at[:, at], sent.at[index]))
        moves[-1].start()
    wait_all(moves)


SPACES = {
    "v": pl.BlockSpec(memory_space=pltpu.VMEM),
    "h": pl.BlockSpec(memory_space=pltpu.HBM),
    "a": pl.BlockSpec(memory_space=pl.ANY),
}


def call(kernel, ins, outs, *args, far=(), alias=None, scratch=(), vmem=24, flops=0, moved=0, after=(),
         name=None):
    given, more = len(args), len(after)
    args = [
        pltpu.with_memory_space_constraint(arg, pltpu.HBM) if kind == "h" else arg
        for kind, arg in zip(ins, args)
    ]
    if more:
        alone = kernel

        def kernel(*refs):
            alone(*refs[:given], *refs[given + more:])

    shapes = [jax.ShapeDtypeStruct(*out) for out in outs]
    moved = moved or sum(a.size * a.dtype.itemsize for a in [*args, *shapes])
    return pl.pallas_call(
        kernel,
        out_shape=shapes,
        in_specs=[SPACES[kind] for kind in ins + "h" * more],
        out_specs=[SPACES["h" if index in far else "v"] for index in range(len(outs))],
        input_output_aliases=alias or {},
        scratch_shapes=list(scratch),
        compiler_params=pltpu.CompilerParams(vmem_limit_bytes=vmem * MIB),
        cost_estimate=pl.CostEstimate(flops=flops, bytes_accessed=moved, transcendentals=0),
        name=name,
    )(*args, *after)


def body(tokens, tally, latents, softness, wq, wk, wv, wo, dq, dk, dv, do, gain):
    cells = lax.axis_size("cell")
    total_rows, model = latents.shape
    rows, width = total_rows // 4, wq.shape[1]
    slots = tokens.shape[0]
    half_slots = slots // 2
    deep = rows + log_rows(rows, width)

    def swap(array):
        return lax.ppermute(array, "qgrp", [(0, 1), (1, 0)])

    def trade(array, bit_0, bit_1):
        pairs = []
        for cell in range(cells):
            pairs.append((2 * cell, 2 * (cell ^ bit_0)))
            pairs.append((2 * cell + 1, 2 * (cell ^ bit_1) + 1))
        return lax.ppermute(array, ("cell", "qgrp"), pairs)

    attention = 4 * 256 * slots * width * 4
    sent = ((deep, width), BF16)
    message, keys, values, scales, count, wq, latents, outputs = call(
        encode_first_kernel, "ahhhhhhhh",
        [
            sent, *[((slots, width), BF16)] * 2,
            ((2, 8, width), F32), ((8, PAIR), jnp.int32), (wq.shape, BF16), (latents.shape, BF16),
            ((width, 2 * model), BF16),
        ],
        tally, softness, latents, tokens, wq, wk, wv, wo, do,
        scratch=[
            pltpu.SMEM(tally.shape, tally.dtype), pltpu.SMEM(softness.shape, F32),
            pltpu.VMEM(tokens.shape, BF16), *[pltpu.VMEM((model, width), BF16)] * 2,
            pltpu.SemaphoreType.DMA((7,)), pltpu.SemaphoreType.DMA((5,)),
        ],
        flops=attention, name="encode_corner",
    )
    came = trade(message, 1, 2)
    state = [((rows, width), F32), ((8, rows), F32)]
    (message,) = call(
        encode_side_kernel, "vvvvvv", [sent], count, scales, latents, wq, keys, values,
        flops=attention, name="encode_side",
    )
    first = trade(message, 1, 2)
    passed = call(
        functools.partial(encode_keep_kernel, False), "vvvvvv", state,
        count, scales, latents, wq, keys, values, flops=attention, after=[message],
        name="encode_pass",
    )
    half = rows // 2
    half_sent = ((half + log_rows(half, width), width), BF16)
    messages = call(
        merge_pass_kernel, "vvv", [half_sent] * 2, *passed, came, name="merge_pass"
    )
    seconds = [trade(message, 2, 1) for message in messages]
    kept, kept_logs = call(
        functools.partial(encode_keep_kernel, True), "vvvvvv", state,
        count, scales, latents, wq, keys, values,
        flops=attention, after=messages, name="encode_own",
    )
    other_outputs = swap(outputs)
    parts = []
    for which in range(2):
        parts += call(
            functools.partial(merge_sides_kernel, which), "vvvv",
            [half_sent], kept, kept_logs, first, seconds[which],
            after=parts, name="merge_sides",
        )
    sizes = [len(group) * PAIR for group in groups_of(width // PAIR)]
    queries, *weights = call(
        decode_prepare_kernel, "vvvvv",
        [
            ((width // PAIR, slots, 2 * PAIR), BF16),
            *[((model, 2 * size), BF16) for size in sizes],
        ],
        scales, tokens, dq, dk, dv, after=parts, name="decode_prepare",
    )
    bits = [4 << i for i in range(max(cells.bit_length() - 3, 0))]
    for index, (bit_0, bit_1) in enumerate(zip(bits, bits[::-1])):
        last = index == len(bits) - 1
        merged = []
        for part, came in [(part, trade(part, bit_0, bit_1)) for part in parts]:
            merged += call(
                functools.partial(merge_even_kernel, bit_0, bit_1, last, half), "vv",
                [((half, width), BF16) if last else (part.shape, BF16)], part, came,
                after=[*merged, queries] if last else merged, name="merge_even",
            )
        parts = merged
    parts = [part[:half] for part in parts]
    (own_low,) = call(
        functools.partial(latent_kernel, 0), "vvvvvv", [((half, model), BF16)],
        parts[0], swap(parts[0]), wo, other_outputs, latents, gain.reshape(1, model),
        after=parts[1:], name="latent_low",
    )
    own, own_half = call(
        functools.partial(latent_kernel, 1), "vvvvvvv",
        [((rows, model), BF16), ((half, model), BF16)],
        parts[1], swap(parts[1]), wo, other_outputs, latents, gain.reshape(1, model), own_low,
        name="latent",
    )
    first = trade(own_half, 1, 2)
    second = trade(own_half, 2, 1)
    whole = ((total_rows, model), F32)
    states_out = [((slots, size), F32) for size in sizes for _ in range(3)]

    def scratch(count, pieces):
        return [pltpu.VMEM((count, model), F32), pltpu.SemaphoreType.DMA((pieces,))]

    latent_out, *states = call(
        decode_own_kernel, "vvvv", [whole, *states_out], queries, *weights, own,
        far=(0,), scratch=scratch(rows, 1), flops=attention, name="decode_own",
    )
    first, states[0] = lax.optimization_barrier((first, states[0]))
    third = trade(first, 2, 1)

    def decode_sides(came, near, far, latent_out, states):
        used = states[:3] if came else states
        latent_out, *used = call(
            functools.partial(decode_sides_kernel, came), "vvvvvh" + "v" * len(used),
            [whole, *states_out[:len(used)]],
            queries, *weights, near, far, latent_out, *used, far=(0,), alias={5: 0},
            scratch=[pltpu.VMEM((rows, model), BF16), *scratch(rows, 2)], flops=attention,
            name="decode_sides",
        )
        return latent_out, [*used, *states[len(used):]]

    came_first, came_second = swap(first), swap(second)
    latent_out, states = decode_sides(False, first, second, latent_out, states)
    latent_out, states = decode_sides(True, came_first, came_second, latent_out, states)
    third, states[0] = lax.optimization_barrier((third, states[0]))
    came = swap(third)
    states[3:] = call(
        decode_rest_kernel, "vvvvvvv", states_out[3:],
        queries, weights[1], came_first, came_second, *states[3:],
        scratch=[pltpu.VMEM((rows, model), BF16)], flops=attention, after=states[1:2],
        name="decode_rest",
    )
    send, *boths = call(
        decode_send_kernel, "vvvvvvvvvvv",
        [((half_slots, width), BF16), *[((rows, 2 * size), BF16) for size in sizes]],
        queries, *weights, third, came, *states, scratch=[pltpu.VMEM((rows, model), BF16)],
        flops=attention // 2, name="decode_send",
    )
    latent_out, base = call(
        decode_keep_kernel, "vvvvvvvhvvvvvv", [whole, ((half_slots, model), F32)],
        queries, *boths, tokens, do, third, came, latent_out, *states, far=(0,), alias={7: 0},
        scratch=[pltpu.VMEM((half_slots, width), BF16), *scratch(rows, 2)],
        flops=attention // 2, name="decode_keep",
    )
    (tokens_out,) = call(
        tokens_kernel, "vvvv", [((half_slots, model), F32)], count, base, swap(send), other_outputs,
        far=(0,), scratch=scratch(half_slots, 3 if model % 384 == 0 else 1), name="tokens",
    )
    return latent_out, tokens_out


def solution(mesh):
    placed = (
        P("cell", None), P("cell"), P(), P(),
        P(None, "qgrp"), P(None, "qgrp"), P(None, "qgrp"), P("qgrp", None),
        P(None, "qgrp"), P(None, "qgrp"), P(None, "qgrp"), P("qgrp", None), P(),
    )
    return jax.shard_map(
        body, mesh=mesh, in_specs=placed, out_specs=(P(), P(("cell", "qgrp"), None)),
        check_vma=False,
    )
```

```python
import functools
import math

import jax
import jax.numpy as jnp
from jax import lax
from jax.experimental import pallas as pl
from jax.experimental.pallas import tpu as pltpu
from jax.sharding import PartitionSpec as P

HEAD_DIM = 64
PAIR = 2 * HEAD_DIM
NORM_EPSILON = 1e-06
LOG2E = math.log2(math.e)
F32 = jnp.float32
BF16 = jnp.bfloat16
MIB = 1 << 20


def nn(a, b):
    return lax.dot_general(a, b, (((1,), (0,)), ((), ())), preferred_element_type=F32)


def nt(a, b):
    return lax.dot_general(a, b, (((1,), (1,)), ((), ())), preferred_element_type=F32)


def tn(a, b):
    return lax.dot_general(a, b, (((0,), (0,)), ((), ())), preferred_element_type=F32)


def log_rows(rows, width):
    return 8 if 3 * rows <= width else 16


def head_of(row):
    return 2 * jnp.bitwise_and(row, 3) + jnp.bitwise_and(lax.shift_right_logical(row, 2), 1)


def compact_logs(totals, tops):
    lane = lax.broadcasted_iota(jnp.int32, tops[0].shape, 1)

    def chosen(parts):
        out = parts[-1]
        for pair in range(len(parts) - 1):
            out = jnp.where(jnp.bitwise_and(lane, 3) == pair, parts[pair], out)
        return out

    turned = (chosen(tops) + jnp.log2(chosen(totals))).T
    row = lax.broadcasted_iota(jnp.int32, (8, turned.shape[1]), 0)
    return jnp.where(row < 4, turned[:8], turned[HEAD_DIM:HEAD_DIM + 8])


def pack_logs(logs, width):
    rows = logs.shape[1]
    high = logs.astype(BF16).astype(F32)
    middle = (logs - high).astype(BF16).astype(F32)
    low = (logs - high - middle).astype(BF16).astype(F32)
    if 3 * rows <= width:
        return jnp.concatenate([high, middle, low], axis=1).astype(BF16)
    half = rows // 2
    below = jnp.concatenate([high, middle], axis=0)
    beside = jnp.concatenate([low[:, :half], low[:, half:]], axis=0)
    return jnp.concatenate([below, beside], axis=1).astype(BF16)


def unpack_logs(packed, rows):
    packed = packed.astype(F32)
    if 3 * rows <= packed.shape[1]:
        return packed[:8, :rows] + packed[:8, rows:2 * rows] + packed[:8, 2 * rows:3 * rows]
    low = jnp.concatenate([packed[:8, rows:], packed[8:, rows:]], axis=1)
    return packed[:8, :rows] + packed[8:, :rows] + low


def merge(values_a, logs_a, values_b, logs_b):
    width = values_a.shape[1]
    top = jnp.maximum(logs_a, logs_b)
    part_a, part_b = jnp.exp2(logs_a - top), jnp.exp2(logs_b - top)
    whole = part_a + part_b
    share = part_a / whole
    high = share.astype(BF16).astype(F32)
    terms = jnp.concatenate([high, share - high], axis=0).astype(BF16)
    row = lax.broadcasted_iota(jnp.int32, (16, width), 0)
    lane = lax.broadcasted_iota(jnp.int32, (16, width), 1)
    inside = jnp.bitwise_and(row, 3) < width // PAIR
    spread = inside & (lax.shift_right_logical(lane, 6) == head_of(row))
    share = tn(terms, jnp.where(spread, 1.0, 0.0).astype(BF16))
    return share * values_a + (1.0 - share) * values_b, top + jnp.log2(whole)


def scale_row(softness_ref, which, heads):
    first = lax.axis_index("qgrp") * heads
    lane_head = lax.shift_right_logical(
        lax.broadcasted_iota(jnp.int32, (1, heads * HEAD_DIM), 1), 6
    )
    row = jnp.zeros((1, heads * HEAD_DIM), F32)
    for head in range(heads):
        row = jnp.where(lane_head == head, softness_ref[which, first + head], row)
    return row * (HEAD_DIM**-0.5 * LOG2E)


def split_scaled(queries, row):
    scaled = queries.astype(BF16).astype(F32) * row
    high = scaled.astype(BF16)
    return high, (scaled - high.astype(F32)).astype(BF16)


def pair_keys(keys):
    lane = lax.broadcasted_iota(jnp.int32, keys.shape, 1)
    zero = jnp.zeros_like(keys)
    first, second = jnp.where(lane < HEAD_DIM, keys, zero), jnp.where(lane < HEAD_DIM, zero, keys)
    return jnp.concatenate(
        [jnp.concatenate([first, first], axis=1), jnp.concatenate([second, second], axis=1)], axis=0
    )


def pair_values(values, counted):
    lane = lax.broadcasted_iota(jnp.int32, values.shape, 1)
    zero = jnp.zeros_like(values)
    low = lane < HEAD_DIM
    top = jnp.concatenate([jnp.where(low, values, zero), jnp.where(low, counted, zero)], axis=1)
    end = jnp.concatenate([jnp.where(low, zero, values), jnp.where(low, zero, counted)], axis=1)
    return jnp.concatenate([top, end], axis=0)


def attend_pair(high, low, keys, values):
    count = keys.shape[0] // 2
    scores = nt(jnp.concatenate([high, low], axis=1), keys)
    top_a = jnp.max(scores[:, :count], axis=1, keepdims=True)
    top_b = jnp.max(scores[:, count:], axis=1, keepdims=True)
    weights = jnp.concatenate(
        [
            jnp.exp2(scores[:, :count] - top_a).astype(BF16),
            jnp.exp2(scores[:, count:] - top_b).astype(BF16),
        ],
        axis=1,
    )
    sums = nn(weights, values)
    lane = lax.broadcasted_iota(jnp.int32, (high.shape[0], PAIR), 1)
    top = jnp.where(lane < HEAD_DIM, top_a, top_b)
    return sums[:, :PAIR], sums[:, PAIR:], top


def encode_rows(part, query_weight, keys, values, count, scale, put):
    width = query_weight.shape[1]
    slots = keys.shape[0]
    slot = lax.broadcasted_iota(jnp.int32, (slots, PAIR), 0)
    counted = jnp.where(slot < count, 1.0, 0.0).astype(BF16)
    high, low = split_scaled(nn(part, query_weight[...]), scale)
    totals, tops = [], []
    for pair in range(width // PAIR):
        lanes = slice(pair * PAIR, (pair + 1) * PAIR)
        key_block = pair_keys(keys[:, lanes])
        value_block = pair_values(values[:, lanes], counted)
        sums, total, top = attend_pair(high[:, lanes], low[:, lanes], key_block, value_block)
        put(lanes, sums / total)
        totals.append(total)
        tops.append(top)
    return compact_logs(totals, tops)


def bits_of():
    cell, core = lax.axis_index("cell"), lax.axis_index("qgrp")
    quad = jnp.bitwise_and(cell, 3)
    return quad, core


def start_all(pairs, arrived):
    moves = [
        pltpu.make_async_copy(source, goal, arrived.at[index])
        for index, (source, goal) in enumerate(pairs)
    ]
    for move in moves:
        move.start()
    return moves


def wait_all(moves):
    for move in moves:
        move.wait()


def quarter(latents, quad, rows):
    return latents.at[pl.ds(pl.multiple_of(quad * rows, rows), rows), :]


def encode_first_kernel(
    tally, softness_far, latents_far, tokens_far, wq_far, wk_far, wv_far, wo_far, do_far,
    message, keys, values, scales, count_out, wq, latents, outputs,
    count, softness, tokens, wk, wv, arrived, arrived_later,
):
    quad, core = bits_of()
    rows, model = latents.shape[0] // 4, wo_far.shape[1]
    moves = start_all(
        [
            (tally, count), (tokens_far, tokens), (wk_far, wk), (wv_far, wv), (wq_far, wq),
            (softness_far, softness),
            (quarter(latents_far, quad ^ 3, rows), quarter(latents, quad ^ 3, rows)),
        ],
        arrived,
    )
    wait_all(moves[:3])
    is_valid = lax.broadcasted_iota(jnp.int32, keys.shape, 0) < count[0]
    made = nn(tokens[...], wk[...])
    keys[...] = jnp.where(is_valid, made, made[0:1, :]).astype(BF16)
    wait_all(moves[3:])
    later = start_all(
        [
            (wo_far, outputs.at[:, :model]), (do_far, outputs.at[:, model:]),
            *[
                (quarter(latents_far, quad ^ other, rows), quarter(latents, quad ^ other, rows))
                for other in (1, 2, 0)
            ],
        ],
        arrived_later,
    )
    values[...] = jnp.where(is_valid, nn(tokens[...], wv[...]), 0.0).astype(BF16)

    @apart
    def _():
        count_out[...] = jnp.full(count_out.shape, count[0], jnp.int32)
        for which in range(2):
            row = scale_row(softness, which, wq.shape[1] // HEAD_DIM)
            scales[which] = jnp.broadcast_to(row, scales.shape[1:])
        part = quarter(latents, quad ^ 3, rows)[...]
        encode_into(message, part, wq, keys, values, count_out, scales)

    wait_all(later)


def encode_into(message, part, wq, keys, values, count, scales):
    rows = part.shape[0]

    def put(lanes, sums):
        message[:rows, lanes] = sums.astype(BF16)

    logs = encode_rows(part, wq, keys, values, count[0:1, :], scales[0, 0:1, :], put)
    message[rows:, :] = pack_logs(logs, message.shape[1])


def encode_side_kernel(count, scales, latents, wq, keys, values, message):
    quad, core = bits_of()
    rows = latents.shape[0] // 4
    side = quad ^ jnp.where(core == 0, 1, 2)
    part = quarter(latents, side, rows)[...]
    encode_into(message, part, wq, keys, values, count, scales)


def encode_keep_kernel(is_own, count, scales, latents, wq, keys, values, kept, logs):
    quad, core = bits_of()
    rows = kept.shape[0]

    def put(lanes, part):
        kept[:, lanes] = part

    at = quad if is_own else quad ^ jnp.where(core == 0, 2, 1)
    part = quarter(latents, at, rows)[...]
    logs[...] = encode_rows(part, wq, keys, values, count[0:1, :], scales[0, 0:1, :], put)

def write_message(message, values, logs):
    rows = values.shape[0]
    message[:rows, :] = values.astype(BF16)
    message[rows:, :] = pack_logs(logs, message.shape[1])


def read_message(message, rows):
    return message[:rows, :].astype(F32), unpack_logs(message[rows:, :], rows)


def merge_pass_kernel(values, logs, came, *messages):
    rows = values.shape[0]
    half = rows // 2
    part, log = merge(values[...], logs[...], *read_message(came, rows))
    for which, message in enumerate(messages):
        at = slice(which * half, (which + 1) * half)
        write_message(message, part[at], log[:, at])


def merge_sides_kernel(which, values, logs, first, second, message):
    rows = values.shape[0]
    half = rows // 2
    at = slice(which * half, (which + 1) * half)
    part, log = values[at, :], logs[:, at]
    came_part, came_log = read_message(first, rows)
    part, log = merge(part, log, came_part[at], came_log[:, at])
    part, log = merge(part, log, *read_message(second, half))
    write_message(message, part, log)


def merge_even_kernel(own_bit, other_bit, last, rows, mine, came, out):
    core = lax.axis_index("qgrp")
    bit = jnp.where(core == 0, own_bit, other_bit)
    is_low = jnp.bitwise_and(lax.axis_index("cell"), bit) == 0

    def both(first, second):
        part, log = merge(*read_message(first, rows), *read_message(second, rows))
        if last:
            out[...] = part.astype(BF16)
        else:
            write_message(out, part, log)

    @pl.when(is_low)
    def _():
        both(mine, came)

    @pl.when(jnp.logical_not(is_low))
    def _():
        both(came, mine)


def latent_kernel(which, attended, other, weight, other_weight, latents, gain, *refs):
    quad, core = bits_of()
    half, model = attended.shape[0], weight.shape[1]
    start = pl.ds(pl.multiple_of((2 * quad + which) * half, half), half)

    def finish(first, second, first_weight, second_weight):
        update = nn(first[...], first_weight) + nn(second[...], second_weight)
        pre = latents[start, :].astype(F32) + update
        mean_square = jnp.mean(pre * pre, axis=-1, keepdims=True)
        done = (pre * lax.rsqrt(mean_square + NORM_EPSILON) * gain[...]).astype(BF16)
        if which == 0:
            refs[0][...] = done
        else:
            low, out, own_half = refs
            out[:half, :] = low[...]
            out[half:, :] = done
            own_half[...] = jnp.where(core == 0, low[...], done)

    @pl.when(core == 0)
    def _():
        finish(attended, other, weight[...], other_weight[:, :model])

    @pl.when(core != 0)
    def _():
        finish(other, attended, other_weight[:, :model], weight[...])


def groups_of(pairs):
    first = -(-2 * pairs // 3)
    return [range(first), range(first, pairs)]


def decode_prepare_kernel(scales, tokens, wq, wk, wv, out, *weights):
    width = wq.shape[1]
    high, low = split_scaled(nn(tokens[...], wq[...]), scales[1, 0:1, :])
    for pair in range(width // PAIR):
        lanes = slice(pair * PAIR, (pair + 1) * PAIR)
        out[pair, :, :PAIR] = high[:, lanes]
        out[pair, :, PAIR:] = low[:, lanes]
    for group, both in zip(groups_of(width // PAIR), weights):
        lanes = slice(group[0] * PAIR, (group[-1] + 1) * PAIR)
        size = len(group) * PAIR
        both[:, :size] = wk[:, lanes]
        both[:, size:] = wv[:, lanes]


def apart(work):
    pl.when(lax.axis_index("qgrp") >= 0)(work)


def place_rows(pieces, spots, latent_out, staged, sent):
    moves, start = [], 0
    for index, (piece, spot) in enumerate(zip(pieces, spots)):
        count = piece.shape[0]
        staged[start:start + count, :] = piece[...].astype(F32)
        moves.append(
            pltpu.make_async_copy(
                staged.at[pl.ds(start, count), :],
                latent_out.at[pl.ds(pl.multiple_of(spot, count), count), :],
                sent.at[index],
            )
        )
        moves[-1].start()
        start += count
    return moves


def decode_part(queries, keys, values, state):
    high, low = queries[:, :PAIR], queries[:, PAIR:]
    one = jnp.ones((keys.shape[0], PAIR), BF16)
    sums, total, top = attend_pair(high, low, pair_keys(keys), pair_values(values, one))
    if state is None:
        return sums, total, top
    old_sums, old_total, old_top = state
    new_top = jnp.maximum(top, old_top)
    old, new = jnp.exp2(old_top - new_top), jnp.exp2(top - new_top)
    return old * old_sums + new * sums, old * old_total + new * total, new_top


def decode_group(group, queries, both, at, state, put):
    size = len(group) * PAIR
    for place, pair in enumerate(group):
        lanes = slice(place * PAIR, (place + 1) * PAIR)
        value_lanes = slice(size + place * PAIR, size + (place + 1) * PAIR)
        old = None if state is None else [part[at, lanes] for part in state]
        put(lanes, pair, decode_part(queries[pair, at, :], both[:, lanes], both[:, value_lanes], old))


def decode_tokens(group, queries, both, state, new_state):
    block = queries.shape[1] // 2
    for index in range(2):
        at = slice(index * block, (index + 1) * block)

        def put(lanes, pair, new):
            for out, part in zip(new_state, new):
                out[at, lanes] = part

        decode_group(group, queries, both, at, state, put)


def decode_own_kernel(queries, weights, more_weights, own, latent_out, *refs):
    *states, staged, sent = refs
    quad, core = bits_of()
    rows = own.shape[0]
    moves = place_rows([own], [quad * rows], latent_out, staged, sent)

    @apart
    def _():
        for group, weight, state in zip(
            groups_of(queries.shape[0]), [weights, more_weights], [states[:3], states[3:]]
        ):
            both = nn(own[...], weight[...]).astype(BF16)
            decode_tokens(group, queries, both, None, state)

    wait_all(moves)


def decode_sides_kernel(came, queries, weights, more_weights, near, far, latent_in, *refs):
    groups = groups_of(queries.shape[0])[:1 if came else 2]
    count = 3 * len(groups)
    states, (latent_out, *refs) = refs[:count], refs[count:]
    new_states, (gathered, staged, sent) = refs[:count], refs[count:]
    quad, core = bits_of()
    half = near.shape[0]
    across = [quad ^ (1 + core), quad ^ (2 - core)]
    which = 1 - core if came else core
    pieces = [near, far]
    spots = [(at * 2 + which) * half for at in (across[::-1] if came else across)]
    moves = place_rows(pieces, spots, latent_out, staged, sent)

    @apart
    def _():
        for index, piece in enumerate(pieces):
            gathered[index * half:(index + 1) * half, :] = piece[...]
        for index, (group, weight) in enumerate(zip(groups, [weights, more_weights])):
            both = nn(gathered[...], weight[...]).astype(BF16)
            at = slice(3 * index, 3 * index + 3)
            decode_tokens(group, queries, both, states[at], new_states[at])

    wait_all(moves)


def decode_rest_kernel(queries, weights, near, far, *refs):
    state, (*new_state, gathered) = refs[:3], refs[3:]
    half = near.shape[0]
    gathered[:half, :] = near[...]
    gathered[half:, :] = far[...]
    both = nn(gathered[...], weights[...]).astype(BF16)
    decode_tokens(groups_of(queries.shape[0])[1], queries, both, state, new_state)


def decode_send_kernel(queries, weights, more_weights, mine, came, *refs):
    states, (send, *boths, gathered) = refs[:6], refs[6:]
    core = lax.axis_index("qgrp")
    half = mine.shape[0]
    gathered[:half, :] = mine[...]
    gathered[half:, :] = came[...]
    for both, weight in zip(boths, [weights, more_weights]):
        both[...] = nn(gathered[...], weight[...]).astype(BF16)
    decode_last(1 - core, queries, boths, states, send)


def decode_last(which, queries, boths, states, out):
    block = out.shape[0]
    at = pl.ds(pl.multiple_of(which * block, block), block)

    def put(lanes, pair, new):
        out[:, pair * PAIR:(pair + 1) * PAIR] = (new[0] / new[1]).astype(BF16)

    for group, both, state in zip(
        groups_of(queries.shape[0]), boths, [states[:3], states[3:]]
    ):
        decode_group(group, queries, both, at, state, put)


def decode_keep_kernel(queries, both, more_both, tokens, weight, mine, came, latent_in, *refs):
    *states, latent_out, base, attended, staged, sent = refs
    quad, core = bits_of()
    half = mine.shape[0]
    corner = (quad ^ 3) * 2 * half
    spots = [corner + core * half, corner + (1 - core) * half]
    moves = place_rows([mine, came], spots, latent_out, staged, sent)

    @apart
    def _():
        decode_last(core, queries, [both, more_both], states, attended)
        rows = base.shape[0]
        own = tokens[pl.ds(pl.multiple_of(core * rows, rows), rows), :].astype(F32)
        base[...] = own + nn(attended[...], weight[...])

    wait_all(moves)


def tokens_kernel(count, base, other, weight, out, staged, sent):
    start = lax.axis_index("qgrp") * base.shape[0]
    pieces = sent.shape[0]
    columns = base.shape[1] // pieces
    moves = []
    for index in range(pieces):
        at = pl.ds(index * columns, columns)
        value = base[:, at] + nn(other[...], weight[:, pl.ds(out.shape[1] + index * columns, columns)])
        slot = start + lax.broadcasted_iota(jnp.int32, value.shape, 0)
        staged[:, at] = jnp.where(slot < count[0:1, 0:1], value, 0.0)
        moves.append(pltpu.make_async_copy(staged.at[:, at], out.at[:, at], sent.at[index]))
        moves[-1].start()
    wait_all(moves)


SPACES = {
    "v": pl.BlockSpec(memory_space=pltpu.VMEM),
    "h": pl.BlockSpec(memory_space=pltpu.HBM),
    "a": pl.BlockSpec(memory_space=pl.ANY),
}


def call(kernel, ins, outs, *args, far=(), alias=None, scratch=(), vmem=24, flops=0, moved=0, after=(),
         name=None):
    given, more = len(args), len(after)
    args = [
        pltpu.with_memory_space_constraint(arg, pltpu.HBM) if kind == "h" else arg
        for kind, arg in zip(ins, args)
    ]
    if more:
        alone = kernel

        def kernel(*refs):
            alone(*refs[:given], *refs[given + more:])

    shapes = [jax.ShapeDtypeStruct(*out) for out in outs]
    moved = moved or sum(a.size * a.dtype.itemsize for a in [*args, *shapes])
    return pl.pallas_call(
        kernel,
        out_shape=shapes,
        in_specs=[SPACES[kind] for kind in ins + "h" * more],
        out_specs=[SPACES["h" if index in far else "v"] for index in range(len(outs))],
        input_output_aliases=alias or {},
        scratch_shapes=list(scratch),
        compiler_params=pltpu.CompilerParams(vmem_limit_bytes=vmem * MIB),
        cost_estimate=pl.CostEstimate(flops=flops, bytes_accessed=moved, transcendentals=0),
        name=name,
    )(*args, *after)


def body(tokens, tally, latents, softness, wq, wk, wv, wo, dq, dk, dv, do, gain):
    cells = lax.axis_size("cell")
    total_rows, model = latents.shape
    rows, width = total_rows // 4, wq.shape[1]
    slots = tokens.shape[0]
    half_slots = slots // 2
    deep = rows + log_rows(rows, width)

    def swap(array):
        return lax.ppermute(array, "qgrp", [(0, 1), (1, 0)])

    def trade(array, bit_0, bit_1):
        pairs = []
        for cell in range(cells):
            pairs.append((2 * cell, 2 * (cell ^ bit_0)))
            pairs.append((2 * cell + 1, 2 * (cell ^ bit_1) + 1))
        return lax.ppermute(array, ("cell", "qgrp"), pairs)

    attention = 4 * 256 * slots * width * 4
    sent = ((deep, width), BF16)
    message, keys, values, scales, count, wq, latents, outputs = call(
        encode_first_kernel, "ahhhhhhhh",
        [
            sent, *[((slots, width), BF16)] * 2,
            ((2, 8, width), F32), ((8, PAIR), jnp.int32), (wq.shape, BF16), (latents.shape, BF16),
            ((width, 2 * model), BF16),
        ],
        tally, softness, latents, tokens, wq, wk, wv, wo, do,
        scratch=[
            pltpu.SMEM(tally.shape, tally.dtype), pltpu.SMEM(softness.shape, F32),
            pltpu.VMEM(tokens.shape, BF16), *[pltpu.VMEM((model, width), BF16)] * 2,
            pltpu.SemaphoreType.DMA((7,)), pltpu.SemaphoreType.DMA((5,)),
        ],
        flops=attention, name="encode_corner",
    )
    came = trade(message, 1, 2)
    state = [((rows, width), F32), ((8, rows), F32)]
    (message,) = call(
        encode_side_kernel, "vvvvvv", [sent], count, scales, latents, wq, keys, values,
        flops=attention, name="encode_side",
    )
    first = trade(message, 1, 2)
    passed = call(
        functools.partial(encode_keep_kernel, False), "vvvvvv", state,
        count, scales, latents, wq, keys, values, flops=attention, after=[message],
        name="encode_pass",
    )
    half = rows // 2
    half_sent = ((half + log_rows(half, width), width), BF16)
    messages = call(
        merge_pass_kernel, "vvv", [half_sent] * 2, *passed, came, name="merge_pass"
    )
    seconds = [trade(message, 2, 1) for message in messages]
    kept, kept_logs = call(
        functools.partial(encode_keep_kernel, True), "vvvvvv", state,
        count, scales, latents, wq, keys, values,
        flops=attention, after=messages, name="encode_own",
    )
    other_outputs = swap(outputs)
    parts = []
    for which in range(2):
        parts += call(
            functools.partial(merge_sides_kernel, which), "vvvv",
            [half_sent], kept, kept_logs, first, seconds[which],
            after=parts, name="merge_sides",
        )
    sizes = [len(group) * PAIR for group in groups_of(width // PAIR)]
    queries, *weights = call(
        decode_prepare_kernel, "vvvvv",
        [
            ((width // PAIR, slots, 2 * PAIR), BF16),
            *[((model, 2 * size), BF16) for size in sizes],
        ],
        scales, tokens, dq, dk, dv, after=parts, name="decode_prepare",
    )
    bits = [4 << i for i in range(max(cells.bit_length() - 3, 0))]
    for index, (bit_0, bit_1) in enumerate(zip(bits, bits[::-1])):
        last = index == len(bits) - 1
        merged = []
        for part, came in [(part, trade(part, bit_0, bit_1)) for part in parts]:
            merged += call(
                functools.partial(merge_even_kernel, bit_0, bit_1, last, half), "vv",
                [((half, width), BF16) if last else (part.shape, BF16)], part, came,
                after=[*merged, queries] if last else merged, name="merge_even",
            )
        parts = merged
    parts = [part[:half] for part in parts]
    (own_low,) = call(
        functools.partial(latent_kernel, 0), "vvvvvv", [((half, model), BF16)],
        parts[0], swap(parts[0]), wo, other_outputs, latents, gain.reshape(1, model),
        after=parts[1:], name="latent_low",
    )
    own, own_half = call(
        functools.partial(latent_kernel, 1), "vvvvvvv",
        [((rows, model), BF16), ((half, model), BF16)],
        parts[1], swap(parts[1]), wo, other_outputs, latents, gain.reshape(1, model), own_low,
        name="latent",
    )
    first = trade(own_half, 1, 2)
    whole = ((total_rows, model), F32)
    states_out = [((slots, size), F32) for size in sizes for _ in range(3)]

    def scratch(count, pieces):
        return [pltpu.VMEM((count, model), F32), pltpu.SemaphoreType.DMA((pieces,))]

    latent_out, *states = call(
        decode_own_kernel, "vvvv", [whole, *states_out], queries, *weights, own,
        far=(0,), scratch=scratch(rows, 1), flops=attention, name="decode_own",
    )
    own_half, states[0] = lax.optimization_barrier((own_half, states[0]))
    second = trade(own_half, 2, 1)
    first, states[0] = lax.optimization_barrier((first, states[0]))
    third = trade(first, 2, 1)

    def decode_sides(came, near, far, latent_out, states):
        used = states[:3] if came else states
        latent_out, *used = call(
            functools.partial(decode_sides_kernel, came), "vvvvvh" + "v" * len(used),
            [whole, *states_out[:len(used)]],
            queries, *weights, near, far, latent_out, *used, far=(0,), alias={5: 0},
            scratch=[pltpu.VMEM((rows, model), BF16), *scratch(rows, 2)], flops=attention,
            name="decode_sides",
        )
        return latent_out, [*used, *states[len(used):]]

    came_first, came_second = swap(first), swap(second)
    latent_out, states = decode_sides(False, first, second, latent_out, states)
    latent_out, states = decode_sides(True, came_first, came_second, latent_out, states)
    third, states[0] = lax.optimization_barrier((third, states[0]))
    came = swap(third)
    states[3:] = call(
        decode_rest_kernel, "vvvvvvv", states_out[3:],
        queries, weights[1], came_first, came_second, *states[3:],
        scratch=[pltpu.VMEM((rows, model), BF16)], flops=attention, after=states[1:2],
        name="decode_rest",
    )
    send, *boths = call(
        decode_send_kernel, "vvvvvvvvvvv",
        [((half_slots, width), BF16), *[((rows, 2 * size), BF16) for size in sizes]],
        queries, *weights, third, came, *states, scratch=[pltpu.VMEM((rows, model), BF16)],
        flops=attention // 2, name="decode_send",
    )
    latent_out, base = call(
        decode_keep_kernel, "vvvvvvvhvvvvvv", [whole, ((half_slots, model), F32)],
        queries, *boths, tokens, do, third, came, latent_out, *states, far=(0,), alias={7: 0},
        scratch=[pltpu.VMEM((half_slots, width), BF16), *scratch(rows, 2)],
        flops=attention // 2, name="decode_keep",
    )
    (tokens_out,) = call(
        tokens_kernel, "vvvv", [((half_slots, model), F32)], count, base, swap(send), other_outputs,
        far=(0,), scratch=scratch(half_slots, 3 if model % 384 == 0 else 1), name="tokens",
    )
    return latent_out, tokens_out


def solution(mesh):
    placed = (
        P("cell", None), P("cell"), P(), P(),
        P(None, "qgrp"), P(None, "qgrp"), P(None, "qgrp"), P("qgrp", None),
        P(None, "qgrp"), P(None, "qgrp"), P(None, "qgrp"), P("qgrp", None), P(),
    )
    return jax.shard_map(
        body, mesh=mesh, in_specs=placed, out_specs=(P(), P(("cell", "qgrp"), None)),
        check_vma=False,
    )
```

```python
import functools
import math

import jax
import jax.numpy as jnp
from jax import lax
from jax.experimental import pallas as pl
from jax.experimental.pallas import tpu as pltpu
from jax.sharding import PartitionSpec as P

HEAD_DIM = 64
PAIR = 2 * HEAD_DIM
NORM_EPSILON = 1e-06
LOG2E = math.log2(math.e)
F32 = jnp.float32
BF16 = jnp.bfloat16
MIB = 1 << 20


def nn(a, b):
    return lax.dot_general(a, b, (((1,), (0,)), ((), ())), preferred_element_type=F32)


def nt(a, b):
    return lax.dot_general(a, b, (((1,), (1,)), ((), ())), preferred_element_type=F32)


def tn(a, b):
    return lax.dot_general(a, b, (((0,), (0,)), ((), ())), preferred_element_type=F32)


def log_rows(rows, width):
    return 8 if 3 * rows <= width else 16


def head_of(row):
    return 2 * jnp.bitwise_and(row, 3) + jnp.bitwise_and(lax.shift_right_logical(row, 2), 1)


def compact_logs(totals, tops):
    lane = lax.broadcasted_iota(jnp.int32, tops[0].shape, 1)

    def chosen(parts):
        out = parts[-1]
        for pair in range(len(parts) - 1):
            out = jnp.where(jnp.bitwise_and(lane, 3) == pair, parts[pair], out)
        return out

    turned = (chosen(tops) + jnp.log2(chosen(totals))).T
    row = lax.broadcasted_iota(jnp.int32, (8, turned.shape[1]), 0)
    return jnp.where(row < 4, turned[:8], turned[HEAD_DIM:HEAD_DIM + 8])


def pack_logs(logs, width):
    rows = logs.shape[1]
    high = logs.astype(BF16).astype(F32)
    middle = (logs - high).astype(BF16).astype(F32)
    low = (logs - high - middle).astype(BF16).astype(F32)
    if 3 * rows <= width:
        return jnp.concatenate([high, middle, low], axis=1).astype(BF16)
    half = rows // 2
    below = jnp.concatenate([high, middle], axis=0)
    beside = jnp.concatenate([low[:, :half], low[:, half:]], axis=0)
    return jnp.concatenate([below, beside], axis=1).astype(BF16)


def unpack_logs(packed, rows):
    packed = packed.astype(F32)
    if 3 * rows <= packed.shape[1]:
        return packed[:8, :rows] + packed[:8, rows:2 * rows] + packed[:8, 2 * rows:3 * rows]
    low = jnp.concatenate([packed[:8, rows:], packed[8:, rows:]], axis=1)
    return packed[:8, :rows] + packed[8:, :rows] + low


def merge(values_a, logs_a, values_b, logs_b):
    width = values_a.shape[1]
    top = jnp.maximum(logs_a, logs_b)
    part_a, part_b = jnp.exp2(logs_a - top), jnp.exp2(logs_b - top)
    whole = part_a + part_b
    share = part_a / whole
    high = share.astype(BF16).astype(F32)
    terms = jnp.concatenate([high, share - high], axis=0).astype(BF16)
    row = lax.broadcasted_iota(jnp.int32, (16, width), 0)
    lane = lax.broadcasted_iota(jnp.int32, (16, width), 1)
    inside = jnp.bitwise_and(row, 3) < width // PAIR
    spread = inside & (lax.shift_right_logical(lane, 6) == head_of(row))
    share = tn(terms, jnp.where(spread, 1.0, 0.0).astype(BF16))
    return share * values_a + (1.0 - share) * values_b, top + jnp.log2(whole)


def scale_row(softness_ref, which, heads):
    first = lax.axis_index("qgrp") * heads
    lane_head = lax.shift_right_logical(
        lax.broadcasted_iota(jnp.int32, (1, heads * HEAD_DIM), 1), 6
    )
    row = jnp.zeros((1, heads * HEAD_DIM), F32)
    for head in range(heads):
        row = jnp.where(lane_head == head, softness_ref[which, first + head], row)
    return row * (HEAD_DIM**-0.5 * LOG2E)


def split_scaled(queries, row):
    scaled = queries.astype(BF16).astype(F32) * row
    high = scaled.astype(BF16)
    return high, (scaled - high.astype(F32)).astype(BF16)


def pair_keys(keys):
    lane = lax.broadcasted_iota(jnp.int32, keys.shape, 1)
    zero = jnp.zeros_like(keys)
    first, second = jnp.where(lane < HEAD_DIM, keys, zero), jnp.where(lane < HEAD_DIM, zero, keys)
    return jnp.concatenate(
        [jnp.concatenate([first, first], axis=1), jnp.concatenate([second, second], axis=1)], axis=0
    )


def pair_values(values, counted):
    lane = lax.broadcasted_iota(jnp.int32, values.shape, 1)
    zero = jnp.zeros_like(values)
    low = lane < HEAD_DIM
    top = jnp.concatenate([jnp.where(low, values, zero), jnp.where(low, counted, zero)], axis=1)
    end = jnp.concatenate([jnp.where(low, zero, values), jnp.where(low, zero, counted)], axis=1)
    return jnp.concatenate([top, end], axis=0)


def attend_pair(high, low, keys, values):
    count = keys.shape[0] // 2
    scores = nt(jnp.concatenate([high, low], axis=1), keys)
    top_a = jnp.max(scores[:, :count], axis=1, keepdims=True)
    top_b = jnp.max(scores[:, count:], axis=1, keepdims=True)
    weights = jnp.concatenate(
        [
            jnp.exp2(scores[:, :count] - top_a).astype(BF16),
            jnp.exp2(scores[:, count:] - top_b).astype(BF16),
        ],
        axis=1,
    )
    sums = nn(weights, values)
    lane = lax.broadcasted_iota(jnp.int32, (high.shape[0], PAIR), 1)
    top = jnp.where(lane < HEAD_DIM, top_a, top_b)
    return sums[:, :PAIR], sums[:, PAIR:], top


def encode_rows(part, query_weight, keys, values, count, scale, put):
    width = query_weight.shape[1]
    slots = keys.shape[0]
    slot = lax.broadcasted_iota(jnp.int32, (slots, PAIR), 0)
    counted = jnp.where(slot < count, 1.0, 0.0).astype(BF16)
    high, low = split_scaled(nn(part, query_weight[...]), scale)
    totals, tops = [], []
    for pair in range(width // PAIR):
        lanes = slice(pair * PAIR, (pair + 1) * PAIR)
        key_block = pair_keys(keys[:, lanes])
        value_block = pair_values(values[:, lanes], counted)
        sums, total, top = attend_pair(high[:, lanes], low[:, lanes], key_block, value_block)
        put(lanes, sums / total)
        totals.append(total)
        tops.append(top)
    return compact_logs(totals, tops)


def bits_of():
    cell, core = lax.axis_index("cell"), lax.axis_index("qgrp")
    quad = jnp.bitwise_and(cell, 3)
    return quad, core


def start_all(pairs, arrived):
    moves = [
        pltpu.make_async_copy(source, goal, arrived.at[index])
        for index, (source, goal) in enumerate(pairs)
    ]
    for move in moves:
        move.start()
    return moves


def wait_all(moves):
    for move in moves:
        move.wait()


def quarter(latents, quad, rows):
    return latents.at[pl.ds(pl.multiple_of(quad * rows, rows), rows), :]


def encode_first_kernel(
    tally, softness_far, latents_far, tokens_far, wq_far, wk_far, wv_far, wo_far, do_far,
    message, keys, values, scales, count_out, wq, latents, outputs,
    count, softness, tokens, wk, wv, arrived, arrived_later,
):
    quad, core = bits_of()
    rows, model = latents.shape[0] // 4, wo_far.shape[1]
    moves = start_all(
        [
            (tally, count), (tokens_far, tokens), (wk_far, wk), (wv_far, wv), (wq_far, wq),
            (softness_far, softness),
            (quarter(latents_far, quad ^ 3, rows), quarter(latents, quad ^ 3, rows)),
        ],
        arrived,
    )
    wait_all(moves[:3])
    is_valid = lax.broadcasted_iota(jnp.int32, keys.shape, 0) < count[0]
    made = nn(tokens[...], wk[...])
    keys[...] = jnp.where(is_valid, made, made[0:1, :]).astype(BF16)
    wait_all(moves[3:])
    later = start_all(
        [
            (wo_far, outputs.at[:, :model]), (do_far, outputs.at[:, model:]),
            *[
                (quarter(latents_far, quad ^ other, rows), quarter(latents, quad ^ other, rows))
                for other in (1, 2, 0)
            ],
        ],
        arrived_later,
    )
    values[...] = jnp.where(is_valid, nn(tokens[...], wv[...]), 0.0).astype(BF16)

    @apart
    def _():
        count_out[...] = jnp.full(count_out.shape, count[0], jnp.int32)
        for which in range(2):
            row = scale_row(softness, which, wq.shape[1] // HEAD_DIM)
            scales[which] = jnp.broadcast_to(row, scales.shape[1:])
        part = quarter(latents, quad ^ 3, rows)[...]
        encode_into(message, part, wq, keys, values, count_out, scales)

    wait_all(later)


def encode_into(message, part, wq, keys, values, count, scales):
    rows = part.shape[0]

    def put(lanes, sums):
        message[:rows, lanes] = sums.astype(BF16)

    logs = encode_rows(part, wq, keys, values, count[0:1, :], scales[0, 0:1, :], put)
    message[rows:, :] = pack_logs(logs, message.shape[1])


def encode_side_kernel(count, scales, latents, wq, keys, values, message):
    quad, core = bits_of()
    rows = latents.shape[0] // 4
    side = quad ^ jnp.where(core == 0, 1, 2)
    part = quarter(latents, side, rows)[...]
    encode_into(message, part, wq, keys, values, count, scales)


def encode_keep_kernel(is_own, count, scales, latents, wq, keys, values, kept, logs):
    quad, core = bits_of()
    rows = kept.shape[0]

    def put(lanes, part):
        kept[:, lanes] = part

    at = quad if is_own else quad ^ jnp.where(core == 0, 2, 1)
    part = quarter(latents, at, rows)[...]
    logs[...] = encode_rows(part, wq, keys, values, count[0:1, :], scales[0, 0:1, :], put)

def write_message(message, values, logs):
    rows = values.shape[0]
    message[:rows, :] = values.astype(BF16)
    message[rows:, :] = pack_logs(logs, message.shape[1])


def read_message(message, rows):
    return message[:rows, :].astype(F32), unpack_logs(message[rows:, :], rows)


def merge_pass_kernel(values, logs, came, *messages):
    rows = values.shape[0]
    half = rows // 2
    part, log = merge(values[...], logs[...], *read_message(came, rows))
    for which, message in enumerate(messages):
        at = slice(which * half, (which + 1) * half)
        write_message(message, part[at], log[:, at])


def merge_sides_kernel(which, values, logs, first, second, message):
    rows = values.shape[0]
    half = rows // 2
    at = slice(which * half, (which + 1) * half)
    part, log = values[at, :], logs[:, at]
    came_part, came_log = read_message(first, rows)
    part, log = merge(part, log, came_part[at], came_log[:, at])
    part, log = merge(part, log, *read_message(second, half))
    write_message(message, part, log)


def merge_even_kernel(own_bit, other_bit, last, rows, mine, came, out):
    core = lax.axis_index("qgrp")
    bit = jnp.where(core == 0, own_bit, other_bit)
    is_low = jnp.bitwise_and(lax.axis_index("cell"), bit) == 0

    def both(first, second):
        part, log = merge(*read_message(first, rows), *read_message(second, rows))
        if last:
            out[...] = part.astype(BF16)
        else:
            write_message(out, part, log)

    @pl.when(is_low)
    def _():
        both(mine, came)

    @pl.when(jnp.logical_not(is_low))
    def _():
        both(came, mine)


def latent_kernel(which, attended, other, weight, other_weight, latents, gain, *refs):
    quad, core = bits_of()
    half, model = attended.shape[0], weight.shape[1]
    start = pl.ds(pl.multiple_of((2 * quad + which) * half, half), half)

    def finish(first, second, first_weight, second_weight):
        update = nn(first[...], first_weight) + nn(second[...], second_weight)
        pre = latents[start, :].astype(F32) + update
        mean_square = jnp.mean(pre * pre, axis=-1, keepdims=True)
        done = (pre * lax.rsqrt(mean_square + NORM_EPSILON) * gain[...]).astype(BF16)
        if which == 0:
            refs[0][...] = done
        else:
            low, out, own_half = refs
            out[:half, :] = low[...]
            out[half:, :] = done
            own_half[...] = jnp.where(core == 0, low[...], done)

    @pl.when(core == 0)
    def _():
        finish(attended, other, weight[...], other_weight[:, :model])

    @pl.when(core != 0)
    def _():
        finish(other, attended, other_weight[:, :model], weight[...])


def groups_of(pairs):
    first = -(-2 * pairs // 3)
    return [range(first), range(first, pairs)]


def decode_prepare_kernel(scales, tokens, wq, wk, wv, out, *weights):
    width = wq.shape[1]
    high, low = split_scaled(nn(tokens[...], wq[...]), scales[1, 0:1, :])
    for pair in range(width // PAIR):
        lanes = slice(pair * PAIR, (pair + 1) * PAIR)
        out[pair, :, :PAIR] = high[:, lanes]
        out[pair, :, PAIR:] = low[:, lanes]
    for group, both in zip(groups_of(width // PAIR), weights):
        lanes = slice(group[0] * PAIR, (group[-1] + 1) * PAIR)
        size = len(group) * PAIR
        both[:, :size] = wk[:, lanes]
        both[:, size:] = wv[:, lanes]


def apart(work):
    pl.when(lax.axis_index("qgrp") >= 0)(work)


def place_rows(pieces, spots, latent_out, staged, sent):
    moves, start = [], 0
    for index, (piece, spot) in enumerate(zip(pieces, spots)):
        count = piece.shape[0]
        staged[start:start + count, :] = piece[...].astype(F32)
        moves.append(
            pltpu.make_async_copy(
                staged.at[pl.ds(start, count), :],
                latent_out.at[pl.ds(pl.multiple_of(spot, count), count), :],
                sent.at[index],
            )
        )
        moves[-1].start()
        start += count
    return moves


def decode_part(queries, keys, values, state):
    high, low = queries[:, :PAIR], queries[:, PAIR:]
    one = jnp.ones((keys.shape[0], PAIR), BF16)
    sums, total, top = attend_pair(high, low, pair_keys(keys), pair_values(values, one))
    if state is None:
        return sums, total, top
    old_sums, old_total, old_top = state
    new_top = jnp.maximum(top, old_top)
    old, new = jnp.exp2(old_top - new_top), jnp.exp2(top - new_top)
    return old * old_sums + new * sums, old * old_total + new * total, new_top


def decode_group(group, queries, both, at, state, put):
    size = len(group) * PAIR
    for place, pair in enumerate(group):
        lanes = slice(place * PAIR, (place + 1) * PAIR)
        value_lanes = slice(size + place * PAIR, size + (place + 1) * PAIR)
        old = None if state is None else [part[at, lanes] for part in state]
        put(lanes, pair, decode_part(queries[pair, at, :], both[:, lanes], both[:, value_lanes], old))


def decode_tokens(group, queries, both, state, new_state):
    block = queries.shape[1] // 2
    for index in range(2):
        at = slice(index * block, (index + 1) * block)

        def put(lanes, pair, new):
            for out, part in zip(new_state, new):
                out[at, lanes] = part

        decode_group(group, queries, both, at, state, put)


def decode_own_kernel(queries, weights, more_weights, own, latent_out, *refs):
    *states, staged, sent = refs
    quad, core = bits_of()
    rows = own.shape[0]
    moves = place_rows([own], [quad * rows], latent_out, staged, sent)

    @apart
    def _():
        for group, weight, state in zip(
            groups_of(queries.shape[0]), [weights, more_weights], [states[:3], states[3:]]
        ):
            both = nn(own[...], weight[...]).astype(BF16)
            decode_tokens(group, queries, both, None, state)

    wait_all(moves)


def decode_sides_kernel(came, queries, weights, more_weights, near, far, latent_in, *refs):
    groups = groups_of(queries.shape[0])[:1 if came else 2]
    count = 3 * len(groups)
    states, (latent_out, *refs) = refs[:count], refs[count:]
    new_states, (gathered, staged, sent) = refs[:count], refs[count:]
    quad, core = bits_of()
    half = near.shape[0]
    across = [quad ^ (1 + core), quad ^ (2 - core)]
    which = 1 - core if came else core
    pieces = [near, far]
    spots = [(at * 2 + which) * half for at in (across[::-1] if came else across)]
    moves = place_rows(pieces, spots, latent_out, staged, sent)

    @apart
    def _():
        for index, piece in enumerate(pieces):
            gathered[index * half:(index + 1) * half, :] = piece[...]
        for index, (group, weight) in enumerate(zip(groups, [weights, more_weights])):
            both = nn(gathered[...], weight[...]).astype(BF16)
            at = slice(3 * index, 3 * index + 3)
            decode_tokens(group, queries, both, states[at], new_states[at])

    wait_all(moves)


def decode_rest_kernel(queries, weights, near, far, *refs):
    state, (*new_state, gathered) = refs[:3], refs[3:]
    half = near.shape[0]
    gathered[:half, :] = near[...]
    gathered[half:, :] = far[...]
    both = nn(gathered[...], weights[...]).astype(BF16)
    decode_tokens(groups_of(queries.shape[0])[1], queries, both, state, new_state)


def decode_send_kernel(queries, weights, more_weights, mine, came, *refs):
    states, (send, *boths, gathered) = refs[:6], refs[6:]
    core = lax.axis_index("qgrp")
    half = mine.shape[0]
    gathered[:half, :] = mine[...]
    gathered[half:, :] = came[...]
    for both, weight in zip(boths, [weights, more_weights]):
        both[...] = nn(gathered[...], weight[...]).astype(BF16)
    decode_last(1 - core, queries, boths, states, send)


def decode_last(which, queries, boths, states, out):
    block = out.shape[0]
    at = pl.ds(pl.multiple_of(which * block, block), block)

    def put(lanes, pair, new):
        out[:, pair * PAIR:(pair + 1) * PAIR] = (new[0] / new[1]).astype(BF16)

    for group, both, state in zip(
        groups_of(queries.shape[0]), boths, [states[:3], states[3:]]
    ):
        decode_group(group, queries, both, at, state, put)


def decode_keep_kernel(queries, both, more_both, tokens, weight, mine, came, latent_in, *refs):
    *states, latent_out, base, attended, staged, sent = refs
    quad, core = bits_of()
    half = mine.shape[0]
    corner = (quad ^ 3) * 2 * half
    spots = [corner + core * half, corner + (1 - core) * half]
    moves = place_rows([mine, came], spots, latent_out, staged, sent)

    @apart
    def _():
        decode_last(core, queries, [both, more_both], states, attended)
        rows = base.shape[0]
        own = tokens[pl.ds(pl.multiple_of(core * rows, rows), rows), :].astype(F32)
        base[...] = own + nn(attended[...], weight[...])

    wait_all(moves)


def tokens_kernel(count, base, other, weight, out, staged, sent):
    start = lax.axis_index("qgrp") * base.shape[0]
    pieces = sent.shape[0]
    columns = base.shape[1] // pieces
    moves = []
    for index in range(pieces):
        at = pl.ds(index * columns, columns)
        value = base[:, at] + nn(other[...], weight[:, pl.ds(out.shape[1] + index * columns, columns)])
        slot = start + lax.broadcasted_iota(jnp.int32, value.shape, 0)
        staged[:, at] = jnp.where(slot < count[0:1, 0:1], value, 0.0)
        moves.append(pltpu.make_async_copy(staged.at[:, at], out.at[:, at], sent.at[index]))
        moves[-1].start()
    wait_all(moves)


SPACES = {
    "v": pl.BlockSpec(memory_space=pltpu.VMEM),
    "h": pl.BlockSpec(memory_space=pltpu.HBM),
    "a": pl.BlockSpec(memory_space=pl.ANY),
}


def call(kernel, ins, outs, *args, far=(), alias=None, scratch=(), vmem=24, flops=0, moved=0, after=(),
         name=None):
    given, more = len(args), len(after)
    args = [
        pltpu.with_memory_space_constraint(arg, pltpu.HBM) if kind == "h" else arg
        for kind, arg in zip(ins, args)
    ]
    if more:
        alone = kernel

        def kernel(*refs):
            alone(*refs[:given], *refs[given + more:])

    shapes = [jax.ShapeDtypeStruct(*out) for out in outs]
    moved = moved or sum(a.size * a.dtype.itemsize for a in [*args, *shapes])
    return pl.pallas_call(
        kernel,
        out_shape=shapes,
        in_specs=[SPACES[kind] for kind in ins + "h" * more],
        out_specs=[SPACES["h" if index in far else "v"] for index in range(len(outs))],
        input_output_aliases=alias or {},
        scratch_shapes=list(scratch),
        compiler_params=pltpu.CompilerParams(vmem_limit_bytes=vmem * MIB),
        cost_estimate=pl.CostEstimate(flops=flops, bytes_accessed=moved, transcendentals=0),
        name=name,
    )(*args, *after)


def body(tokens, tally, latents, softness, wq, wk, wv, wo, dq, dk, dv, do, gain):
    cells = lax.axis_size("cell")
    total_rows, model = latents.shape
    rows, width = total_rows // 4, wq.shape[1]
    slots = tokens.shape[0]
    half_slots = slots // 2
    deep = rows + log_rows(rows, width)

    def swap(array):
        return lax.ppermute(array, "qgrp", [(0, 1), (1, 0)])

    def trade(array, bit_0, bit_1):
        pairs = []
        for cell in range(cells):
            pairs.append((2 * cell, 2 * (cell ^ bit_0)))
            pairs.append((2 * cell + 1, 2 * (cell ^ bit_1) + 1))
        return lax.ppermute(array, ("cell", "qgrp"), pairs)

    attention = 4 * 256 * slots * width * 4
    sent = ((deep, width), BF16)
    message, keys, values, scales, count, wq, latents, outputs = call(
        encode_first_kernel, "ahhhhhhhh",
        [
            sent, *[((slots, width), BF16)] * 2,
            ((2, 8, width), F32), ((8, PAIR), jnp.int32), (wq.shape, BF16), (latents.shape, BF16),
            ((width, 2 * model), BF16),
        ],
        tally, softness, latents, tokens, wq, wk, wv, wo, do,
        scratch=[
            pltpu.SMEM(tally.shape, tally.dtype), pltpu.SMEM(softness.shape, F32),
            pltpu.VMEM(tokens.shape, BF16), *[pltpu.VMEM((model, width), BF16)] * 2,
            pltpu.SemaphoreType.DMA((7,)), pltpu.SemaphoreType.DMA((5,)),
        ],
        flops=attention, name="encode_corner",
    )
    came = trade(message, 1, 2)
    state = [((rows, width), F32), ((8, rows), F32)]
    (message,) = call(
        encode_side_kernel, "vvvvvv", [sent], count, scales, latents, wq, keys, values,
        flops=attention, name="encode_side",
    )
    first = trade(message, 1, 2)
    passed = call(
        functools.partial(encode_keep_kernel, False), "vvvvvv", state,
        count, scales, latents, wq, keys, values, flops=attention, after=[message],
        name="encode_pass",
    )
    half = rows // 2
    half_sent = ((half + log_rows(half, width), width), BF16)
    messages = call(
        merge_pass_kernel, "vvv", [half_sent] * 2, *passed, came, name="merge_pass"
    )
    seconds = [trade(message, 2, 1) for message in messages]
    kept, kept_logs = call(
        functools.partial(encode_keep_kernel, True), "vvvvvv", state,
        count, scales, latents, wq, keys, values,
        flops=attention, after=messages, name="encode_own",
    )
    other_outputs = swap(outputs)
    parts = []
    for which in range(2):
        parts += call(
            functools.partial(merge_sides_kernel, which), "vvvv",
            [half_sent], kept, kept_logs, first, seconds[which],
            after=parts, name="merge_sides",
        )
    sizes = [len(group) * PAIR for group in groups_of(width // PAIR)]
    queries, *weights = call(
        decode_prepare_kernel, "vvvvv",
        [
            ((width // PAIR, slots, 2 * PAIR), BF16),
            *[((model, 2 * size), BF16) for size in sizes],
        ],
        scales, tokens, dq, dk, dv, after=parts, name="decode_prepare",
    )
    bits = [4 << i for i in range(max(cells.bit_length() - 3, 0))]
    for index, (bit_0, bit_1) in enumerate(zip(bits, bits[::-1])):
        last = index == len(bits) - 1
        merged = []
        for part, came in [(part, trade(part, bit_0, bit_1)) for part in parts]:
            merged += call(
                functools.partial(merge_even_kernel, bit_0, bit_1, last, half), "vv",
                [((half, width), BF16) if last else (part.shape, BF16)], part, came,
                after=[*merged, queries] if last else merged, name="merge_even",
            )
        parts = merged
    parts = [part[:half] for part in parts]
    (own_low,) = call(
        functools.partial(latent_kernel, 0), "vvvvvv", [((half, model), BF16)],
        parts[0], swap(parts[0]), wo, other_outputs, latents, gain.reshape(1, model),
        after=parts[1:], name="latent_low",
    )
    own, own_half = call(
        functools.partial(latent_kernel, 1), "vvvvvvv",
        [((rows, model), BF16), ((half, model), BF16)],
        parts[1], swap(parts[1]), wo, other_outputs, latents, gain.reshape(1, model), own_low,
        name="latent",
    )
    first = trade(own_half, 1, 2)
    second = trade(own_half, 2, 1)
    whole = ((total_rows, model), F32)
    states_out = [((slots, size), F32) for size in sizes for _ in range(3)]

    def scratch(count, pieces):
        return [pltpu.VMEM((count, model), F32), pltpu.SemaphoreType.DMA((pieces,))]

    latent_out, *states = call(
        decode_own_kernel, "vvvv", [whole, *states_out], queries, *weights, own,
        far=(0,), scratch=scratch(rows, 1), flops=attention, name="decode_own",
    )
    first, states[0] = lax.optimization_barrier((first, states[0]))
    third = trade(first, 2, 1)

    def decode_sides(came, near, far, latent_out, states):
        used = states[:3] if came else states
        latent_out, *used = call(
            functools.partial(decode_sides_kernel, came), "vvvvvh" + "v" * len(used),
            [whole, *states_out[:len(used)]],
            queries, *weights, near, far, latent_out, *used, far=(0,), alias={5: 0},
            scratch=[pltpu.VMEM((rows, model), BF16), *scratch(rows, 2)], flops=attention,
            name="decode_sides",
        )
        return latent_out, [*used, *states[len(used):]]

    came_first, came_second = swap(first), swap(second)
    latent_out, states = decode_sides(False, first, second, latent_out, states)
    latent_out, states = decode_sides(True, came_first, came_second, latent_out, states)
    third, states[0] = lax.optimization_barrier((third, states[0]))
    came = swap(third)
    states[3:] = call(
        decode_rest_kernel, "vvvvvvv", states_out[3:],
        queries, weights[1], came_first, came_second, *states[3:],
        scratch=[pltpu.VMEM((rows, model), BF16)], flops=attention, after=states[1:2],
        name="decode_rest",
    )
    send, *boths = call(
        decode_send_kernel, "vvvvvvvvvvv",
        [((half_slots, width), BF16), *[((rows, 2 * size), BF16) for size in sizes]],
        queries, *weights, third, came, *states, scratch=[pltpu.VMEM((rows, model), BF16)],
        flops=attention // 2, name="decode_send",
    )
    latent_out, base = call(
        decode_keep_kernel, "vvvvvvvhvvvvvv", [whole, ((half_slots, model), F32)],
        queries, *boths, tokens, do, third, came, latent_out, *states, far=(0,), alias={7: 0},
        scratch=[pltpu.VMEM((half_slots, width), BF16), *scratch(rows, 2)],
        flops=attention // 2, name="decode_keep",
    )
    (tokens_out,) = call(
        tokens_kernel, "vvvv", [((half_slots, model), F32)], count, base, swap(send), other_outputs,
        far=(0,), scratch=scratch(half_slots, 1), name="tokens",
    )
    return latent_out, tokens_out


def solution(mesh):
    placed = (
        P("cell", None), P("cell"), P(), P(),
        P(None, "qgrp"), P(None, "qgrp"), P(None, "qgrp"), P("qgrp", None),
        P(None, "qgrp"), P(None, "qgrp"), P(None, "qgrp"), P("qgrp", None), P(),
    )
    return jax.shard_map(
        body, mesh=mesh, in_specs=placed, out_specs=(P(), P(("cell", "qgrp"), None)),
        check_vma=False,
    )
```
